256 devices in a mesh: dp: 32 (over y, x, core), mp: 8 (over z).
Axes of the slice: x: 4, y: 4, z: 8, core: 2. Of those that a mesh axis runs over, the one named last changes fastest.
Arguments:
- patches: bfloat16 [4096, 3200], P('dp'), may hold values from -6 to 6
- upstream: bfloat16 [4096, 3200], P('dp'), may hold values from -6 to 6
- norm_gain: float32 [3200], replicated, may hold values from 0.25 to 1.75
- layer_scale: float32 [3200], replicated, may hold values from 0.3 to 1.5
- w_in: bfloat16 [3200, 6400], P('dp', 'mp'), may hold values from -0.109375 to 0.109375
- w_out: bfloat16 [6400, 3200], P('mp', 'dp'), may hold values from -0.078125 to 0.078125
- slot_block: int32 [64], P('dp'), may hold values from -1 to 255, as said below
Outputs:
- vision_tokens: bfloat16 [4096, 4, 3200], P('dp', None, 'mp')
- grad_patches: bfloat16 [4096, 3200], P('dp', 'mp')
- grad_w_in: float32 [3200, 6400], P('dp', 'mp')
- grad_w_out: float32 [6400, 3200], P('mp', 'dp')
The draws below stay inside these ranges and needn't reach their ends.
Inputs may be any that keep to these rules, and one draw needn't show every extreme that they name: `slot_block`: every used block value is different. The used slots of one dp index send their tiles to different dp indices (block // 8), so one dp index receives at most one tile from each dp index and at most 2 tiles in all.
All inputs are finite; a program needn't handle non-finite values.
Results may differ from the reference program's by a relative error of at most 0.02.
Values may be sent and summed in bfloat16 or wider, within the bound.
A program may use at most 128 MiB of HBM per device.

```python
import math
import jax
import jax.numpy as jnp
from jax import lax

DV = 3200
FFV = 6400
TROWS = 64
SLOTS = 2
BLK = 8
ROWS = 4096
N_DP = 32


def draw_slot_block(key, part):
    key = jax.random.fold_in(key, 11)
    key_sigma, key_tau, key_offset, key_inner, key_used = jax.random.split(key, 5)
    sigma = jax.random.permutation(key_sigma, N_DP).astype(jnp.int32)
    tau = jax.random.permutation(key_tau, N_DP).astype(jnp.int32)
    offsets = jax.random.permutation(key_offset, N_DP).astype(jnp.int32)[:SLOTS]
    devices = jnp.arange(N_DP, dtype=jnp.int32)[:, None]
    shard = sigma[(tau[devices] + offsets[None, :]) % N_DP]
    inner_keys = jax.random.split(key_inner, N_DP)
    orders = jax.vmap(lambda single: jax.random.permutation(single, BLK).astype(jnp.int32))(inner_keys)
    orders = ((orders - orders[:, :1] + (BLK - 1)) % BLK).astype(jnp.int32)
    slot_index = jnp.arange(SLOTS, dtype=jnp.int32)[None, :]
    inside = orders[shard, slot_index]
    used = jax.random.randint(key_used, (N_DP, SLOTS), 0, 2) == 1
    first_slot = slot_index == 0
    used = jnp.where(first_slot & (shard == N_DP - 1), True, used)
    used = jnp.where(first_slot & (shard == 0), False, used)
    blocks = jnp.where(used, shard * BLK + inside, -1)
    return blocks.reshape(N_DP * SLOTS).astype(jnp.int32)


def raised(drawn, rng, source, target, blocks, factor):
    def block_of(dim):
        return (jnp.arange(drawn.shape[dim]) // (drawn.shape[dim] // blocks)).reshape((-1,) + (1,) * (drawn.ndim - 1 - dim))

    one_side = jax.random.permutation(rng, blocks)[block_of(target)]
    other_side = (block_of(target) + blocks // 2) % blocks
    return jnp.where((block_of(source) == one_side) | (block_of(source) == other_side), factor * drawn, drawn)


def block_scale(own_key, dims, shards, least, top_value):
    level = 1.0
    for axis_at, blocks in shards:
        steps = jax.random.uniform(jax.random.fold_in(jax.random.fold_in(own_key, 6), axis_at), (blocks,), jnp.float32, least / len(shards), top_value / len(shards))
        level = level * jnp.repeat(jnp.exp(steps), dims[axis_at] // blocks).reshape((-1,) + (1,) * (len(dims) - 1 - axis_at))
    return level


def noise(rng, dims, width, limit, cuts=(), kind=jnp.bfloat16):
    entries = width * jax.random.normal(rng, dims, jnp.float32)
    if cuts:
        entries = entries * block_scale(rng, dims, cuts, -0.22, 0.18)
    return jnp.clip(entries, -limit, limit).astype(kind)


def gaussian_with(key, dims, width, limit, shards, heavy, held_as=jnp.bfloat16):
    array = width * jax.random.normal(key, dims, jnp.float32)
    if shards:
        array = array * block_scale(key, dims, shards, -0.22, 0.18)
    return jnp.clip(raised(array, jax.random.fold_in(key, 3), *heavy), -limit, limit).astype(held_as)


def setup_inputs(seed: int = 0) -> dict:
    key_list = jax.random.split(jax.random.key(seed), 8)
    return {
        "patches": noise(key_list[0], (ROWS, DV), 1.0, 6.0, ((0, 32),)),
        "upstream": gaussian_with(key_list[1], (ROWS, DV), 1.0, 6.0, ((0, 32),), (0, 1, 32, 2.75)),
        "norm_gain": jnp.clip(1.0 + 0.15 * jax.random.normal(key_list[2], (DV,), jnp.float32), 0.25, 1.75),
        "layer_scale": jnp.clip(jnp.exp(jax.random.uniform(key_list[3], (DV,), jnp.float32, math.log(0.3), math.log(1.5))), 0.3, 1.5),
        "w_in": noise(key_list[4], (DV, FFV), DV ** -0.5, 0.109375, ((0, 32), (1, 8))),
        "w_out": noise(key_list[5], (FFV, DV), FFV ** -0.5, 0.078125, ((0, 8), (1, 32))),
        "slot_block": draw_slot_block(jax.random.fold_in(key_list[7], 71), 0),
    }


def gelu_terms(values):
    cumul = 0.5 * (1.0 + jax.scipy.special.erf(values * 0.7071067811865476))
    density = jnp.exp(-0.5 * values * values) * 0.3989422804014327
    return (cumul, density)

def reference(patches, upstream, norm_gain, layer_scale, w_in, w_out, slot_block):
    inputs = patches.astype(jnp.float32)
    root_mean = jnp.sqrt(lax.optimization_barrier(jnp.mean(inputs * inputs, axis=-1, keepdims=True)) + 1e-06)
    unit_rows = inputs / root_mean
    normed = (unit_rows * norm_gain).astype(jnp.bfloat16)
    hidden_in = jnp.dot(normed, w_in, preferred_element_type=jnp.float32)
    cumul, density = gelu_terms(hidden_in)
    hidden_out = (hidden_in * cumul).astype(jnp.bfloat16)
    mixed = jnp.dot(hidden_out, w_out, preferred_element_type=jnp.float32)
    result = (inputs + layer_scale * mixed).astype(jnp.bfloat16)
    tiles = N_DP * SLOTS
    image_tok = TROWS // 4
    shuffled = result.reshape(tiles, 2, image_tok, 2, DV).transpose(0, 2, 1, 3, 4).reshape(tiles, image_tok, 4, DV)
    target = jnp.where(slot_block >= 0, slot_block, N_DP * BLK).astype(jnp.int32)
    packed = jnp.zeros((N_DP * BLK, image_tok, 4, DV), jnp.bfloat16).at[target].set(shuffled, mode='drop')
    vision_tokens = packed.reshape(N_DP * BLK * image_tok, 4, DV)
    live_row = jnp.repeat((slot_block >= 0).astype(jnp.float32), TROWS)[:, None]
    live = upstream.astype(jnp.float32) * live_row
    grad_mixed = (live * layer_scale).astype(jnp.bfloat16)
    grad_hidden = lax.dot_general(grad_mixed, w_out, (((1,), (1,)), ((), ())), preferred_element_type=jnp.float32)
    grad_in = (grad_hidden * (cumul + hidden_in * density)).astype(jnp.bfloat16)
    grad_normed = lax.dot_general(grad_in, w_in, (((1,), (1,)), ((), ())), preferred_element_type=jnp.float32)
    scaled = norm_gain * grad_normed
    center = lax.optimization_barrier(jnp.mean(scaled * unit_rows, axis=-1, keepdims=True))
    grad_patches = (live + (scaled - unit_rows * center) / root_mean).astype(jnp.bfloat16)
    per_device = SLOTS * TROWS

    def accumulate(carry, pieces):
        normed_dev, grad_in_dev, hidden_dev, grad_mixed_dev = pieces
        part_in = lax.dot_general(normed_dev, grad_in_dev, (((0,), (0,)), ((), ())), preferred_element_type=jnp.float32)
        part_out = lax.dot_general(hidden_dev, grad_mixed_dev, (((0,), (0,)), ((), ())), preferred_element_type=jnp.float32)
        part_in = lax.optimization_barrier(part_in.astype(jnp.bfloat16)).astype(jnp.float32)
        part_out = lax.optimization_barrier(part_out.astype(jnp.bfloat16)).astype(jnp.float32)
        return ((carry[0] + part_in, carry[1] + part_out), None)
    start = (jnp.zeros((DV, FFV), jnp.float32), jnp.zeros((FFV, DV), jnp.float32))
    stacked = (normed.reshape(N_DP, per_device, DV), grad_in.reshape(N_DP, per_device, FFV), hidden_out.reshape(N_DP, per_device, FFV), grad_mixed.reshape(N_DP, per_device, DV))
    (grad_w_in, grad_w_out), unused = lax.scan(accumulate, start, stacked)
    return (vision_tokens, grad_patches, grad_w_in, grad_w_out)
```

```python
import functools
import jax
import jax.numpy as jnp
from jax import lax
from jax.experimental import pallas as pl
from jax.experimental.pallas import tpu as pltpu
from jax.sharding import PartitionSpec as P

BLK = 8
FE = 100
HH = 400
UR = 208
PK = 656
HA = 336
MESH = pl.DeviceIdType.MESH
F32 = jnp.float32
BF = jnp.bfloat16


def fold_tail(tail):
    tail = jnp.concatenate([tail, jnp.zeros((16, 128), F32)], axis=0)
    out = tail[0:32]
    for g in range(1, 7):
        out = out + pltpu.roll(tail[32 * g : 32 * g + 32], 16 * g, 1)
    return out


def unfold_tail(packed):
    packed = packed.astype(F32)
    rows = [packed] + [pltpu.roll(packed, 128 - 16 * g, 1) for g in range(1, 7)]
    return jnp.concatenate(rows, axis=0)[:UR]


def kernel(
    wu, acts, base, scale, g_out, z_out, v_out,
    U, C2, CT, hacc, S, ST, PG, rb1, rb2, ra1, ra2, fin, M, MR, zrm, zrp, V, cen,
    ag_s, ag_r, rs_s, rs_r, vg_s, vg_r, vf_s, vf_r, sq_s, sq_r, zz_s, zz_r, mi_s, mi_r, loc,
):
    dp = lax.axis_index("dp")
    z = lax.axis_index("mp")
    c = lax.rem(dp, 2)
    x = lax.rem(dp // 2, 4)
    y = dp // 8
    me = y * 4 + x

    def chip_of(u, da, db):
        if u == 0:
            return lax.rem(y + db, 4) * 4 + lax.rem(x + da, 4)
        return lax.rem(y + da, 4) * 4 + lax.rem(x + db, 4)

    def dev(u, da, db):
        return (chip_of(u, da, db) * 2 + c, z)

    def zdev(dz):
        return (dp, lax.rem(z + dz, 8))

    sib = (me * 2 + 1 - c, z)
    nbrs = [sib, dev(0, 1, 0), dev(0, 3, 0), dev(0, 0, 1), dev(0, 0, 3), zdev(1), zdev(7)]

    def rc(src, dst, ss, rs, d):
        return pltpu.make_async_remote_copy(
            src_ref=src, dst_ref=dst, send_sem=ss, recv_sem=rs, device_id=d, device_id_type=MESH
        )

    def core_of(u):
        return c if u == 0 else 1 - c

    def uidx(u, da, db):
        return chip_of(u, da, db) * 2 + core_of(u)

    def da_of(k):
        return k + k // 2 - 2 * (k // 3)

    barrier = pltpu.get_barrier_semaphore()
    for d in nbrs:
        pl.semaphore_signal(barrier, inc=1, device_id=d, device_id_type=MESH)
    pl.semaphore_wait(barrier, len(nbrs))

    class Gather:
        def __init__(self, slot, split, ss, rs):
            self.slot, self.split, self.ss, self.rs = slot, split, ss, rs

        def copy(self, u, m, da, db, d, part=None):
            ref = self.slot(u, da, db, part)
            return rc(ref, ref, self.ss.at[u, m], self.rs.at[u, m], d)

        def start(self, u):
            for m, d in ((0, dev(u, 1, 0)), (1, dev(u, 3, 0)), (4, dev(u, 0, 1)), (8, dev(u, 0, 3))):
                self.copy(u, m, 0, 0, d).start()

        def wait(self, u, m, da, db, part=None):
            self.copy(u, m, da, db, sib, part).wait_recv()

        def near(self, u):
            self.wait(u, 0, 3, 0)
            self.copy(u, 2, 3, 0, dev(u, 1, 0), 0).start()
            self.copy(u, 6, 3, 0, dev(u, 0, 1)).start()
            self.copy(u, 10, 3, 0, dev(u, 0, 3)).start()
            self.wait(u, 1, 1, 0)
            self.copy(u, 3, 1, 0, dev(u, 3, 0), 1).start()
            self.copy(u, 5, 1, 0, dev(u, 0, 1)).start()
            self.copy(u, 9, 1, 0, dev(u, 0, 3)).start()

        def far(self, u):
            self.wait(u, 2, 2, 0, 0)
            self.wait(u, 3, 2, 0, 1)
            self.copy(u, 7, 2, 0, dev(u, 0, 1)).start()
            self.copy(u, 11, 2, 0, dev(u, 0, 3)).start()

        def side(self, u, k):
            da = da_of(k)
            self.wait(u, 4 + k, da, 3)
            self.wait(u, 8 + k, da, 1)

            @pl.when(k < 2)
            def _():
                self.copy(u, 12 + k, da, 3, dev(u, 0, 1)).start()

            @pl.when(k >= 2)
            def _():
                self.copy(u, 12 + k, da, 1, dev(u, 0, 3)).start()

        def last(self, u, k):
            self.wait(u, 12 + k, da_of(k), 2)

        def done(self):
            for u in (0, 1):
                for m in (2,):
                    self.copy(u, m, 0, 0, sib, 0).wait_send()
                for m in (3,):
                    self.copy(u, m, 0, 0, sib, 1).wait_send()
                for m in (0, 1) + tuple(range(4, 16)):
                    self.copy(u, m, 0, 0, sib).wait_send()

    def wslot(u, da, db, part):
        ref = U.at[uidx(u, da, db)]
        if part is None:
            return ref
        return ref.at[pl.ds(0, HA)] if part == 0 else ref.at[pl.ds(HA, PK - HA)]

    ag = Gather(wslot, HA, ag_s, ag_r)

    own = pltpu.make_async_copy(wu.at[c], U.at[me * 2 + c], loc.at[0])
    own.start()
    to_sib = rc(wu.at[1 - c], U.at[me * 2 + c], mi_s.at[0], mi_r.at[0], sib)
    to_sib.start()
    act_own = pltpu.make_async_copy(acts, C2.at[c], loc.at[1])
    act_own.start()
    act_sib = rc(acts, C2.at[c], mi_s.at[1], mi_r.at[1], sib)
    own.wait()
    ag.start(0)
    rc(wu.at[0], U.at[me * 2 + 1 - c], mi_s.at[0], mi_r.at[0], sib).wait_recv()
    ag.start(1)
    act_sib.start()
    hacc[...] = jnp.zeros_like(hacc)
    act_own.wait()
    rc(acts, C2.at[1 - c], mi_s.at[1], mi_r.at[1], sib).wait_recv()

    def weight(i):
        w = U[i]
        tail = unfold_tail(w[624:656]).astype(BF)
        return jnp.concatenate([w[0:208], w[208:416], w[416:624], tail], axis=1)

    def up(i):
        act = jnp.concatenate([C2[0, i], C2[1, i]], axis=0)
        CT[i] = act.T[:UR]
        a = act[:, :UR]
        first = lax.broadcasted_iota(jnp.int32, a.shape, 1) < FE
        zero = jnp.zeros_like(a)
        lhs = jnp.concatenate([jnp.where(first, a, zero), jnp.where(first, zero, a)], axis=0)
        hacc[...] += jnp.dot(lhs, weight(i), preferred_element_type=F32)

    for u in (0, 1):
        up(uidx(u, 0, 0))
    for u in (0, 1):
        ag.near(u)
    for u in (0, 1):
        up(uidx(u, 3, 0))
        up(uidx(u, 1, 0))
    for u in (0, 1):
        ag.far(u)
    for u in (0, 1):
        up(uidx(u, 2, 0))

    def side_step(k, carry):
        for u in (0, 1):
            ag.side(u, k)
        for u in (0, 1):
            up(uidx(u, da_of(k), 3))
            up(uidx(u, da_of(k), 1))
        return carry

    lax.fori_loop(0, 4, side_step, 0)

    def last_step(k, carry):
        for u in (0, 1):
            ag.last(u, k)
            up(uidx(u, da_of(k), 2))
        return carry

    lax.fori_loop(0, 4, last_step, 0)

    def gelu_step(r, carry):
        r0 = pl.multiple_of(r * 32, 32)
        h = hacc[pl.ds(r0, 32), :]
        gh = hacc[pl.ds(r0 + 256, 32), :]
        live = lax.broadcasted_iota(jnp.int32, h.shape, 1) < HH
        cumul = 0.5 * (1.0 + lax.erf(h * 0.7071067811865476))
        density = jnp.exp(-0.5 * h * h) * 0.3989422804014327
        ho = jnp.where(live, h * cumul, 0.0).astype(BF)
        gi = jnp.where(live, gh * (cumul + h * density), 0.0).astype(BF)
        S[pl.ds(r0, 32), :] = gi
        S[pl.ds(r0 + 256, 32), :] = ho
        row = jnp.sum(gi.astype(F32) * jnp.where(live, h, 0.0), axis=1, keepdims=True)
        cen[pl.ds(r0, 32), :] = jnp.broadcast_to(row, (32, 128))
        return carry

    lax.fori_loop(0, 8, gelu_step, 0)
    ST[...] = S[...].T
    center = cen[...].T[0:1]
    cen_hi = center.astype(BF).astype(F32)
    cen_lo = center - cen_hi

    def down(i):
        ct = CT[i]
        first = lax.broadcasted_iota(jnp.int32, ct.shape, 0) < FE
        zero = jnp.zeros_like(ct)
        lhs = jnp.concatenate([jnp.where(first, ct, zero), jnp.where(first, zero, ct)], axis=1)
        out = jnp.dot(lhs, S[...], preferred_element_type=F32)
        return [out[:, 0:128], out[:, 128:256], out[:, 256:384], fold_tail(out[:, 384:512])]

    ROWS4 = ((0, 208), (208, 416), (416, 624), (624, 656))

    def store_unit(i, *adds):
        for (lo, hi), part in zip(ROWS4, down(i)):
            for ref in adds:
                part = part + ref[lo:hi].astype(F32)
            PG[i, lo:hi] = part.astype(BF)

    def rs(u, m, i, dst, d, lo=0, hi=PK):
        return rc(PG.at[i, pl.ds(lo, hi - lo)], dst, rs_s.at[u, m], rs_r.at[u, m], d)

    def first_down(k, carry):
        for u in (0, 1):
            i = uidx(u, da_of(k), 2)
            store_unit(i)

            @pl.when(k < 2)
            def _():
                rs(u, k, i, rb1.at[u, k], dev(u, 0, 1)).start()

            @pl.when(k >= 2)
            def _():
                rs(u, k, i, rb1.at[u, k], dev(u, 0, 3)).start()

        return carry

    lax.fori_loop(0, 4, first_down, 0)

    def zblk(r):
        return lax.rem(z + r, 8)

    def mix(b):
        def body(j, carry):
            i = b * 4 + j
            out = jnp.dot(weight(i), ST[...], preferred_element_type=F32)
            row = lax.broadcasted_iota(jnp.int32, (UR, 256), 0)
            m = jnp.where(row < FE, out[:, :256], out[:, 256:])
            m = jnp.where(row == 200, cen_hi, jnp.where(row == 201, cen_lo, m)).astype(BF)
            M[0, i] = m[:, :128]
            M[1, i] = m[:, 128:]
            return carry

        lax.fori_loop(0, 4, body, 0)

    def zr_of(s):
        return 4 + (1 - 2 * (s % 2)) * ((s + 1) // 2) - 8 * (s // 8)

    def zsend_copy(s, r):
        b = zblk(r)
        return rc(M.at[1 - c, pl.ds(4 * b, 4)], MR.at[pl.ds(4 * b, 4)], sq_s.at[s], sq_r.at[s], sib)

    zorder = (4, 3, 5, 2, 6, 1, 7, 0)

    def mix_step(s, carry):
        h = (s + 1) // 2
        r = 4 + h - 2 * h * (s % 2)
        mix(zblk(r))
        zsend_copy(s, r).start()
        return carry

    lax.fori_loop(0, 8, mix_step, 0)

    def combine(r, *adds):
        b = zblk(r)

        def body(j, carry):
            i = b * 4 + j
            t = M[c, i].astype(F32) + MR[i].astype(F32)
            for ref in adds:
                t = t + ref[j].astype(F32)
            M[c, i] = t.astype(BF)
            return carry

        lax.fori_loop(0, 4, body, 0)

    def zcopy_m(j):
        return rc(M.at[c, pl.ds(4 * zblk(4 + j), 4)], zrm.at[j], zz_s.at[j], zz_r.at[j], zdev(7))

    def zcopy_p(j):
        return rc(M.at[c, pl.ds(4 * zblk(3 - j), 4)], zrp.at[j], zz_s.at[4 + j], zz_r.at[4 + j], zdev(1))

    def zstep(j):
        s = 2 * j
        zsend_copy(s, 4 + j).wait_recv()
        if j == 0:
            combine(4 + j)
        else:
            zcopy_m(j - 1).wait_recv()
            combine(4 + j, zrm.at[j - 1])
        zcopy_m(j).start()
        if j < 3:
            zsend_copy(s + 1, 3 - j).wait_recv()
            if j == 0:
                combine(3 - j)
            else:
                zcopy_p(j - 1).wait_recv()
                combine(3 - j, zrp.at[j - 1])
            zcopy_p(j).start()

    zstep(0)

    def second_down(k, carry):
        for u in (0, 1):
            ip = uidx(u, da_of(k), 1)
            im = uidx(u, da_of(k), 3)

            rs(u, k, ip, rb1.at[u, k], sib).wait_recv()

            @pl.when(k < 2)
            def _():
                store_unit(ip, rb1.at[u, k])
                store_unit(im)

            @pl.when(k >= 2)
            def _():
                store_unit(ip)
                store_unit(im, rb1.at[u, k])

            rs(u, 4 + k, ip, rb2.at[u, 0, k], dev(u, 0, 1)).start()
            rs(u, 8 + k, im, rb2.at[u, 1, k], dev(u, 0, 3)).start()
        return carry

    lax.fori_loop(0, 2, second_down, 0)
    zstep(1)
    lax.fori_loop(2, 4, second_down, 0)
    zstep(2)

    def third_wait(u, k):
        rs(u, 4 + k, uidx(u, 0, 0), rb2.at[u, 0, k], sib).wait_recv()
        rs(u, 8 + k, uidx(u, 0, 0), rb2.at[u, 1, k], sib).wait_recv()

    def third(u, k):
        third_wait(u, k)
        i = uidx(u, da_of(k), 0)
        store_unit(i, rb2.at[u, 0, k], rb2.at[u, 1, k])
        return i

    for u in (0, 1):
        i = third(u, 3)
        rs(u, 12, i, ra1.at[u, pl.ds(0, HA)], dev(u, 1, 0), 0, HA).start()
        rs(u, 13, i, ra1.at[u, pl.ds(HA, PK - HA)], dev(u, 3, 0), HA, PK).start()
    zstep(3)
    for u in (0, 1):
        third(u, 1)
        third(u, 2)
    for u in (0, 1):
        i = uidx(u, 1, 0)
        rs(u, 12, i, ra1.at[u, pl.ds(0, HA)], sib, 0, HA).wait_recv()
        PG[i, 0:HA] = (PG[i, 0:HA].astype(F32) + ra1[u, 0:HA].astype(F32)).astype(BF)
        rs(u, 14, i, ra2.at[u, 0], dev(u, 1, 0)).start()
        i = uidx(u, 3, 0)
        rs(u, 13, i, ra1.at[u, pl.ds(HA, PK - HA)], sib, HA, PK).wait_recv()
        PG[i, HA:PK] = (PG[i, HA:PK].astype(F32) + ra1[u, HA:PK].astype(F32)).astype(BF)
        rs(u, 15, i, ra2.at[u, 1], dev(u, 3, 0)).start()

    zcopy_m(3).wait_recv()
    zcopy_p(2).wait_recv()
    zsend_copy(7, 0).wait_recv()
    for j in range(4):
        i = z * 4 + j
        t = M[c, i].astype(F32) + MR[i].astype(F32) + zrm[3, j].astype(F32) + zrp[2, j].astype(F32)
        z_out[j] = t
        V[c, me, pl.ds(112 * j, 112), :] = (base[j] + scale[j] * t[96:208]).astype(BF)

    def vslot(u, da, db, part):
        lo = 224 * u
        n = 224
        if part is not None:
            lo, n = lo + 112 * part, 112
        return V.at[c, chip_of(u, da, db), pl.ds(lo, n)]

    vg = Gather(vslot, 112, vg_s, vg_r)

    def fwd(u, da, db):
        ch = chip_of(u, da, db)
        ref = V.at[c, ch, pl.ds(224 * u, 224)]
        return rc(ref, ref, vf_s.at[u, ch], vf_r.at[u, ch], sib)

    for u in (0, 1):
        vg.start(u)
    for u in (0, 1):
        fwd(u, 0, 0).start()

    def finish(u):
        third_wait(u, 0)
        i = uidx(u, 0, 0)
        parts = down(i)
        rs(u, 14, i, ra2.at[u, 0], sib).wait_recv()
        rs(u, 15, i, ra2.at[u, 1], sib).wait_recv()
        out = []
        for (lo, hi), part in zip(ROWS4, parts):
            for ref in (rb2.at[u, 0, 0], rb2.at[u, 1, 0], ra2.at[u, 0], ra2.at[u, 1]):
                part = part + ref[lo:hi].astype(F32)
            out.append(part)
        return i, out

    i, parts = finish(1)
    for (lo, hi), part in zip(ROWS4, parts):
        PG[i, lo:hi] = part.astype(BF)
    to_fin = rc(PG.at[i], fin, mi_s.at[2], mi_r.at[2], sib)
    to_fin.start()
    _, parts = finish(0)
    for t in range(3):
        g_out[c, :, 128 * t : 128 * t + 128] = parts[t]
    g_out[c, :, 384:512] = unfold_tail(parts[3])

    for u in (0, 1):
        vg.near(u)
    for u in (0, 1):
        fwd(u, 3, 0).start()
        fwd(u, 1, 0).start()
    for u in (0, 1):
        vg.far(u)
        fwd(u, 2, 0).start()

    def vside(k, carry):
        for u in (0, 1):
            vg.side(u, k)
            fwd(u, da_of(k), 3).start()
            fwd(u, da_of(k), 1).start()
        return carry

    lax.fori_loop(0, 4, vside, 0)

    to_fin.wait_recv()
    for t in range(3):
        g_out[1 - c, :, 128 * t : 128 * t + 128] = fin[208 * t : 208 * t + 208].astype(F32)
    g_out[1 - c, :, 384:512] = unfold_tail(fin[624:656])

    def vlast(k, carry):
        for u in (0, 1):
            vg.last(u, k)
            fwd(u, da_of(k), 2).start()
        return carry

    lax.fori_loop(0, 4, vlast, 0)

    def vfwd_wait(ch, carry):
        for u in (0, 1):
            ref = V.at[1 - c, ch, pl.ds(224 * u, 224)]
            d = rc(ref, ref, vf_s.at[u, ch], vf_r.at[u, ch], sib)
            d.wait_recv()
            d.wait_send()
        return carry

    lax.fori_loop(0, 16, vfwd_wait, 0)
    vcopy = pltpu.make_async_copy(V, v_out, loc.at[2])
    vcopy.start()

    ag.done()
    vg.done()
    to_sib.wait_send()
    act_sib.wait_send()
    to_fin.wait_send()
    for s in range(8):
        zsend_copy(s, zorder[s]).wait_send()
    for j in range(4):
        zcopy_m(j).wait_send()
    for j in range(3):
        zcopy_p(j).wait_send()
    for u in (0, 1):
        i = uidx(u, 0, 0)
        for m in range(16):
            lo, hi = (0, HA) if m == 12 else (HA, PK) if m == 13 else (0, PK)
            dst = ra1.at[u, pl.ds(lo, hi - lo)]
            rs(u, m, i, dst, sib, lo, hi).wait_send()
    vcopy.wait()


def mega(wu, acts, base, scale):
    dma = pltpu.SemaphoreType.DMA
    vm = pl.BlockSpec(memory_space=pltpu.VMEM)
    return pl.pallas_call(
        kernel,
        out_shape=(
            jax.ShapeDtypeStruct((2, UR, 512), F32),
            jax.ShapeDtypeStruct((4, UR, 128), F32),
            jax.ShapeDtypeStruct((2, 16, 448, 128), BF),
        ),
        in_specs=[vm] * 4,
        out_specs=(vm, vm, pl.BlockSpec(memory_space=pl.ANY)),
        scratch_shapes=[
            pltpu.VMEM((32, PK, 128), BF),
            pltpu.VMEM((2, 32, 128, 256), BF),
            pltpu.VMEM((32, UR, 256), BF),
            pltpu.VMEM((512, 512), F32),
            pltpu.VMEM((512, 512), BF),
            pltpu.VMEM((512, 512), BF),
            pltpu.VMEM((32, PK, 128), BF),
            pltpu.VMEM((2, 4, PK, 128), BF),
            pltpu.VMEM((2, 2, 4, PK, 128), BF),
            pltpu.VMEM((2, PK, 128), BF),
            pltpu.VMEM((2, 2, PK, 128), BF),
            pltpu.VMEM((PK, 128), BF),
            pltpu.VMEM((2, 32, UR, 128), BF),
            pltpu.VMEM((32, UR, 128), BF),
            pltpu.VMEM((4, 4, UR, 128), BF),
            pltpu.VMEM((3, 4, UR, 128), BF),
            pltpu.VMEM((2, 16, 448, 128), BF),
            pltpu.VMEM((256, 128), F32),
            dma((2, 16)), dma((2, 16)),
            dma((2, 16)), dma((2, 16)),
            dma((2, 16)), dma((2, 16)),
            dma((2, 16)), dma((2, 16)),
            dma((8,)), dma((8,)),
            dma((7,)), dma((7,)),
            dma((3,)), dma((3,)),
            dma((3,)),
        ],
        compiler_params=pltpu.CompilerParams(
            collective_id=0, has_side_effects=True, vmem_limit_bytes=60 * 2**20
        ),
    )(wu, acts, base, scale)


def columns(array, count, axis):
    return lax.dynamic_slice_in_dim(array, lax.axis_index("mp") * count, count, axis)


def pack_units(w_in, w_out):
    both = jnp.concatenate([w_in, w_out.T, jnp.zeros((8, 2 * HH), BF)], axis=0)
    halves = []
    for h in (0, 1):
        part = both[:, HH * h : HH * h + HH]
        tail = jnp.pad(part[:, 384:], ((0, 48), (0, 0)))
        tail = tail.reshape(8, 32, 16).transpose(1, 0, 2).reshape(32, 128)
        halves.append(
            jnp.concatenate([part[:, 0:128], part[:, 128:256], part[:, 256:384], tail], axis=0)
        )
    return jnp.stack(halves)


def shards(patches, upstream, norm_gain, layer_scale, w_in, w_out, slot_block):
    rows, width = patches.shape
    share = width // lax.axis_size("mp")
    wu = pack_units(w_in, w_out)
    inputs = patches.astype(F32)
    root_mean = jnp.sqrt(jnp.mean(inputs * inputs, axis=-1, keepdims=True) + 1e-06)
    normed = (inputs / root_mean * norm_gain).astype(BF)
    live_row = jnp.repeat((slot_block >= 0).astype(F32), rows // 2)[:, None]
    grad_mixed = (upstream.astype(F32) * live_row * layer_scale).astype(BF)
    acts = jnp.concatenate(
        [
            normed.reshape(rows, 32, FE),
            grad_mixed.reshape(rows, 32, FE),
            jnp.zeros((rows, 32, 256 - 2 * FE), BF),
        ],
        axis=2,
    ).transpose(1, 0, 2)
    mine = columns(patches, share, 1).astype(F32)
    blocks_row = jnp.repeat(slot_block, rows // 2).astype(F32)[None, None, :]
    base = jnp.concatenate(
        [
            jnp.zeros((4, 4, rows), F32),
            mine.T.reshape(4, FE, rows),
            jnp.broadcast_to(blocks_row, (4, 1, rows)),
            jnp.zeros((4, 7, rows), F32),
        ],
        axis=1,
    )
    scale = jnp.pad(columns(layer_scale, share, 0).reshape(4, FE), ((0, 0), (4, 8)))
    scale = jnp.broadcast_to(scale[:, :, None], (4, 112, rows))
    g, zsum, arrived = mega(wu, acts, base, scale)

    grad_w_in = jnp.concatenate([g[0, :FE, :HH], g[1, :FE, :HH]], axis=1)
    grad_w_out = jnp.concatenate([g[0, FE : 2 * FE, :HH], g[1, FE : 2 * FE, :HH]], axis=1).T

    tiles = arrived.reshape(32, 4, 112, 2, 64)
    blocks = tiles[:, 0, 104, :, 0].astype(jnp.int32)
    blocks = blocks.reshape(64)
    want = lax.axis_index("dp") * BLK + jnp.arange(BLK, dtype=jnp.int32)
    hit = blocks[None, :] == want[:, None]
    found = jnp.any(hit, axis=1)
    which = jnp.argmax(hit, axis=1)
    flat = tiles[:, :, 4:104].transpose(0, 3, 1, 2, 4).reshape(64, share, 64)
    tok = jnp.where(found[:, None, None], jnp.take(flat, which, axis=0), 0)
    tok = tok.transpose(0, 2, 1)
    vision = (
        tok.reshape(BLK, 2, 16, 2, share).transpose(0, 2, 1, 3, 4).reshape(BLK * 16, 4, share)
    )

    grad_normed = zsum[:, :FE].reshape(share, rows).T
    center = ((zsum[0, 200] + zsum[0, 201]) / width)[:, None]
    unit_mine = mine / root_mean
    live_mine = columns(upstream, share, 1).astype(F32) * live_row
    scaled = columns(norm_gain, share, 0) * grad_normed
    grad_patches = (live_mine + (scaled - unit_mine * center) / root_mean).astype(BF)
    return (vision, grad_patches, grad_w_in, grad_w_out)


def solution(mesh):
    return jax.shard_map(
        shards,
        mesh=mesh,
        in_specs=(P("dp", None), P("dp", None), P(), P(), P("dp", "mp"), P("mp", "dp"), P("dp")),
        out_specs=(P("dp", None, "mp"), P("dp", "mp"), P("dp", "mp"), P("mp", "dp")),
        check_vma=False,
    )
```

```python
import jax
import jax.numpy as jnp
from jax import lax
from jax.experimental import pallas as pl
from jax.experimental.pallas import tpu as pltpu
from jax.sharding import PartitionSpec as P

BLK = 8
FE = 100
HH = 400
UR = 208
PK = 656
HA = 336
PARTS = ((0, HA), (HA, PK - HA))
MESH = pl.DeviceIdType.MESH
F32 = jnp.float32
BF = jnp.bfloat16


def fold_tail(tail):
    tail = jnp.concatenate([tail, jnp.zeros((16, 128), F32)], axis=0)
    out = tail[0:32]
    for g in range(1, 7):
        out = out + pltpu.roll(tail[32 * g : 32 * g + 32], 16 * g, 1)
    return out


def unfold_tail(packed):
    packed = packed.astype(F32)
    rows = [packed] + [pltpu.roll(packed, 128 - 16 * g, 1) for g in range(1, 7)]
    return jnp.concatenate(rows, axis=0)[:UR]


def kernel(
    wu, vec, live, patches, upstream, g_out, gp_out, tab_out, v_out,
    xin, uin, nsc, gsc, rsc, RM, U, C2, X2, CT, hacc, S, ST, PG, rb1, rb2, ra1, ra2, fin, M, MR, zrm, zrp, V, cen,
    ag_s, ag_r, rs_s, rs_r, vg_s, vg_r, vf_s, vf_r, sq_s, sq_r, zz_s, zz_r, mi_s, mi_r, loc,
):
    dp = lax.axis_index("dp")
    z = lax.axis_index("mp")
    c = lax.rem(dp, 2)
    x = lax.rem(dp // 2, 4)
    y = dp // 8
    me = y * 4 + x
    UU = (0, 1)

    def chip_of(u, da, db):
        if u == 0:
            return lax.rem(y + db, 4) * 4 + lax.rem(x + da, 4)
        return lax.rem(y + da, 4) * 4 + lax.rem(x + db, 4)

    def dev(u, da, db):
        return (chip_of(u, da, db) * 2 + c, z)

    def zdev(dz):
        return (dp, lax.rem(z + dz, 8))

    sib = (me * 2 + 1 - c, z)
    ap = [dev(u, 1, 0) for u in UU]
    am = [dev(u, 3, 0) for u in UU]
    bp = [dev(u, 0, 1) for u in UU]
    bm = [dev(u, 0, 3) for u in UU]
    nbrs = [sib, ap[0], am[0], bp[0], bm[0], zdev(1), zdev(7)]

    def rc(src, dst, ss, rs, d):
        return pltpu.make_async_remote_copy(
            src_ref=src, dst_ref=dst, send_sem=ss, recv_sem=rs, device_id=d, device_id_type=MESH
        )

    def uidx(u, da, db):
        return chip_of(u, da, db) * 2 + (c if u == 0 else 1 - c)

    def da_of(k):
        return k + k // 2 - 2 * (k // 3)

    get_p = pltpu.make_async_copy(patches, xin, loc.at[1])
    get_u = pltpu.make_async_copy(upstream, uin, loc.at[2])
    own = pltpu.make_async_copy(wu.at[c], U.at[me * 2 + c], loc.at[0])
    own.start()
    get_p.start()
    get_u.start()
    barrier = pltpu.get_barrier_semaphore()
    for d in nbrs:
        pl.semaphore_signal(barrier, inc=1, device_id=d, device_id_type=MESH)
    pl.semaphore_wait(barrier, len(nbrs))

    class Gather:
        def __init__(self, slot, ss, rs):
            self.slot, self.ss, self.rs = slot, ss, rs

        def copy(self, u, m, p, da, db, d):
            ref = self.slot(u, p, da, db)
            return rc(ref, ref, self.ss.at[u, m, p], self.rs.at[u, m, p], d)

        def send(self, u, m, p, da, db, d):
            self.copy(u, m, p, da, db, d).start()

        def wait(self, u, m, p, da, db):
            self.copy(u, m, p, da, db, sib).wait_recv()

        def bsend(self, u, k, p):
            da = da_of(k)
            self.send(u, 3 + 3 * k, p, da, 0, bp[u])
            self.send(u, 4 + 3 * k, p, da, 0, bm[u])

        def start_a(self, u):
            self.send(u, 0, 0, 0, 0, ap[u])
            self.send(u, 1, 1, 0, 0, am[u])
            self.send(u, 0, 1, 0, 0, ap[u])
            self.send(u, 1, 0, 0, 0, am[u])

        def start_b(self, u):
            self.send(u, 3, 0, 0, 0, bp[u])
            self.send(u, 4, 1, 0, 0, bm[u])
            self.send(u, 3, 1, 0, 0, bp[u])
            self.send(u, 4, 0, 0, 0, bm[u])

        def near0(self, u):
            self.wait(u, 0, 0, 3, 0)
            self.send(u, 2, 0, 3, 0, ap[u])
            self.wait(u, 1, 1, 1, 0)
            self.send(u, 2, 1, 1, 0, am[u])
            self.bsend(u, 2, 0)
            self.bsend(u, 1, 1)

        def near1(self, u):
            self.wait(u, 0, 1, 3, 0)
            self.bsend(u, 2, 1)
            self.wait(u, 1, 0, 1, 0)
            self.bsend(u, 1, 0)

        def far(self, u):
            self.wait(u, 2, 0, 2, 0)
            self.bsend(u, 3, 0)
            self.wait(u, 2, 1, 2, 0)
            self.bsend(u, 3, 1)

        def bfwd(self, u, k):
            da = da_of(k)
            self.wait(u, 3 + 3 * k, 0, da, 3)
            self.send(u, 5 + 3 * k, 0, da, 3, bp[u])
            self.wait(u, 4 + 3 * k, 1, da, 1)
            self.send(u, 5 + 3 * k, 1, da, 1, bm[u])

        def brest(self, u, k):
            da = da_of(k)
            self.wait(u, 3 + 3 * k, 1, da, 3)
            self.wait(u, 4 + 3 * k, 0, da, 1)

        def blast(self, u, k):
            da = da_of(k)
            self.wait(u, 5 + 3 * k, 0, da, 2)
            self.wait(u, 5 + 3 * k, 1, da, 2)

        def done(self):
            def body(m, carry):
                for u in UU:
                    for p in (0, 1):
                        self.copy(u, m, p, 0, 0, sib).wait_send()
                return carry

            lax.fori_loop(0, 15, body, 0)

    def wslot(u, p, da, db):
        return U.at[uidx(u, da, db), pl.ds(*PARTS[p])]

    ag = Gather(wslot, ag_s, ag_r)

    to_sib = rc(wu.at[1 - c], U.at[me * 2 + c], mi_s.at[0], mi_r.at[0], sib)
    to_sib.start()
    own.wait()
    ag.start_a(0)
    rc(wu.at[0], U.at[me * 2 + 1 - c], mi_s.at[0], mi_r.at[0], sib).wait_recv()
    ag.start_a(1)
    ag.start_b(0)
    ag.start_b(1)

    hacc[...] = jnp.zeros_like(hacc)
    get_p.wait()
    get_u.wait()

    def act_step(r, carry):
        r0 = pl.multiple_of(r * 16, 16)
        xs = xin[pl.ds(r0, 16), :].astype(F32)
        root = jnp.sqrt(jnp.sum(xs * xs, axis=1, keepdims=True) * (1.0 / 3200.0) + 1e-06)
        RM[pl.ds(r0, 16), :] = jnp.broadcast_to(root, (16, 128))
        up_live = uin[pl.ds(r0, 16), :].astype(F32) * live[pl.ds(r0, 16), 0:1]
        nsc[...] = xs / root * vec[0:1, :]
        gsc[...] = up_live * vec[1:2, :]
        rsc[0] = up_live
        rsc[1] = xs
        lane = lax.broadcasted_iota(jnp.int32, (16, 256), 1)
        for i in range(32):
            q = min(100 * i // 128, 23)
            sh = 100 * i - 128 * q
            win = slice(128 * q, 128 * q + 256)

            def pair(a, b):
                a = pltpu.roll(a, (256 - sh) % 256, 1)
                b = pltpu.roll(b, (100 - sh) % 256, 1)
                return jnp.where(lane < FE, a, jnp.where(lane < 2 * FE, b, 0.0)).astype(BF)

            C2[c, i, pl.ds(r0, 16), :] = pair(nsc[:, win], gsc[:, win])
            X2[i, pl.ds(r0, 16), :] = pair(rsc[0, :, win], rsc[1, :, win])
        return carry

    lax.fori_loop(0, 8, act_step, 0)
    act_sib = rc(C2.at[c], C2.at[c], mi_s.at[1], mi_r.at[1], sib)
    act_sib.start()

    def weight(i):
        w = U[i]
        tail = unfold_tail(w[624:656]).astype(BF)
        return jnp.concatenate([w[0:208], w[208:416], w[416:624], tail], axis=1)

    def up(i):
        act = jnp.concatenate([C2[0, i], C2[1, i]], axis=0)
        CT[i] = act.T[:UR]
        a = act[:, :UR]
        first = lax.broadcasted_iota(jnp.int32, a.shape, 1) < FE
        zero = jnp.zeros_like(a)
        lhs = jnp.concatenate([jnp.where(first, a, zero), jnp.where(first, zero, a)], axis=0)
        hacc[...] += jnp.dot(lhs, weight(i), preferred_element_type=F32)

    def up_all(units):
        for u, da, db in units:
            up(uidx(u, da, db))

    for u in UU:
        ag.near0(u)
    for u in UU:
        ag.near1(u)
    rc(C2.at[c], C2.at[1 - c], mi_s.at[1], mi_r.at[1], sib).wait_recv()
    for u in UU:
        ag.bfwd(u, 0)
    up_all([(0, 0, 0), (1, 0, 0)])
    for u in UU:
        ag.far(u)
    up_all([(u, da, 0) for u in UU for da in (3, 1)])

    def fwd_step(k, carry):
        for u in UU:
            ag.bfwd(u, k)
        for u in UU:
            ag.brest(u, k - 1)
        up_all([(u, da_of(k - 1), db) for u in UU for db in (3, 1)])
        return carry

    lax.fori_loop(1, 4, fwd_step, 0)
    up_all([(0, 2, 0), (1, 2, 0)])

    def last_step(k, carry):
        for u in UU:
            ag.blast(u, k)
        up_all([(u, da_of(k), 2) for u in UU])
        return carry

    lax.fori_loop(0, 3, last_step, 0)
    for u in UU:
        ag.brest(u, 3)
    up_all([(u, da_of(3), db) for u in UU for db in (3, 1)])
    last_step(3, 0)

    def gelu_step(r, carry):
        r0 = pl.multiple_of(r * 32, 32)
        h = hacc[pl.ds(r0, 32), :]
        gh = hacc[pl.ds(r0 + 256, 32), :]
        valid = lax.broadcasted_iota(jnp.int32, h.shape, 1) < HH
        cumul = 0.5 * (1.0 + lax.erf(h * 0.7071067811865476))
        density = jnp.exp(-0.5 * h * h) * 0.3989422804014327
        ho = jnp.where(valid, h * cumul, 0.0).astype(BF)
        gi = jnp.where(valid, gh * (cumul + h * density), 0.0).astype(BF)
        S[pl.ds(r0, 32), :] = gi
        S[pl.ds(r0 + 256, 32), :] = ho
        row = jnp.sum(gi.astype(F32) * jnp.where(valid, h, 0.0), axis=1, keepdims=True)
        cen[pl.ds(r0, 32), :] = jnp.broadcast_to(row, (32, 128))
        return carry

    lax.fori_loop(0, 8, gelu_step, 0)

    def down(i):
        ct = CT[i]
        first = lax.broadcasted_iota(jnp.int32, ct.shape, 0) < FE
        zero = jnp.zeros_like(ct)
        lhs = jnp.concatenate([jnp.where(first, ct, zero), jnp.where(first, zero, ct)], axis=1)
        out = jnp.dot(lhs, S[...], preferred_element_type=F32)
        return [out[:, 0:128], out[:, 128:256], out[:, 256:384], fold_tail(out[:, 384:512])]

    ROWS4 = ((0, 208), (208, 416), (416, 624), (624, 656))

    def store_unit(i, *adds):
        for (lo, hi), part in zip(ROWS4, down(i)):
            for ref in adds:
                part = part + ref[lo:hi].astype(F32)
            PG[i, lo:hi] = part.astype(BF)

    def add_part(i, p, ref):
        lo, n = PARTS[p]
        PG[i, lo : lo + n] = (PG[i, lo : lo + n].astype(F32) + ref[lo : lo + n].astype(F32)).astype(BF)

    def rs(u, m, p, i, buf, d):
        return rc(
            PG.at[i, pl.ds(*PARTS[p])], buf.at[pl.ds(*PARTS[p])], rs_s.at[u, m, p], rs_r.at[u, m, p], d
        )

    def rs_wait(u, m, p, buf):
        rs(u, m, p, 0, buf, sib).wait_recv()

    def first_down(kk, carry):
        k = 3 - kk
        for u in UU:
            i = uidx(u, da_of(k), 2)
            store_unit(i)
            rs(u, 3 + 3 * k, 0, i, rb1.at[u, k], bp[u]).start()
            rs(u, 3 + 3 * k, 1, i, rb1.at[u, k], bm[u]).start()
        return carry

    lax.fori_loop(0, 4, first_down, 0)
    ST[...] = S[...].T
    center = cen[...].T[0:1]
    cen_hi = center.astype(BF).astype(F32)
    cen_lo = center - cen_hi

    def zblk(r):
        return lax.rem(z + r, 8)

    def mix(b):
        def body(j, carry):
            i = b * 4 + j
            out = jnp.dot(weight(i), ST[...], preferred_element_type=F32)
            row = lax.broadcasted_iota(jnp.int32, (UR, 256), 0)
            m = jnp.where(row < FE, out[:, :256], out[:, 256:])
            m = jnp.where(row == 200, cen_hi, jnp.where(row == 201, cen_lo, m)).astype(BF)
            M[0, i] = m[:, :128]
            M[1, i] = m[:, 128:]
            return carry

        lax.fori_loop(0, 4, body, 0)

    def to_sibling(s, r):
        b = zblk(r)
        return rc(M.at[1 - c, pl.ds(4 * b, 4)], MR.at[pl.ds(4 * b, 4)], sq_s.at[s], sq_r.at[s], sib)

    zorder = (4, 3, 5, 2, 6, 1, 7, 0)

    def mix_step(s, carry):
        h = (s + 1) // 2
        r = 4 + h - 2 * h * lax.rem(s, 2)
        mix(zblk(r))
        to_sibling(s, r).start()
        return carry

    def zcopy(way, j, h):
        r = 4 + j if way == 0 else 4 - j
        buf = zrm if way == 0 else zrp
        return rc(
            M.at[c, pl.ds(4 * zblk(r) + 2 * h, 2)], buf.at[j, pl.ds(2 * h, 2)],
            zz_s.at[way, j, h], zz_r.at[way, j, h], zdev(7 if way == 0 else 1),
        )

    def combine(r, h, ref):
        b = zblk(r)
        for j in (2 * h, 2 * h + 1):
            i = b * 4 + j
            t = M[c, i].astype(F32) + MR[i].astype(F32)
            if ref is not None:
                t = t + ref[j].astype(F32)
            M[c, i] = t.astype(BF)

    def zfirst():
        to_sibling(0, 4).wait_recv()
        for way in (0, 1):
            combine(4, way, None)
            zcopy(way, 0, way).start()

    def zstep(j):
        for h in ((1, 0) if j == 1 else (0, 1)):
            for way in (0, 1):
                buf = zrm if way == 0 else zrp
                r = 4 + j if way == 0 else 4 - j
                if h == 1 if j == 1 else h == 0:
                    to_sibling(2 * j if way == 0 else 2 * j - 1, r).wait_recv()
                hh = h if way == 0 or j > 1 else 1 - h
                if j == 1 and hh != way:
                    combine(r, hh, None)
                else:
                    zcopy(way, j - 1, hh).wait_recv()
                    combine(r, hh, buf.at[j - 1])
                zcopy(way, j, hh).start()

    lax.fori_loop(0, 4, mix_step, 0)
    zfirst()
    lax.fori_loop(4, 8, mix_step, 0)

    def second_down(kk, carry):
        k = 3 - kk
        for u in UU:
            i = uidx(u, da_of(k), 1)
            store_unit(i)
            rs(u, 4 + 3 * k, 1, i, rb2.at[u, 0, k], bp[u]).start()
            i = uidx(u, da_of(k), 3)
            store_unit(i)
            rs(u, 5 + 3 * k, 0, i, rb2.at[u, 1, k], bm[u]).start()
        for u in UU:
            i = uidx(u, da_of(k), 1)
            rs_wait(u, 3 + 3 * k, 0, rb1.at[u, k])
            add_part(i, 0, rb1.at[u, k])
            rs(u, 4 + 3 * k, 0, i, rb2.at[u, 0, k], bp[u]).start()
            i = uidx(u, da_of(k), 3)
            rs_wait(u, 3 + 3 * k, 1, rb1.at[u, k])
            add_part(i, 1, rb1.at[u, k])
            rs(u, 5 + 3 * k, 1, i, rb2.at[u, 1, k], bm[u]).start()
        return carry

    lax.fori_loop(0, 2, second_down, 0)
    zstep(1)
    lax.fori_loop(2, 4, second_down, 0)
    zstep(2)

    def third(u, k):
        for w in (0, 1):
            for p in (1, 0) if w == 0 else (0, 1):
                rs_wait(u, 4 + 3 * k + w, p, rb2.at[u, w, k])
        i = uidx(u, da_of(k), 0)
        store_unit(i, rb2.at[u, 0, k], rb2.at[u, 1, k])
        return i

    for u in UU:
        i = third(u, 3)
        rs(u, 0, 0, i, ra1.at[u], ap[u]).start()
        rs(u, 0, 1, i, ra1.at[u], am[u]).start()
    for u in UU:
        i = third(u, 1)
        rs(u, 1, 1, i, ra2.at[u, 0], ap[u]).start()
        i = third(u, 2)
        rs(u, 2, 0, i, ra2.at[u, 1], am[u]).start()
    zstep(3)
    for u in UU:
        rs_wait(u, 0, 0, ra1.at[u])
        i = uidx(u, 1, 0)
        add_part(i, 0, ra1.at[u])
        rs(u, 1, 0, i, ra2.at[u, 0], ap[u]).start()
        rs_wait(u, 0, 1, ra1.at[u])
        i = uidx(u, 3, 0)
        add_part(i, 1, ra1.at[u])
        rs(u, 2, 1, i, ra2.at[u, 1], am[u]).start()

    to_sibling(7, 0).wait_recv()
    for h in (0, 1):
        for way in (0, 1):
            zcopy(way, 3, h).wait_recv()
    root = RM[:, 0:1]
    lane = lax.broadcasted_iota(jnp.int32, (128, 256), 1)
    centre = None
    res = []
    for j in range(4):
        i = z * 4 + j
        t = M[c, i].astype(F32) + MR[i].astype(F32) + zrm[3, j].astype(F32) + zrp[3, j].astype(F32)
        t = jnp.concatenate([t, jnp.zeros((256 - UR, 128), F32)], axis=0).T
        if j == 0:
            centre = (t[:, 200:201] + t[:, 201:202]) * (1.0 / 3200.0)
        raw = X2[i].astype(F32)
        gains = vec_units(vec, i)
        moved = pltpu.roll(raw, 156, 1)
        gp = raw + (gains * t - moved / root * centre) / root
        gp_out[j] = gp[:, :128].astype(BF)
        res.append(pltpu.roll(raw + gains * t, 156, 1)[:, :128])
    out = jnp.where(lane[:, :128] < FE, res[0], 0.0)
    wide = [out, jnp.zeros_like(out), jnp.zeros_like(out), jnp.zeros_like(out)]
    for j in (1, 2, 3):
        at, sh = divmod(FE * j, 128)
        r = pltpu.roll(res[j], sh, 1)
        ln = lane[:, :128]
        first = (ln >= sh) & (ln < sh + FE)
        wide[at] = jnp.where(first, r, wide[at])
        if sh + FE > 128:
            wide[at + 1] = jnp.where(ln < sh + FE - 128, r, wide[at + 1])
    tail = jnp.where(lane[:, :128] < 16, wide[3], 0.0)
    folded = tail[0:16]
    for g in range(1, 8):
        folded = folded + pltpu.roll(tail[16 * g : 16 * g + 16], 16 * g, 1)
    for t in range(3):
        V[c, me, 128 * t : 128 * t + 128, :] = wide[t].astype(BF)
    V[c, me, 384:400, :] = folded.astype(BF)

    VP = (((0, 112), (112, 96)), ((208, 96), (304, 96)))

    def vslot(u, p, da, db):
        return V.at[c, chip_of(u, da, db), pl.ds(*VP[u][p])]

    vg = Gather(vslot, vg_s, vg_r)

    def fwd(u, da, db):
        ch = chip_of(u, da, db)
        ref = V.at[c, ch, pl.ds(208 * u, 208 - 16 * u)]
        return rc(ref, ref, vf_s.at[u, ch], vf_r.at[u, ch], sib)

    for u in UU:
        vg.start_a(u)
    for u in UU:
        vg.start_b(u)
    for u in UU:
        fwd(u, 0, 0).start()

    def finish(u):
        for w in (0, 1):
            for p in (1, 0) if w == 0 else (0, 1):
                rs_wait(u, 4 + w, p, rb2.at[u, w, 0])
        i = uidx(u, 0, 0)
        parts = down(i)
        for w in (0, 1):
            for p in (1, 0) if w == 0 else (0, 1):
                rs_wait(u, 1 + w, p, ra2.at[u, w])
        out = []
        for (lo, hi), part in zip(ROWS4, parts):
            for ref in (rb2.at[u, 0, 0], rb2.at[u, 1, 0], ra2.at[u, 0], ra2.at[u, 1]):
                part = part + ref[lo:hi].astype(F32)
            out.append(part)
        return i, out

    i, parts = finish(1)
    for (lo, hi), part in zip(ROWS4, parts):
        PG[i, lo:hi] = part.astype(BF)
    to_fin = rc(PG.at[i], fin, mi_s.at[2], mi_r.at[2], sib)
    to_fin.start()
    for u in UU:
        vg.near0(u)
    for u in UU:
        vg.near1(u)
    _, parts = finish(0)
    for t in range(3):
        g_out[c, :, 128 * t : 128 * t + 128] = parts[t]
    g_out[c, :, 384:512] = unfold_tail(parts[3])

    for u in UU:
        fwd(u, 3, 0).start()
        fwd(u, 1, 0).start()
    for u in UU:
        vg.bfwd(u, 0)
    for u in UU:
        vg.far(u)
        fwd(u, 2, 0).start()

    def vstep(k, carry):
        for u in UU:
            vg.bfwd(u, k)
        for u in UU:
            vg.brest(u, k - 1)
            fwd(u, da_of(k - 1), 3).start()
            fwd(u, da_of(k - 1), 1).start()
        return carry

    lax.fori_loop(1, 4, vstep, 0)

    to_fin.wait_recv()
    for t in range(3):
        g_out[1 - c, :, 128 * t : 128 * t + 128] = fin[208 * t : 208 * t + 208].astype(F32)
    g_out[1 - c, :, 384:512] = unfold_tail(fin[624:656])
    tab_out[...] = U[:, 192:208, :].astype(F32)[:, 8, :]

    for u in UU:
        vg.brest(u, 3)
        fwd(u, 2, 3).start()
        fwd(u, 2, 1).start()

    def vlast(k, carry):
        for u in UU:
            vg.blast(u, k)
            fwd(u, da_of(k), 2).start()
        return carry

    lax.fori_loop(0, 4, vlast, 0)

    def vfwd_wait(ch, carry):
        for u in UU:
            ref = V.at[1 - c, ch, pl.ds(208 * u, 208 - 16 * u)]
            d = rc(ref, ref, vf_s.at[u, ch], vf_r.at[u, ch], sib)
            d.wait_recv()
            d.wait_send()
        return carry

    lax.fori_loop(0, 16, vfwd_wait, 0)
    vcopy = pltpu.make_async_copy(V, v_out, loc.at[3])
    vcopy.start()

    ag.done()
    vg.done()
    to_sib.wait_send()
    act_sib.wait_send()
    to_fin.wait_send()
    for s in range(8):
        to_sibling(s, zorder[s]).wait_send()
    for way in (0, 1):
        zcopy(way, 0, way).wait_send()
        for j in (1, 2, 3):
            for h in (0, 1):
                zcopy(way, j, h).wait_send()

    def rs_done(m, carry):
        for u in UU:
            for p in (0, 1):
                rs(u, m, p, 0, ra1.at[u], sib).wait_send()
        return carry

    lax.fori_loop(0, 15, rs_done, 0)
    vcopy.wait()


def vec_units(vec, i):
    return vec[pl.ds(2 + i, 1), 0:256]


def mega(wu, vec, live, patches, upstream):
    dma = pltpu.SemaphoreType.DMA
    vm = pl.BlockSpec(memory_space=pltpu.VMEM)
    hbm = pl.BlockSpec(memory_space=pl.ANY)
    return pl.pallas_call(
        kernel,
        out_shape=(
            jax.ShapeDtypeStruct((2, UR, 512), F32),
            jax.ShapeDtypeStruct((4, 128, 128), BF),
            jax.ShapeDtypeStruct((32, 128), F32),
            jax.ShapeDtypeStruct((2, 16, 400, 128), BF),
        ),
        in_specs=[vm, vm, vm, hbm, hbm],
        out_specs=(vm, vm, vm, hbm),
        scratch_shapes=[
            pltpu.VMEM((128, 3200), BF),
            pltpu.VMEM((128, 3200), BF),
            pltpu.VMEM((16, 3200), F32),
            pltpu.VMEM((16, 3200), F32),
            pltpu.VMEM((2, 16, 3200), F32),
            pltpu.VMEM((128, 128), F32),
            pltpu.VMEM((32, PK, 128), BF),
            pltpu.VMEM((2, 32, 128, 256), BF),
            pltpu.VMEM((32, 128, 256), BF),
            pltpu.VMEM((32, UR, 256), BF),
            pltpu.VMEM((512, 512), F32),
            pltpu.VMEM((512, 512), BF),
            pltpu.VMEM((512, 512), BF),
            pltpu.VMEM((32, PK, 128), BF),
            pltpu.VMEM((2, 4, PK, 128), BF),
            pltpu.VMEM((2, 2, 4, PK, 128), BF),
            pltpu.VMEM((2, PK, 128), BF),
            pltpu.VMEM((2, 2, PK, 128), BF),
            pltpu.VMEM((PK, 128), BF),
            pltpu.VMEM((2, 32, UR, 128), BF),
            pltpu.VMEM((32, UR, 128), BF),
            pltpu.VMEM((4, 4, UR, 128), BF),
            pltpu.VMEM((4, 4, UR, 128), BF),
            pltpu.VMEM((2, 16, 400, 128), BF),
            pltpu.VMEM((256, 128), F32),
            dma((2, 15, 2)), dma((2, 15, 2)),
            dma((2, 15, 2)), dma((2, 15, 2)),
            dma((2, 15, 2)), dma((2, 15, 2)),
            dma((2, 16)), dma((2, 16)),
            dma((8,)), dma((8,)),
            dma((2, 4, 2)), dma((2, 4, 2)),
            dma((3,)), dma((3,)),
            dma((4,)),
        ],
        compiler_params=pltpu.CompilerParams(
            collective_id=0, has_side_effects=True, vmem_limit_bytes=60 * 2**20
        ),
    )(wu, vec, live, patches, upstream)


def finish_kernel(g, gp, tab, v, w_in_out, w_out_out, gp_out, vis_out, tiles, sem):
    first = lax.axis_index("dp") * BLK
    table = tab[...]
    row = lax.broadcasted_iota(jnp.int32, table.shape, 0)
    lane = lax.broadcasted_iota(jnp.int32, table.shape, 1)
    code = (2 * row + lane).astype(F32)
    which = []
    copies = []
    for b in range(BLK):
        hit = (table == (first + b).astype(F32)) & (lane < 2)
        at = jnp.max(jnp.where(hit, code, -1.0)).astype(jnp.int32)
        which.append(at)
        dev = jnp.maximum(at, 0) // 2
        copy = pltpu.make_async_copy(v.at[lax.rem(dev, 2), dev // 2], tiles.at[b], sem.at[b])
        copy.start()
        copies.append(copy)
    for h in (0, 1):
        w_in_out[:, HH * h : HH * h + HH] = g[h, 0:FE, 0:HH]
        w_out_out[HH * h : HH * h + HH, :] = g[h, FE : 2 * FE, 0:HH].T
    for j in range(4):
        gp_out[:, FE * j : FE * j + FE] = gp[j, :, 0:FE]
    to = lax.broadcasted_iota(jnp.int32, (64, 64), 0)
    fr = lax.broadcasted_iota(jnp.int32, (64, 64), 1)
    perm = (fr == 32 * (lax.rem(to, 4) // 2) + 2 * (to // 4) + lax.rem(to, 2)).astype(BF)
    for b in range(BLK):
        copies[b].wait()
        at = which[b]
        odd = lax.rem(at, 2) == 1
        parts = []
        for t in range(3):
            lo = tiles[b, 128 * t : 128 * t + 64]
            hi = tiles[b, 128 * t + 64 : 128 * t + 128]
            parts.append(jnp.where(odd, hi, lo))
        tail = tiles[b, 384:400].astype(F32)
        tail = jnp.where(odd, pltpu.roll(tail, 64, 1), tail)
        tail = [tail] + [pltpu.roll(tail, 128 - 16 * g, 1) for g in (1, 2, 3)]
        parts.append(jnp.concatenate(tail, axis=0).astype(BF))
        tile = jnp.concatenate(parts, axis=1)
        out = jnp.dot(perm, tile, preferred_element_type=F32)
        out = jnp.where(at >= 0, out, 0.0).astype(BF)
        vis_out[64 * b : 64 * b + 64, :] = out[:, 0:HH]


def finish(g, gp, tab, v):
    vm = pl.BlockSpec(memory_space=pltpu.VMEM)
    return pl.pallas_call(
        finish_kernel,
        out_shape=(
            jax.ShapeDtypeStruct((FE, 2 * HH), F32),
            jax.ShapeDtypeStruct((2 * HH, FE), F32),
            jax.ShapeDtypeStruct((128, HH), BF),
            jax.ShapeDtypeStruct((BLK * 64, HH), BF),
        ),
        in_specs=[vm, vm, vm, pl.BlockSpec(memory_space=pl.ANY)],
        out_specs=(vm, vm, vm, vm),
        scratch_shapes=[pltpu.VMEM((BLK, 400, 128), BF), pltpu.SemaphoreType.DMA((BLK,))],
        compiler_params=pltpu.CompilerParams(vmem_limit_bytes=32 * 2**20),
    )(g, gp, tab, v)


def pack_units(w_in, w_out, slot_block):
    table = jnp.pad(slot_block.astype(BF)[None, :], ((0, 7), (0, 2 * HH - 2)))
    table = table + jnp.roll(table, HH, axis=1)
    both = jnp.concatenate([w_in, w_out.T, table], axis=0)
    halves = []
    for h in (0, 1):
        part = both[:, HH * h : HH * h + HH]
        tail = jnp.pad(part[:, 384:], ((0, 48), (0, 0)))
        tail = tail.reshape(8, 32, 16).transpose(1, 0, 2).reshape(32, 128)
        halves.append(
            jnp.concatenate([part[:, 0:128], part[:, 128:256], part[:, 256:384], tail], axis=0)
        )
    return jnp.stack(halves)


def shards(patches, upstream, norm_gain, layer_scale, w_in, w_out, slot_block):
    rows = patches.shape[0]
    wu = pack_units(w_in, w_out, slot_block)
    live = jnp.repeat((slot_block >= 0).astype(F32), rows // 2)[:, None]
    live = jnp.broadcast_to(live, (rows, 128))
    units = jnp.concatenate([norm_gain.reshape(32, FE), layer_scale.reshape(32, FE)], axis=1)
    units = jnp.pad(units, ((0, 0), (0, 3200 - 2 * FE)))
    vec = jnp.concatenate([norm_gain[None], layer_scale[None], units], axis=0)
    g, gp, tab, v = mega(wu, vec, live, patches, upstream)
    grad_w_in, grad_w_out, grad_patches, vision = finish(g, gp, tab, v)
    return (vision.reshape(BLK * 16, 4, HH), grad_patches, grad_w_in, grad_w_out)


def solution(mesh):
    return jax.shard_map(
        shards,
        mesh=mesh,
        in_specs=(P("dp", None), P("dp", None), P(), P(), P("dp", "mp"), P("mp", "dp"), P("dp")),
        out_specs=(P("dp", None, "mp"), P("dp", "mp"), P("dp", "mp"), P("mp", "dp")),
        check_vma=False,
    )
```

```python
import jax
import jax.numpy as jnp
from jax import lax
from jax.experimental import pallas as pl
from jax.experimental.pallas import tpu as pltpu
from jax.sharding import PartitionSpec as P

BLK = 8
FE = 100
HH = 400
UR = 208
PK = 656
HA = 336
PARTS = ((0, HA), (HA, PK - HA))
MESH = pl.DeviceIdType.MESH
F32 = jnp.float32
BF = jnp.bfloat16


def fold_tail(tail):
    tail = jnp.concatenate([tail, jnp.zeros((16, 128), F32)], axis=0)
    out = tail[0:32]
    for g in range(1, 7):
        out = out + pltpu.roll(tail[32 * g : 32 * g + 32], 16 * g, 1)
    return out


def unfold_tail(packed):
    packed = packed.astype(F32)
    rows = [packed] + [pltpu.roll(packed, 128 - 16 * g, 1) for g in range(1, 7)]
    return jnp.concatenate(rows, axis=0)[:UR]


def kernel(
    slots, w_in, w_out, gain, lscale, patches, upstream, gin_out, gout_out, gp_out, vis_out,
    xin, uin, nsc, rsc, RM, VC, PM, WB, wu, GU, U, WT, C2, XU, XP, CT, hacc, S, ST, PG, rb1, rb2, ra1, ra2, fin, GS,
    M, MR, zrm, zrp, V, GP, cen,
    ag_s, ag_r, rs_s, rs_r, vg_s, vg_r, vf_s, vf_r, sq_s, sq_r, zz_s, zz_r, mi_s, mi_r, loc,
):
    dp = lax.axis_index("dp")
    z = lax.axis_index("mp")
    c = lax.rem(dp, 2)
    x = lax.rem(dp // 2, 4)
    y = dp // 8
    me = y * 4 + x
    UU = (0, 1)

    def chip_of(u, da, db):
        if u == 0:
            return lax.rem(y + db, 4) * 4 + lax.rem(x + da, 4)
        return lax.rem(y + da, 4) * 4 + lax.rem(x + db, 4)

    def dev(u, da, db):
        return (chip_of(u, da, db) * 2 + c, z)

    def zdev(dz):
        return (dp, lax.rem(z + dz, 8))

    sib = (me * 2 + 1 - c, z)
    ap = [dev(u, 1, 0) for u in UU]
    am = [dev(u, 3, 0) for u in UU]
    bp = [dev(u, 0, 1) for u in UU]
    bm = [dev(u, 0, 3) for u in UU]
    nbrs = [sib, ap[0], am[0], bp[0], bm[0], zdev(1), zdev(7)]

    def rc(src, dst, ss, rs, d):
        return pltpu.make_async_remote_copy(
            src_ref=src, dst_ref=dst, send_sem=ss, recv_sem=rs, device_id=d, device_id_type=MESH
        )

    def uidx(u, da, db):
        return chip_of(u, da, db) * 2 + (c if u == 0 else 1 - c)

    def da_of(k):
        return k + k // 2 - 2 * (k // 3)

    get_p = pltpu.make_async_copy(patches, xin, loc.at[1])
    get_u = pltpu.make_async_copy(upstream, uin, loc.at[2])
    get_p.start()
    get_u.start()
    barrier = pltpu.get_barrier_semaphore()
    for d in nbrs:
        pl.semaphore_signal(barrier, inc=1, device_id=d, device_id_type=MESH)

    WB[0:FE, 0:800] = w_in[...].astype(F32)
    WB[FE : 2 * FE, 0:800] = w_out[...].astype(F32)
    at = lax.broadcasted_iota(jnp.int32, (8, 800), 1)
    at = jnp.where(at < HH, at, at - HH)
    slot0 = slots[0].astype(F32)
    slot1 = slots[1].astype(F32)
    WB[2 * FE : UR, 0:800] = jnp.where(at == 0, slot0, jnp.where(at == 1, slot1, 0.0))
    for h in (0, 1):
        part = WB[:, 0:512] if h == 0 else pltpu.roll(WB[:, 384:896], 496, 1)
        for t in range(3):
            wu[h, UR * t : UR * t + UR] = part[:, 128 * t : 128 * t + 128].astype(BF)
        tail = part[:, 384:512]
        tail = jnp.where(lax.broadcasted_iota(jnp.int32, tail.shape, 1) < 16, tail, 0.0)
        wu[h, 3 * UR : PK] = fold_tail(tail).astype(BF)
    pl.semaphore_wait(barrier, len(nbrs))

    class Gather:
        def __init__(self, slot, ss, rs):
            self.slot, self.ss, self.rs = slot, ss, rs

        def copy(self, u, m, p, da, db, d):
            ref = self.slot(u, p, da, db)
            return rc(ref, ref, self.ss.at[u, m, p], self.rs.at[u, m, p], d)

        def send(self, u, m, p, da, db, d):
            self.copy(u, m, p, da, db, d).start()

        def wait(self, u, m, p, da, db):
            self.copy(u, m, p, da, db, sib).wait_recv()

        def bsend(self, u, k, p):
            da = da_of(k)
            self.send(u, 3 + 3 * k, p, da, 0, bp[u])
            self.send(u, 4 + 3 * k, p, da, 0, bm[u])

        def start_a(self, u):
            self.send(u, 0, 0, 0, 0, ap[u])
            self.send(u, 1, 1, 0, 0, am[u])
            self.send(u, 0, 1, 0, 0, ap[u])
            self.send(u, 1, 0, 0, 0, am[u])

        def start_b(self, u):
            self.send(u, 3, 0, 0, 0, bp[u])
            self.send(u, 4, 1, 0, 0, bm[u])
            self.send(u, 3, 1, 0, 0, bp[u])
            self.send(u, 4, 0, 0, 0, bm[u])

        def near0(self, u):
            self.wait(u, 0, 0, 3, 0)
            self.send(u, 2, 0, 3, 0, ap[u])
            self.wait(u, 1, 1, 1, 0)
            self.send(u, 2, 1, 1, 0, am[u])
            self.bsend(u, 2, 0)
            self.bsend(u, 1, 1)

        def near1(self, u):
            self.wait(u, 0, 1, 3, 0)
            self.bsend(u, 2, 1)
            self.wait(u, 1, 0, 1, 0)
            self.bsend(u, 1, 0)

        def far(self, u):
            self.wait(u, 2, 0, 2, 0)
            self.bsend(u, 3, 0)
            self.wait(u, 2, 1, 2, 0)
            self.bsend(u, 3, 1)

        def bfwd(self, u, k):
            da = da_of(k)
            self.wait(u, 3 + 3 * k, 0, da, 3)
            self.send(u, 5 + 3 * k, 0, da, 3, bp[u])
            self.wait(u, 4 + 3 * k, 1, da, 1)
            self.send(u, 5 + 3 * k, 1, da, 1, bm[u])

        def brest(self, u, k):
            da = da_of(k)
            self.wait(u, 3 + 3 * k, 1, da, 3)
            self.wait(u, 4 + 3 * k, 0, da, 1)

        def blast(self, u, k):
            da = da_of(k)
            self.wait(u, 5 + 3 * k, 0, da, 2)
            self.wait(u, 5 + 3 * k, 1, da, 2)

        def done(self):
            def body(m, carry):
                for u in UU:
                    for p in (0, 1):
                        self.copy(u, m, p, 0, 0, sib).wait_send()
                return carry

            lax.fori_loop(0, 15, body, 0)

    def wslot(u, p, da, db):
        return U.at[uidx(u, da, db), pl.ds(*PARTS[p])]

    ag = Gather(wslot, ag_s, ag_r)

    to_sib = rc(wu.at[1 - c], U.at[me * 2 + c], mi_s.at[0], mi_r.at[0], sib)
    to_sib.start()
    own = pltpu.make_async_copy(wu.at[c], U.at[me * 2 + c], loc.at[0])
    own.start()
    own.wait()
    ag.start_a(0)
    ag.start_b(0)
    rc(wu.at[0], U.at[me * 2 + 1 - c], mi_s.at[0], mi_r.at[0], sib).wait_recv()
    ag.start_a(1)
    ag.start_b(1)

    hacc[...] = jnp.zeros_like(hacc)
    get_p.wait()
    get_u.wait()

    def act_step(r, carry):
        r0 = pl.multiple_of(r * 16, 16)
        xs = xin[pl.ds(r0, 16), :].astype(F32)
        root = jnp.sqrt(jnp.sum(xs * xs, axis=1, keepdims=True) * (1.0 / 3200.0) + 1e-06)
        RM[pl.ds(r0, 16), :] = jnp.broadcast_to(root, (16, 128))
        up_live = uin[pl.ds(r0, 16), :].astype(F32)
        up_live = up_live * jnp.where(slots[r // 4] >= 0, 1.0, 0.0)
        nsc[0] = xs / root * VC[0, 0:1, :]
        nsc[1] = up_live * VC[1, 0:1, :]
        rsc[0] = up_live
        rsc[1] = xs
        lane = lax.broadcasted_iota(jnp.int32, (16, 256), 1)
        for i in range(32):
            q = min(100 * i // 128, 23)
            sh = 100 * i - 128 * q
            win = slice(128 * q, 128 * q + 256)
            a = pltpu.roll(nsc[0, :, win], (256 - sh) % 256, 1)
            b = pltpu.roll(nsc[1, :, win], (100 - sh) % 256, 1)
            both = jnp.where(lane < FE, a, jnp.where(lane < 2 * FE, b, 0.0))
            C2[c, i, pl.ds(r0, 16), :] = both.astype(BF)
            a = pltpu.roll(rsc[0, :, win], (256 - sh) % 256, 1)
            b = pltpu.roll(rsc[1, :, win], (4 - sh) % 256, 1)
            XU[i, pl.ds(r0, 16), :] = a[:, :128].astype(BF)
            XP[i, pl.ds(r0, 16), :] = b[:, :128].astype(BF)
        return carry

    for q in range(25):
        VC[0, :, 128 * q : 128 * q + 128] = jnp.broadcast_to(gain[q : q + 1, :], (8, 128))
        VC[1, :, 128 * q : 128 * q + 128] = jnp.broadcast_to(lscale[q : q + 1, :], (8, 128))
    for i in range(32):
        q = min(100 * i // 128, 23)
        sh = 100 * i - 128 * q
        win = slice(128 * q, 128 * q + 256)
        GU[0, i] = pltpu.roll(VC[0, :, win], (256 - sh) % 256, 1)[:, :128]
        GU[1, i] = pltpu.roll(VC[1, :, win], (4 - sh) % 256, 1)[:, :128]
    lax.fori_loop(0, 8, act_step, 0)
    act_sib = rc(C2.at[c], C2.at[c], mi_s.at[1], mi_r.at[1], sib)
    act_sib.start()
    to = lax.broadcasted_iota(jnp.int32, (512, 256), 0)
    fr = lax.rem(lax.broadcasted_iota(jnp.int32, (512, 256), 1), 64)
    same = fr == 32 * (to // 256) + 2 * lax.rem(to, 16) + lax.rem(to // 128, 2)
    PM[...] = jnp.where(same, (dp * BLK + lax.rem(to // 16, 8)).astype(F32), -5.0)

    def weight(i):
        w = U[i]
        return jnp.concatenate([w[0:208], w[208:416], w[416:624], WT[i]], axis=1)

    def up(i):
        act = jnp.concatenate([C2[0, i], C2[1, i]], axis=0)
        CT[i] = act.T[:UR]
        a = act[:, :UR]
        first = lax.broadcasted_iota(jnp.int32, a.shape, 1) < FE
        zero = jnp.zeros_like(a)
        lhs = jnp.concatenate([jnp.where(first, a, zero), jnp.where(first, zero, a)], axis=0)
        WT[i] = unfold_tail(U[i, 3 * UR : PK]).astype(BF)
        hacc[...] += jnp.dot(lhs, weight(i), preferred_element_type=F32)

    def up_all(units):
        for u, da, db in units:
            up(uidx(u, da, db))

    for u in UU:
        ag.near0(u)
    for u in UU:
        ag.near1(u)
    rc(C2.at[c], C2.at[1 - c], mi_s.at[1], mi_r.at[1], sib).wait_recv()
    for u in UU:
        ag.bfwd(u, 0)
    up_all([(0, 0, 0), (1, 0, 0)])
    for u in UU:
        ag.far(u)
    up_all([(u, da, 0) for u in UU for da in (3, 1)])

    def fwd_step(k, carry):
        for u in UU:
            ag.bfwd(u, k)
        for u in UU:
            ag.brest(u, k - 1)
        up_all([(u, da_of(k - 1), db) for u in UU for db in (3, 1)])
        return carry

    lax.fori_loop(1, 4, fwd_step, 0)
    up_all([(0, 2, 0), (1, 2, 0)])

    def last_step(k, carry):
        for u in UU:
            ag.blast(u, k)
        up_all([(u, da_of(k), 2) for u in UU])
        return carry

    lax.fori_loop(0, 3, last_step, 0)
    for u in UU:
        ag.brest(u, 3)
    up_all([(u, da_of(3), db) for u in UU for db in (3, 1)])
    last_step(3, 0)

    def gelu_step(r, carry):
        r0 = pl.multiple_of(r * 32, 32)
        h = hacc[pl.ds(r0, 32), :]
        gh = hacc[pl.ds(r0 + 256, 32), :]
        valid = lax.broadcasted_iota(jnp.int32, h.shape, 1) < HH
        cumul = 0.5 * (1.0 + lax.erf(h * 0.7071067811865476))
        density = jnp.exp(-0.5 * h * h) * 0.3989422804014327
        ho = jnp.where(valid, h * cumul, 0.0).astype(BF)
        gi = jnp.where(valid, gh * (cumul + h * density), 0.0).astype(BF)
        S[pl.ds(r0, 32), :] = gi
        S[pl.ds(r0 + 256, 32), :] = ho
        row = jnp.sum(gi.astype(F32) * jnp.where(valid, h, 0.0), axis=1, keepdims=True)
        cen[pl.ds(r0, 32), :] = jnp.broadcast_to(row, (32, 128))
        return carry

    lax.fori_loop(0, 8, gelu_step, 0)

    def down(i):
        ct = CT[i]
        first = lax.broadcasted_iota(jnp.int32, ct.shape, 0) < FE
        zero = jnp.zeros_like(ct)
        lhs = jnp.concatenate([jnp.where(first, ct, zero), jnp.where(first, zero, ct)], axis=1)
        out = jnp.dot(lhs, S[...], preferred_element_type=F32)
        return [out[:, 0:128], out[:, 128:256], out[:, 256:384], fold_tail(out[:, 384:512])]

    ROWS4 = ((0, 208), (208, 416), (416, 624), (624, 656))

    def store_unit(i, *adds):
        for (lo, hi), part in zip(ROWS4, down(i)):
            for ref in adds:
                part = part + ref[lo:hi].astype(F32)
            PG[i, lo:hi] = part.astype(BF)

    def add_part(i, p, ref):
        lo, n = PARTS[p]
        PG[i, lo : lo + n] = (PG[i, lo : lo + n].astype(F32) + ref[lo : lo + n].astype(F32)).astype(BF)

    def rs(u, m, p, i, buf, d):
        return rc(
            PG.at[i, pl.ds(*PARTS[p])], buf.at[pl.ds(*PARTS[p])], rs_s.at[u, m, p], rs_r.at[u, m, p], d
        )

    def rs_wait(u, m, p, buf):
        rs(u, m, p, 0, buf, sib).wait_recv()

    def first_down(kk, carry):
        k = 3 - kk
        for u in UU:
            i = uidx(u, da_of(k), 2)
            store_unit(i)
            rs(u, 3 + 3 * k, 0, i, rb1.at[u, k], bp[u]).start()
            rs(u, 3 + 3 * k, 1, i, rb1.at[u, k], bm[u]).start()
        return carry

    def second_free(k):
        for u in UU:
            i = uidx(u, da_of(k), 1)
            store_unit(i)
            rs(u, 4 + 3 * k, 1, i, rb2.at[u, 0, k], bp[u]).start()
            i = uidx(u, da_of(k), 3)
            store_unit(i)
            rs(u, 5 + 3 * k, 0, i, rb2.at[u, 1, k], bm[u]).start()

    def second_sum(k):
        for u in UU:
            i = uidx(u, da_of(k), 1)
            rs_wait(u, 3 + 3 * k, 0, rb1.at[u, k])
            add_part(i, 0, rb1.at[u, k])
            rs(u, 4 + 3 * k, 0, i, rb2.at[u, 0, k], bp[u]).start()
            i = uidx(u, da_of(k), 3)
            rs_wait(u, 3 + 3 * k, 1, rb1.at[u, k])
            add_part(i, 1, rb1.at[u, k])
            rs(u, 5 + 3 * k, 1, i, rb2.at[u, 1, k], bm[u]).start()

    def second_down(kk, carry):
        second_free(3 - kk)
        second_sum(3 - kk)
        return carry

    def third(u, k):
        for w in (0, 1):
            for p in (1, 0) if w == 0 else (0, 1):
                rs_wait(u, 4 + 3 * k + w, p, rb2.at[u, w, k])
        i = uidx(u, da_of(k), 0)
        store_unit(i, rb2.at[u, 0, k], rb2.at[u, 1, k])
        return i

    def zblk(r):
        return lax.rem(z + r, 8)

    def mix(b):
        def body(j, carry):
            i = b * 4 + j
            w = weight(i)
            m = jnp.dot(w[96:208], ST[:, 256:512], preferred_element_type=F32)
            row = lax.broadcasted_iota(jnp.int32, m.shape, 0)
            m = jnp.where(row == 104, cen_hi, jnp.where(row == 105, cen_lo, m)).astype(BF)
            n = jnp.dot(w[0:112], ST[:, 0:256], preferred_element_type=F32).astype(BF)
            for e in (0, 1):
                M[e, 0, i] = m[:, 128 * e : 128 * e + 128]
                M[e, 1, i] = n[:, 128 * e : 128 * e + 128]
            return carry

        lax.fori_loop(0, 4, body, 0)

    def to_sibling(s, r):
        b = 4 * zblk(r)
        return rc(
            M.at[1 - c, :, pl.ds(b, 4)], MR.at[:, pl.ds(b, 4)], sq_s.at[s], sq_r.at[s], sib
        )

    zorder = (4, 3, 5, 2, 6, 1, 7, 0)

    def mix_step(s, carry):
        h = (s + 1) // 2
        r = 4 + h - 2 * h * lax.rem(s, 2)
        mix(zblk(r))
        to_sibling(s, r).start()
        return carry

    def zcopy(t, way, j, h):
        r = 4 + j if way == 0 else 4 - j
        buf = zrm if way == 0 else zrp
        return rc(
            M.at[c, t, pl.ds(4 * zblk(r) + 2 * h, 2)], buf.at[t, j, pl.ds(2 * h, 2)],
            zz_s.at[t, way, j, h], zz_r.at[t, way, j, h], zdev(7 if way == 0 else 1),
        )

    def combine(t, r, h, ref):
        b = zblk(r)
        for j in (2 * h, 2 * h + 1):
            i = b * 4 + j
            v = M[c, t, i].astype(F32) + MR[t, i].astype(F32)
            if ref is not None:
                v = v + ref[j].astype(F32)
            M[c, t, i] = v.astype(BF)

    def zfirst(t):
        if t == 0:
            to_sibling(0, 4).wait_recv()
        for way in (0, 1):
            combine(t, 4, way, None)
            zcopy(t, way, 0, way).start()

    def zstep(t, j):
        for n in (0, 1):
            for way in (0, 1):
                buf = zrm if way == 0 else zrp
                r = 4 + j if way == 0 else 4 - j
                if n == 0 and t == 0:
                    to_sibling(2 * j if way == 0 else 2 * j - 1, r).wait_recv()
                h = (1 - way if n == 0 else way) if j == 1 else n
                if j == 1 and n == 0:
                    combine(t, r, h, None)
                else:
                    zcopy(t, way, j - 1, h).wait_recv()
                    combine(t, r, h, buf.at[t, j - 1])
                zcopy(t, way, j, h).start()

    def zlast(t, j):
        i = z * 4 + j
        v = M[c, t, i].astype(F32) + MR[t, i].astype(F32)
        v = v + zrm[t, 3, j].astype(F32) + zrp[t, 3, j].astype(F32)
        return jnp.concatenate([v, jnp.zeros((16, 128), F32)], axis=0).T

    lax.fori_loop(0, 2, first_down, 0)
    ST[...] = S[...].T
    center = cen[...].T[0:1]
    cen_hi = center.astype(BF).astype(F32)
    cen_lo = center - cen_hi
    lax.fori_loop(0, 2, mix_step, 0)
    lax.fori_loop(2, 4, first_down, 0)
    lax.fori_loop(2, 4, mix_step, 0)
    zfirst(0)
    second_free(3)
    lax.fori_loop(4, 8, mix_step, 0)
    zstep(0, 1)
    zfirst(1)
    second_sum(3)
    lax.fori_loop(1, 4, second_down, 0)
    zstep(0, 2)
    zstep(1, 1)

    for u in UU:
        i = third(u, 3)
        rs(u, 0, 0, i, ra1.at[u], ap[u]).start()
        rs(u, 0, 1, i, ra1.at[u], am[u]).start()
    for u in UU:
        i = third(u, 2)
        rs(u, 2, 0, i, ra2.at[u, 1], am[u]).start()
    zstep(0, 3)
    zstep(1, 2)
    for u in UU:
        i = third(u, 1)
        rs(u, 1, 1, i, ra2.at[u, 0], ap[u]).start()
    for u in UU:
        rs_wait(u, 0, 0, ra1.at[u])
        i = uidx(u, 1, 0)
        add_part(i, 0, ra1.at[u])
        rs(u, 1, 0, i, ra2.at[u, 0], ap[u]).start()
        rs_wait(u, 0, 1, ra1.at[u])
        i = uidx(u, 3, 0)
        add_part(i, 1, ra1.at[u])
        rs(u, 2, 1, i, ra2.at[u, 1], am[u]).start()

    to_sibling(7, 0).wait_recv()
    for h in (0, 1):
        for way in (0, 1):
            zcopy(0, way, 3, h).wait_recv()
    ln = lax.broadcasted_iota(jnp.int32, (128, 128), 1)
    wide = [jnp.zeros((128, 128), F32) for _ in range(4)]
    centre = None
    for j in range(4):
        t = zlast(0, j)
        if j == 0:
            centre = (t[:, 104:105] + t[:, 105:106]) * (1.0 / 3200.0)
        i = z * 4 + j
        r = XP[i].astype(F32) + GU[1, i][0:1] * t
        at, sh = divmod(FE * j, 128)
        r = pltpu.roll(r, (sh + 124) % 128, 1)
        wide[at] = jnp.where((ln >= sh) & (ln < sh + FE), r, wide[at])
        if sh + FE > 128:
            wide[at + 1] = jnp.where(ln < sh + FE - 128, r, wide[at + 1])
    cen[0:128, :] = jnp.broadcast_to(centre, (128, 128))
    tail = jnp.where(ln < 16, wide[3], 0.0)
    folded = tail[0:16]
    for g in range(1, 8):
        folded = folded + pltpu.roll(tail[16 * g : 16 * g + 16], 16 * g, 1)
    for t in range(3):
        V[c, me, 128 * t : 128 * t + 128, :] = wide[t].astype(BF)
    V[c, me, 384:400, :] = folded.astype(BF)

    VP = (((0, 112), (112, 96)), ((208, 96), (304, 96)))

    def vslot(u, p, da, db):
        return V.at[c, chip_of(u, da, db), pl.ds(*VP[u][p])]

    vg = Gather(vslot, vg_s, vg_r)

    def fwd(u, da, db):
        ch = chip_of(u, da, db)
        ref = V.at[c, ch, pl.ds(208 * u, 208 - 16 * u)]
        return rc(ref, ref, vf_s.at[u, ch], vf_r.at[u, ch], sib)

    for u in UU:
        vg.start_a(u)
    for u in UU:
        vg.start_b(u)
    for u in UU:
        fwd(u, 0, 0).start()

    def finish(u):
        for w in (0, 1):
            for p in (1, 0) if w == 0 else (0, 1):
                rs_wait(u, 4 + w, p, rb2.at[u, w, 0])
        i = uidx(u, 0, 0)
        parts = down(i)
        for w in (0, 1):
            for p in (1, 0) if w == 0 else (0, 1):
                rs_wait(u, 1 + w, p, ra2.at[u, w])
        out = []
        for (lo, hi), part in zip(ROWS4, parts):
            for ref in (rb2.at[u, 0, 0], rb2.at[u, 1, 0], ra2.at[u, 0], ra2.at[u, 1]):
                part = part + ref[lo:hi].astype(F32)
            out.append(part)
        return i, out

    zstep(1, 3)
    i, parts = finish(1)
    for (lo, hi), part in zip(ROWS4, parts):
        PG[i, lo:hi] = part.astype(BF)
    to_fin = rc(PG.at[i], fin, mi_s.at[2], mi_r.at[2], sib)
    to_fin.start()
    for u in UU:
        vg.near0(u)
    for u in UU:
        vg.near1(u)
    for u in UU:
        fwd(u, 3, 0).start()
        fwd(u, 1, 0).start()
    for u in UU:
        vg.bfwd(u, 0)
    _, parts = finish(0)
    for t in range(3):
        GS[:, 128 * t : 128 * t + 128] = parts[t]
    GS[:, 384:512] = unfold_tail(parts[3])
    for u in UU:
        vg.far(u)
        fwd(u, 2, 0).start()

    hacc[...] = jnp.zeros_like(hacc)

    for h in (0, 1):
        for way in (0, 1):
            zcopy(1, way, 3, h).wait_recv()
    root = RM[:, 0:1]
    centre = cen[0:128, 0:1]
    for j in range(4):
        i = z * 4 + j
        t = zlast(1, j)
        moved = pltpu.roll(XP[i].astype(F32), 124, 1)
        gp = XU[i].astype(F32) + (GU[0, i][0:1] * t - moved / root * centre) / root
        GP[FE * j : FE * j + FE, :] = gp.T[:FE]
    gp_out[...] = GP[...].astype(BF)

    def take(ch):
        for u in UU:
            ref = V.at[1 - c, ch, pl.ds(208 * u, 208 - 16 * u)]
            rc(ref, ref, vf_s.at[u, ch], vf_r.at[u, ch], sib).wait_recv()
        rows = []
        blocks = []
        ln = lax.broadcasted_iota(jnp.int32, (1, 128), 1)
        for e in (0, 1):
            tail = V[e, ch, 384:400].astype(F32)
            tail = [tail] + [pltpu.roll(tail, 128 - 16 * g, 1) for g in range(1, 8)]
            tail = jnp.concatenate(tail, axis=0).astype(BF)
            rows.append(
                jnp.concatenate([V[e, ch, 128 * t : 128 * t + 128] for t in range(3)] + [tail], axis=1)
            )
            pair = U[2 * ch + e, 192:208].astype(F32)[8:9]
            blocks.append(jnp.where(ln < 64, pair[:, 0:1], pair[:, 1:2]))
        place = (PM[...] == jnp.concatenate(blocks, axis=1)).astype(BF)
        hacc[...] += jnp.dot(place, jnp.concatenate(rows, axis=0), preferred_element_type=F32)

    def take4(kind):
        def body(n, carry):
            h, m = n // 2, lax.rem(n, 2)
            if kind == 0:
                dx, dy = (1 - m) * (n + 1), m * n
            elif kind == 1:
                dx, dy = 1 + 2 * m, 1 + 2 * h
            else:
                dx, dy = 2 * (1 - h) + h * (1 + 2 * m), (1 - h) * (1 + 2 * m) + 2 * h
            take(lax.rem(y + dy, 4) * 4 + lax.rem(x + dx, 4))
            return carry

        lax.fori_loop(0, 4, body, 0)

    def vstep(k, carry):
        for u in UU:
            vg.bfwd(u, k)
        for u in UU:
            vg.brest(u, k - 1)
            fwd(u, da_of(k - 1), 3).start()
            fwd(u, da_of(k - 1), 1).start()
        return carry

    take(me)
    vstep(1, 0)
    take4(0)
    lax.fori_loop(2, 4, vstep, 0)

    to_fin.wait_recv()
    mine = GS[...]
    other = [fin[208 * t : 208 * t + 208].astype(F32) for t in range(3)] + [unfold_tail(fin[624:656])]
    other = jnp.concatenate(other, axis=1)
    for h in (0, 1):
        half = jnp.where(c == h, mine, other)
        gin_out[:, HH * h : HH * h + HH] = half[0:FE, 0:HH]
        gout_out[:, HH * h : HH * h + HH] = half[FE : 2 * FE, 0:HH]

    take4(1)
    for u in UU:
        vg.brest(u, 3)
        fwd(u, 2, 3).start()
        fwd(u, 2, 1).start()
    for k in range(4):
        for u in UU:
            vg.blast(u, k)
            fwd(u, da_of(k), 2).start()
        if k == 0:
            take(lax.rem(y, 4) * 4 + lax.rem(x + 2, 4))
            take(lax.rem(y + 2, 4) * 4 + x)
        if k == 2:
            take4(2)
    take(lax.rem(y + 2, 4) * 4 + lax.rem(x + 2, 4))
    for q in range(4):
        vis_out[q] = hacc[128 * q : 128 * q + 128, :].astype(BF).T[:HH]

    def vfwd_wait(ch, carry):
        for u in UU:
            ref = V.at[1 - c, ch, pl.ds(208 * u, 208 - 16 * u)]
            rc(ref, ref, vf_s.at[u, ch], vf_r.at[u, ch], sib).wait_send()
        return carry

    lax.fori_loop(0, 16, vfwd_wait, 0)

    ag.done()
    vg.done()
    to_sib.wait_send()
    act_sib.wait_send()
    to_fin.wait_send()
    for s in range(8):
        to_sibling(s, zorder[s]).wait_send()
    for t in (0, 1):
        for way in (0, 1):
            zcopy(t, way, 0, way).wait_send()
            for j in (1, 2, 3):
                for h in (0, 1):
                    zcopy(t, way, j, h).wait_send()

    def rs_done(m, carry):
        for u in UU:
            for p in (0, 1):
                rs(u, m, p, 0, ra1.at[u], sib).wait_send()
        return carry

    lax.fori_loop(0, 15, rs_done, 0)


def mega(slots, w_in, w_out, gain, lscale, patches, upstream):
    dma = pltpu.SemaphoreType.DMA
    vm = pl.BlockSpec(memory_space=pltpu.VMEM)
    sm = pl.BlockSpec(memory_space=pltpu.SMEM)
    hbm = pl.BlockSpec(memory_space=pl.ANY)
    return pl.pallas_call(
        kernel,
        out_shape=(
            jax.ShapeDtypeStruct((FE, 2 * HH), F32),
            jax.ShapeDtypeStruct((FE, 2 * HH), F32),
            jax.ShapeDtypeStruct((HH, 128), BF),
            jax.ShapeDtypeStruct((4, HH, BLK * 16), BF),
        ),
        in_specs=[sm, vm, vm, vm, vm, hbm, hbm],
        out_specs=(vm, vm, vm, vm),
        scratch_shapes=[
            pltpu.VMEM((128, 3200), BF),
            pltpu.VMEM((128, 3200), BF),
            pltpu.VMEM((2, 16, 3200), F32),
            pltpu.VMEM((2, 16, 3200), F32),
            pltpu.VMEM((128, 128), F32),
            pltpu.VMEM((2, 8, 3200), F32),
            pltpu.VMEM((512, 256), F32),
            pltpu.VMEM((UR, 896), F32),
            pltpu.VMEM((2, PK, 128), BF),
            pltpu.VMEM((2, 32, 8, 128), F32),
            pltpu.VMEM((32, PK, 128), BF),
            pltpu.VMEM((32, UR, 128), BF),
            pltpu.VMEM((2, 32, 128, 256), BF),
            pltpu.VMEM((32, 128, 128), BF),
            pltpu.VMEM((32, 128, 128), BF),
            pltpu.VMEM((32, UR, 256), BF),
            pltpu.VMEM((512, 512), F32),
            pltpu.VMEM((512, 512), BF),
            pltpu.VMEM((512, 512), BF),
            pltpu.VMEM((32, PK, 128), BF),
            pltpu.VMEM((2, 4, PK, 128), BF),
            pltpu.VMEM((2, 2, 4, PK, 128), BF),
            pltpu.VMEM((2, PK, 128), BF),
            pltpu.VMEM((2, 2, PK, 128), BF),
            pltpu.VMEM((PK, 128), BF),
            pltpu.VMEM((UR, 512), F32),
            pltpu.VMEM((2, 2, 32, 112, 128), BF),
            pltpu.VMEM((2, 32, 112, 128), BF),
            pltpu.VMEM((2, 4, 4, 112, 128), BF),
            pltpu.VMEM((2, 4, 4, 112, 128), BF),
            pltpu.VMEM((2, 16, 400, 128), BF),
            pltpu.VMEM((HH, 128), F32),
            pltpu.VMEM((256, 128), F32),
            dma((2, 15, 2)), dma((2, 15, 2)),
            dma((2, 15, 2)), dma((2, 15, 2)),
            dma((2, 15, 2)), dma((2, 15, 2)),
            dma((2, 16)), dma((2, 16)),
            dma((8,)), dma((8,)),
            dma((2, 2, 4, 2)), dma((2, 2, 4, 2)),
            dma((3,)), dma((3,)),
            dma((3,)),
        ],
        compiler_params=pltpu.CompilerParams(
            collective_id=0, has_side_effects=True, vmem_limit_bytes=60 * 2**20
        ),
    )(slots, w_in, w_out, gain, lscale, patches, upstream)


def shards(patches, upstream, norm_gain, layer_scale, w_in, w_out, slot_block):
    grad_w_in, grad_w_out, grad_patches, vision = mega(
        slot_block, w_in, w_out.T, norm_gain.reshape(25, 128), layer_scale.reshape(25, 128), patches, upstream
    )
    return (vision.transpose(2, 0, 1), grad_patches.T, grad_w_in, grad_w_out.T)


def solution(mesh):
    return jax.shard_map(
        shards,
        mesh=mesh,
        in_specs=(P("dp", None), P("dp", None), P(), P(), P("dp", "mp"), P("mp", "dp"), P("dp")),
        out_specs=(P("dp", None, "mp"), P("dp", "mp"), P("dp", "mp"), P("mp", "dp")),
        check_vma=False,
    )
```

```python
import jax
import jax.numpy as jnp
from jax import lax
from jax.experimental import pallas as pl
from jax.experimental.pallas import tpu as pltpu
from jax.sharding import PartitionSpec as P

BLK = 8
FE = 100
HH = 400
UR = 208
PK = 656
HA = 336
PARTS = ((0, HA), (HA, PK - HA))
MESH = pl.DeviceIdType.MESH
F32 = jnp.float32
BF = jnp.bfloat16


def fold_tail(tail):
    tail = jnp.concatenate([tail, jnp.zeros((16, 128), F32)], axis=0)
    out = tail[0:32]
    for g in range(1, 7):
        out = out + pltpu.roll(tail[32 * g : 32 * g + 32], 16 * g, 1)
    return out


def unfold_tail(packed):
    packed = packed.astype(F32)
    rows = [packed] + [pltpu.roll(packed, 128 - 16 * g, 1) for g in range(1, 7)]
    return jnp.concatenate(rows, axis=0)[:UR]


def kernel(
    slots, w_in, w_out, gain, lscale, patches, upstream, gin_out, gout_out, gp_out, vis_out,
    xin, uin, nsc, rsc, RM, VC, PM, VT, WB, wu, GU, U, WT, C2, XU, XP, CT, hacc, S, ST, PG, rb1, rb2, ra1, ra2, fin, GS,
    M, MR, zrm, zrp, V, GP, cen,
    ag_s, ag_r, rs_s, rs_r, vg_s, vg_r, vf_s, vf_r, sq_s, sq_r, zz_s, zz_r, mi_s, mi_r, loc,
):
    dp = lax.axis_index("dp")
    z = lax.axis_index("mp")
    c = lax.rem(dp, 2)
    x = lax.rem(dp // 2, 4)
    y = dp // 8
    me = y * 4 + x
    UU = (0, 1)

    def chip_of(u, da, db):
        if u == 0:
            return lax.rem(y + db, 4) * 4 + lax.rem(x + da, 4)
        return lax.rem(y + da, 4) * 4 + lax.rem(x + db, 4)

    def dev(u, da, db):
        return (chip_of(u, da, db) * 2 + c, z)

    def zdev(dz):
        return (dp, lax.rem(z + dz, 8))

    sib = (me * 2 + 1 - c, z)
    ap = [dev(u, 1, 0) for u in UU]
    am = [dev(u, 3, 0) for u in UU]
    bp = [dev(u, 0, 1) for u in UU]
    bm = [dev(u, 0, 3) for u in UU]
    nbrs = [sib, ap[0], am[0], bp[0], bm[0], zdev(1), zdev(7)]

    def rc(src, dst, ss, rs, d):
        return pltpu.make_async_remote_copy(
            src_ref=src, dst_ref=dst, send_sem=ss, recv_sem=rs, device_id=d, device_id_type=MESH
        )

    def uidx(u, da, db):
        return chip_of(u, da, db) * 2 + (c if u == 0 else 1 - c)

    def da_of(k):
        return k + k // 2 - 2 * (k // 3)

    get_p = pltpu.make_async_copy(patches, xin, loc.at[1])
    get_u = pltpu.make_async_copy(upstream, uin, loc.at[2])
    get_p.start()
    get_u.start()
    barrier = pltpu.get_barrier_semaphore()
    for d in nbrs:
        pl.semaphore_signal(barrier, inc=1, device_id=d, device_id_type=MESH)

    WB[0:FE, 0:800] = w_in[...].astype(F32)
    WB[FE : 2 * FE, 0:800] = w_out[...].astype(F32)
    at = lax.broadcasted_iota(jnp.int32, (8, 800), 1)
    at = jnp.where(at < HH, at, at - HH)
    slot0 = slots[0].astype(F32)
    slot1 = slots[1].astype(F32)
    WB[2 * FE : UR, 0:800] = jnp.where(at == 0, slot0, jnp.where(at == 1, slot1, 0.0))
    for h in (0, 1):
        part = WB[:, 0:512] if h == 0 else pltpu.roll(WB[:, 384:896], 496, 1)
        for t in range(3):
            wu[h, UR * t : UR * t + UR] = part[:, 128 * t : 128 * t + 128].astype(BF)
        tail = part[:, 384:512]
        tail = jnp.where(lax.broadcasted_iota(jnp.int32, tail.shape, 1) < 16, tail, 0.0)
        wu[h, 3 * UR : PK] = fold_tail(tail).astype(BF)
    pl.semaphore_wait(barrier, len(nbrs))

    class Gather:
        def __init__(self, slot, ss, rs):
            self.slot, self.ss, self.rs = slot, ss, rs

        def copy(self, u, m, p, da, db, d, src=None):
            ref = self.slot(u, p, da, db)
            src = ref if src is None else src.at[c, pl.ds(*PARTS[p])]
            return rc(src, ref, self.ss.at[u, m, p], self.rs.at[u, m, p], d)

        def send(self, u, m, p, da, db, d, src=None):
            self.copy(u, m, p, da, db, d, src).start()

        def wait(self, u, m, p, da, db):
            self.copy(u, m, p, da, db, sib).wait_recv()

        def bsend(self, u, k, p):
            da = da_of(k)
            self.send(u, 3 + 3 * k, p, da, 0, bp[u])
            self.send(u, 4 + 3 * k, p, da, 0, bm[u])

        def start_a(self, u, src=None):
            self.send(u, 0, 0, 0, 0, ap[u], src)
            self.send(u, 1, 1, 0, 0, am[u], src)
            self.send(u, 0, 1, 0, 0, ap[u], src)
            self.send(u, 1, 0, 0, 0, am[u], src)

        def start_b(self, u, src=None):
            self.send(u, 3, 0, 0, 0, bp[u], src)
            self.send(u, 4, 1, 0, 0, bm[u], src)
            self.send(u, 3, 1, 0, 0, bp[u], src)
            self.send(u, 4, 0, 0, 0, bm[u], src)

        def near0(self, u):
            self.wait(u, 0, 0, 3, 0)
            self.send(u, 2, 0, 3, 0, ap[u])
            self.wait(u, 1, 1, 1, 0)
            self.send(u, 2, 1, 1, 0, am[u])
            self.bsend(u, 2, 0)
            self.bsend(u, 1, 1)

        def near1(self, u):
            self.wait(u, 0, 1, 3, 0)
            self.bsend(u, 2, 1)
            self.wait(u, 1, 0, 1, 0)
            self.bsend(u, 1, 0)

        def far(self, u):
            self.wait(u, 2, 0, 2, 0)
            self.bsend(u, 3, 0)
            self.wait(u, 2, 1, 2, 0)
            self.bsend(u, 3, 1)

        def bfwd(self, u, k):
            da = da_of(k)
            self.wait(u, 3 + 3 * k, 0, da, 3)
            self.send(u, 5 + 3 * k, 0, da, 3, bp[u])
            self.wait(u, 4 + 3 * k, 1, da, 1)
            self.send(u, 5 + 3 * k, 1, da, 1, bm[u])

        def brest(self, u, k):
            da = da_of(k)
            self.wait(u, 3 + 3 * k, 1, da, 3)
            self.wait(u, 4 + 3 * k, 0, da, 1)

        def blast(self, u, k):
            da = da_of(k)
            self.wait(u, 5 + 3 * k, 0, da, 2)
            self.wait(u, 5 + 3 * k, 1, da, 2)

        def done(self):
            def body(m, carry):
                for u in UU:
                    for p in (0, 1):
                        self.copy(u, m, p, 0, 0, sib).wait_send()
                return carry

            lax.fori_loop(0, 15, body, 0)

    def wslot(u, p, da, db):
        return U.at[uidx(u, da, db), pl.ds(*PARTS[p])]

    ag = Gather(wslot, ag_s, ag_r)

    to_sib = rc(wu.at[1 - c], U.at[me * 2 + c], mi_s.at[0], mi_r.at[0], sib)
    to_sib.start()
    own = pltpu.make_async_copy(wu.at[c], U.at[me * 2 + c], loc.at[0])
    own.start()
    ag.start_a(0, wu)
    ag.start_b(0, wu)
    rc(wu.at[0], U.at[me * 2 + 1 - c], mi_s.at[0], mi_r.at[0], sib).wait_recv()
    ag.start_a(1)
    ag.start_b(1)

    hacc[...] = jnp.zeros_like(hacc)
    get_p.wait()
    get_u.wait()

    def act_step(r, carry):
        r0 = pl.multiple_of(r * 16, 16)
        xs = xin[pl.ds(r0, 16), :].astype(F32)
        root = jnp.sqrt(jnp.sum(xs * xs, axis=1, keepdims=True) * (1.0 / 3200.0) + 1e-06)
        RM[pl.ds(r0, 16), :] = jnp.broadcast_to(root, (16, 128))
        up_live = uin[pl.ds(r0, 16), :].astype(F32)
        up_live = up_live * jnp.where(slots[r // 4] >= 0, 1.0, 0.0)
        nsc[0] = xs / root * VC[0, 0:1, :]
        nsc[1] = up_live * VC[1, 0:1, :]
        rsc[0] = up_live
        rsc[1] = xs
        lane = lax.broadcasted_iota(jnp.int32, (16, 256), 1)
        for i in range(32):
            q = min(100 * i // 128, 23)
            sh = 100 * i - 128 * q
            win = slice(128 * q, 128 * q + 256)
            a = pltpu.roll(nsc[0, :, win], (256 - sh) % 256, 1)
            b = pltpu.roll(nsc[1, :, win], (100 - sh) % 256, 1)
            both = jnp.where(lane < FE, a, jnp.where(lane < 2 * FE, b, 0.0))
            C2[c, i, pl.ds(r0, 16), :] = both.astype(BF)
            a = pltpu.roll(rsc[0, :, win], (256 - sh) % 256, 1)
            b = pltpu.roll(rsc[1, :, win], (4 - sh) % 256, 1)
            XU[i, pl.ds(r0, 16), :] = a[:, :128].astype(BF)
            XP[i, pl.ds(r0, 16), :] = b[:, :128].astype(BF)
        return carry

    for q in range(25):
        VC[0, :, 128 * q : 128 * q + 128] = jnp.broadcast_to(gain[q : q + 1, :], (8, 128))
        VC[1, :, 128 * q : 128 * q + 128] = jnp.broadcast_to(lscale[q : q + 1, :], (8, 128))
    for i in range(32):
        q = min(100 * i // 128, 23)
        sh = 100 * i - 128 * q
        win = slice(128 * q, 128 * q + 256)
        GU[0, i] = pltpu.roll(VC[0, :, win], (256 - sh) % 256, 1)[:, :128]
        GU[1, i] = pltpu.roll(VC[1, :, win], (4 - sh) % 256, 1)[:, :128]
    lax.fori_loop(0, 8, act_step, 0)
    act_sib = rc(C2.at[c], C2.at[c], mi_s.at[1], mi_r.at[1], sib)
    act_sib.start()
    def weight(i):
        w = U[i]
        return jnp.concatenate([w[0:208], w[208:416], w[416:624], WT[i]], axis=1)

    def up(i):
        act = jnp.concatenate([C2[0, i], C2[1, i]], axis=0)
        CT[i] = act.T[:UR]
        a = act[:, :UR]
        first = lax.broadcasted_iota(jnp.int32, a.shape, 1) < FE
        zero = jnp.zeros_like(a)
        lhs = jnp.concatenate([jnp.where(first, a, zero), jnp.where(first, zero, a)], axis=0)
        WT[i] = unfold_tail(U[i, 3 * UR : PK]).astype(BF)
        hacc[...] += jnp.dot(lhs, weight(i), preferred_element_type=F32)

    def up_all(units):
        for u, da, db in units:
            up(uidx(u, da, db))

    for u in UU:
        ag.near0(u)
    for u in UU:
        ag.near1(u)
    rc(C2.at[c], C2.at[1 - c], mi_s.at[1], mi_r.at[1], sib).wait_recv()
    for u in UU:
        ag.bfwd(u, 0)
    own.wait()
    up_all([(0, 0, 0), (1, 0, 0)])
    for u in UU:
        ag.far(u)
    up_all([(u, da, 0) for u in UU for da in (3, 1)])

    def fwd_step(k, carry):
        for u in UU:
            ag.bfwd(u, k)
        for u in UU:
            ag.brest(u, k - 1)
        up_all([(u, da_of(k - 1), db) for u in UU for db in (3, 1)])
        return carry

    lax.fori_loop(1, 4, fwd_step, 0)
    up_all([(0, 2, 0), (1, 2, 0)])

    def last_step(k, carry):
        for u in UU:
            ag.blast(u, k)
        up_all([(u, da_of(k), 2) for u in UU])
        return carry

    lax.fori_loop(0, 3, last_step, 0)
    for u in UU:
        ag.brest(u, 3)
    up_all([(u, da_of(3), db) for u in UU for db in (3, 1)])
    last_step(3, 0)

    def gelu_step(r, carry):
        r0 = pl.multiple_of(r * 32, 32)
        h = hacc[pl.ds(r0, 32), :]
        gh = hacc[pl.ds(r0 + 256, 32), :]
        valid = lax.broadcasted_iota(jnp.int32, h.shape, 1) < HH
        cumul = 0.5 * (1.0 + lax.erf(h * 0.7071067811865476))
        density = jnp.exp(-0.5 * h * h) * 0.3989422804014327
        ho = jnp.where(valid, h * cumul, 0.0).astype(BF)
        gi = jnp.where(valid, gh * (cumul + h * density), 0.0).astype(BF)
        S[pl.ds(r0, 32), :] = gi
        S[pl.ds(r0 + 256, 32), :] = ho
        row = jnp.sum(gi.astype(F32) * jnp.where(valid, h, 0.0), axis=1, keepdims=True)
        cen[pl.ds(r0, 32), :] = jnp.broadcast_to(row, (32, 128))
        return carry

    lax.fori_loop(0, 8, gelu_step, 0)

    def down_all(units):
        lows = jnp.concatenate([CT[i, 0:112] for i in units], axis=0)
        highs = jnp.concatenate([CT[i, 96:208] for i in units], axis=0)
        lows = jnp.dot(lows, S[0:256], preferred_element_type=F32)
        highs = jnp.dot(highs, S[256:512], preferred_element_type=F32)
        row = lax.broadcasted_iota(jnp.int32, (16, 512), 0)
        res = []
        for n in range(len(units)):
            low, high = lows[112 * n : 112 * n + 112], highs[112 * n : 112 * n + 112]
            mid = jnp.where(row < 4, low[96:112], high[0:16])
            out = jnp.concatenate([low[0:96], mid, high[16:112]], axis=0)
            tail = fold_tail(out[:, 384:512])
            res.append([out[:, 0:128], out[:, 128:256], out[:, 256:384], tail])
        return res

    def down(i):
        return down_all([i])[0]

    ROWS4 = ((0, 208), (208, 416), (416, 624), (624, 656))

    def store_units(*units):
        for i, parts in zip(units, down_all(units)):
            for (lo, hi), part in zip(ROWS4, parts):
                PG[i, lo:hi] = part.astype(BF)

    def store_unit(i, *adds):
        for (lo, hi), part in zip(ROWS4, down(i)):
            for ref in adds:
                part = part + ref[lo:hi].astype(F32)
            PG[i, lo:hi] = part.astype(BF)

    def add_part(i, p, ref):
        lo, n = PARTS[p]
        PG[i, lo : lo + n] = (PG[i, lo : lo + n].astype(F32) + ref[lo : lo + n].astype(F32)).astype(BF)

    def rs(u, m, p, i, buf, d):
        return rc(
            PG.at[i, pl.ds(*PARTS[p])], buf.at[pl.ds(*PARTS[p])], rs_s.at[u, m, p], rs_r.at[u, m, p], d
        )

    def rs_wait(u, m, p, buf):
        rs(u, m, p, 0, buf, sib).wait_recv()

    def first_down(kk, carry):
        ks = (3 - 2 * kk, 2 - 2 * kk)
        store_units(*[uidx(u, da_of(k), 2) for k in ks for u in UU])
        for k in ks:
            for u in UU:
                i = uidx(u, da_of(k), 2)
                rs(u, 3 + 3 * k, 0, i, rb1.at[u, k], bp[u]).start()
                rs(u, 3 + 3 * k, 1, i, rb1.at[u, k], bm[u]).start()
        return carry

    def second_free(k):
        store_units(*[uidx(u, da_of(k), db) for db in (1, 3) for u in UU])
        for u in UU:
            rs(u, 4 + 3 * k, 1, uidx(u, da_of(k), 1), rb2.at[u, 0, k], bp[u]).start()
            rs(u, 5 + 3 * k, 0, uidx(u, da_of(k), 3), rb2.at[u, 1, k], bm[u]).start()

    def second_sum(k):
        for u in UU:
            i = uidx(u, da_of(k), 1)
            rs_wait(u, 3 + 3 * k, 0, rb1.at[u, k])
            add_part(i, 0, rb1.at[u, k])
            rs(u, 4 + 3 * k, 0, i, rb2.at[u, 0, k], bp[u]).start()
            i = uidx(u, da_of(k), 3)
            rs_wait(u, 3 + 3 * k, 1, rb1.at[u, k])
            add_part(i, 1, rb1.at[u, k])
            rs(u, 5 + 3 * k, 1, i, rb2.at[u, 1, k], bm[u]).start()

    def third(u, k):
        for w in (0, 1):
            for p in (1, 0) if w == 0 else (0, 1):
                rs_wait(u, 4 + 3 * k + w, p, rb2.at[u, w, k])
        i = uidx(u, da_of(k), 0)
        store_unit(i, rb2.at[u, 0, k], rb2.at[u, 1, k])
        return i

    def zblk(r):
        return lax.rem(z + r, 8)

    def mix(b):
        def rows(lo):
            tiles = []
            for j in range(4):
                w = [U[b * 4 + j, UR * t + lo : UR * t + lo + 112] for t in range(3)]
                tiles.append(jnp.concatenate(w + [WT[b * 4 + j, lo : lo + 112]], axis=1))
            return jnp.concatenate(tiles, axis=0)

        ms = jnp.dot(rows(96), ST[:, 256:512], preferred_element_type=F32)
        ns = jnp.dot(rows(0), ST[:, 0:256], preferred_element_type=F32).astype(BF)
        row = lax.broadcasted_iota(jnp.int32, (112, 256), 0)
        for j in range(4):
            m = ms[112 * j : 112 * j + 112]
            m = jnp.where(row == 104, cen_hi, jnp.where(row == 105, cen_lo, m)).astype(BF)
            n = ns[112 * j : 112 * j + 112]
            for e in (0, 1):
                M[e, 0, b * 4 + j] = m[:, 128 * e : 128 * e + 128]
                M[e, 1, b * 4 + j] = n[:, 128 * e : 128 * e + 128]

    def to_sibling(s, r):
        b = 4 * zblk(r)
        return rc(
            M.at[1 - c, :, pl.ds(b, 4)], MR.at[:, pl.ds(b, 4)], sq_s.at[s], sq_r.at[s], sib
        )

    zorder = (4, 3, 5, 2, 6, 1, 7, 0)

    def mix_step(s, carry):
        h = (s + 1) // 2
        r = 4 + h - 2 * h * lax.rem(s, 2)
        mix(zblk(r))
        to_sibling(s, r).start()
        return carry

    def zcopy(t, way, j, h):
        r = 4 + j if way == 0 else 4 - j
        buf = zrm if way == 0 else zrp
        return rc(
            M.at[c, t, pl.ds(4 * zblk(r) + 2 * h, 2)], buf.at[t, j, pl.ds(2 * h, 2)],
            zz_s.at[t, way, j, h], zz_r.at[t, way, j, h], zdev(7 if way == 0 else 1),
        )

    def combine(t, r, h, ref):
        b = zblk(r)
        for j in (2 * h, 2 * h + 1):
            i = b * 4 + j
            v = M[c, t, i].astype(F32) + MR[t, i].astype(F32)
            if ref is not None:
                v = v + ref[j].astype(F32)
            M[c, t, i] = v.astype(BF)

    def zfirst(t):
        if t == 0:
            to_sibling(0, 4).wait_recv()
        for way in (0, 1):
            combine(t, 4, way, None)
            zcopy(t, way, 0, way).start()

    def zstep(t, j):
        for n in (0, 1):
            for way in (0, 1):
                buf = zrm if way == 0 else zrp
                r = 4 + j if way == 0 else 4 - j
                if n == 0 and t == 0:
                    to_sibling(2 * j if way == 0 else 2 * j - 1, r).wait_recv()
                h = (1 - way if n == 0 else way) if j == 1 else n
                if j == 1 and n == 0:
                    combine(t, r, h, None)
                else:
                    zcopy(t, way, j - 1, h).wait_recv()
                    combine(t, r, h, buf.at[t, j - 1])
                zcopy(t, way, j, h).start()

    def zlast(t, j):
        i = z * 4 + j
        v = M[c, t, i].astype(F32) + MR[t, i].astype(F32)
        v = v + zrm[t, 3, j].astype(F32) + zrp[t, 3, j].astype(F32)
        return jnp.concatenate([v, jnp.zeros((16, 128), F32)], axis=0).T

    lax.fori_loop(0, 2, first_down, 0)
    second_free(3)
    ST[...] = S[...].T
    center = cen[...].T[0:1]
    cen_hi = center.astype(BF).astype(F32)
    cen_lo = center - cen_hi
    lax.fori_loop(0, 4, mix_step, 0)
    zfirst(0)
    second_free(2)
    second_sum(3)
    lax.fori_loop(4, 8, mix_step, 0)
    second_sum(2)
    zstep(0, 1)
    zfirst(1)
    second_free(1)
    second_sum(1)
    second_free(0)
    zstep(0, 2)
    second_sum(0)
    zstep(1, 1)

    for u in UU:
        i = third(u, 3)
        rs(u, 0, 0, i, ra1.at[u], ap[u]).start()
        rs(u, 0, 1, i, ra1.at[u], am[u]).start()
    zstep(0, 3)
    for u in UU:
        i = third(u, 2)
        rs(u, 2, 0, i, ra2.at[u, 1], am[u]).start()
    zstep(1, 2)
    for u in UU:
        i = third(u, 1)
        rs(u, 1, 1, i, ra2.at[u, 0], ap[u]).start()

    to_sibling(7, 0).wait_recv()
    for h in (0, 1):
        for way in (0, 1):
            zcopy(0, way, 3, h).wait_recv()
    ln = lax.broadcasted_iota(jnp.int32, (128, 128), 1)
    wide = [jnp.zeros((128, 128), F32) for _ in range(4)]
    centre = None
    for j in range(4):
        t = zlast(0, j)
        if j == 0:
            centre = (t[:, 104:105] + t[:, 105:106]) * (1.0 / 3200.0)
        i = z * 4 + j
        r = XP[i].astype(F32) + GU[1, i][0:1] * t
        at, sh = divmod(FE * j, 128)
        r = pltpu.roll(r, (sh + 124) % 128, 1)
        wide[at] = jnp.where((ln >= sh) & (ln < sh + FE), r, wide[at])
        if sh + FE > 128:
            wide[at + 1] = jnp.where(ln < sh + FE - 128, r, wide[at + 1])
    cen[0:128, :] = jnp.broadcast_to(centre, (128, 128))
    to, fr = (lax.broadcasted_iota(jnp.int32, (128, 128), d) for d in (0, 1))
    tr = lax.rem(to, 64)
    perm = fr == 64 * (to // 64) + 32 * (tr // 32) + 2 * lax.rem(tr, 16) + lax.rem(tr // 16, 2)
    wide = jnp.concatenate(wide, axis=1).astype(BF)
    wide = jnp.dot(perm.astype(BF), wide, preferred_element_type=F32)
    tail = jnp.where(ln < 16, wide[:, 384:512], 0.0)
    wide = [wide[:, 128 * t : 128 * t + 128].astype(BF) for t in range(3)]
    folded = tail[0:16]
    for g in range(1, 8):
        folded = folded + pltpu.roll(tail[16 * g : 16 * g + 16], 16 * g, 1)
    for t in range(3):
        V[c, me, 128 * t : 128 * t + 128, :] = wide[t]
    V[c, me, 384:400, :] = folded.astype(BF)

    VP = (((0, 112), (112, 96)), ((208, 96), (304, 96)))

    def vslot(u, p, da, db):
        return V.at[c, chip_of(u, da, db), pl.ds(*VP[u][p])]

    vg = Gather(vslot, vg_s, vg_r)

    def fwd(u, da, db):
        ch = chip_of(u, da, db)
        ref = V.at[c, ch, pl.ds(208 * u, 208 - 16 * u)]
        return rc(ref, ref, vf_s.at[u, ch], vf_r.at[u, ch], sib)

    for u in UU:
        vg.start_a(u)
    for u in UU:
        vg.start_b(u)
    for u in UU:
        fwd(u, 0, 0).start()

    zstep(1, 3)
    for u in UU:
        rs_wait(u, 0, 0, ra1.at[u])
        i = uidx(u, 1, 0)
        add_part(i, 0, ra1.at[u])
        rs(u, 1, 0, i, ra2.at[u, 0], ap[u]).start()
        rs_wait(u, 0, 1, ra1.at[u])
        i = uidx(u, 3, 0)
        add_part(i, 1, ra1.at[u])
        rs(u, 2, 1, i, ra2.at[u, 1], am[u]).start()

    def finish(u):
        for w in (0, 1):
            for p in (1, 0) if w == 0 else (0, 1):
                rs_wait(u, 4 + w, p, rb2.at[u, w, 0])
        i = uidx(u, 0, 0)
        parts = down(i)
        for w in (0, 1):
            for p in (1, 0) if w == 0 else (0, 1):
                rs_wait(u, 1 + w, p, ra2.at[u, w])
        out = []
        for (lo, hi), part in zip(ROWS4, parts):
            for ref in (rb2.at[u, 0, 0], rb2.at[u, 1, 0], ra2.at[u, 0], ra2.at[u, 1]):
                part = part + ref[lo:hi].astype(F32)
            out.append(part)
        return i, out

    for u in UU:
        vg.near0(u)
    for u in UU:
        vg.near1(u)
    for u in UU:
        fwd(u, 3, 0).start()
        fwd(u, 1, 0).start()
    for u in UU:
        vg.bfwd(u, 0)
    i, parts = finish(1)
    for (lo, hi), part in zip(ROWS4, parts):
        PG[i, lo:hi] = part.astype(BF)
    to_fin = rc(PG.at[i], fin, mi_s.at[2], mi_r.at[2], sib)
    to_fin.start()
    for u in UU:
        vg.far(u)
        fwd(u, 2, 0).start()
    _, parts = finish(0)
    for t in range(3):
        GS[:, 128 * t : 128 * t + 128] = parts[t]
    GS[:, 384:512] = unfold_tail(parts[3])
    for h in (0, 1):
        for way in (0, 1):
            zcopy(1, way, 3, h).wait_recv()
    root = RM[:, 0:1]
    centre = cen[0:128, 0:1]
    for j in range(4):
        i = z * 4 + j
        t = zlast(1, j)
        moved = pltpu.roll(XP[i].astype(F32), 124, 1)
        gp = XU[i].astype(F32) + (GU[0, i][0:1] * t - moved / root * centre) / root
        GP[FE * j : FE * j + FE, :] = gp.T[:FE]
    gp_out[...] = GP[...].astype(BF)

    table = U[:, 192:208, :].astype(F32)[:, 8, :]
    first_block = (dp * BLK).astype(F32)
    hit = (table >= first_block) & (table < first_block + BLK)
    hit = hit & (lax.broadcasted_iota(jnp.int32, table.shape, 1) < 2)
    least = jnp.min(jnp.where(hit, table, 1000.0))
    most = jnp.max(jnp.where(hit, table, -9.0))
    to, fr = (lax.broadcasted_iota(jnp.int32, (128, 256), d) for d in (0, 1))
    PM[...] = jnp.where(lax.rem(to, 64) == lax.rem(fr, 64), jnp.where(to < 64, least, most), -5.0)
    hacc[0:128] = jnp.zeros((128, 512), F32)

    def take(ch):
        for u in UU:
            ref = V.at[1 - c, ch, pl.ds(208 * u, 208 - 16 * u)]
            rc(ref, ref, vf_s.at[u, ch], vf_r.at[u, ch], sib).wait_recv()
        rows = []
        numbers = []
        ln = lax.broadcasted_iota(jnp.int32, (1, 128), 1)
        for e in (0, 1):
            tail = V[e, ch, 384:400].astype(F32)
            tail = [tail] + [pltpu.roll(tail, 128 - 16 * g, 1) for g in range(1, 8)]
            tail = jnp.concatenate(tail, axis=0).astype(BF)
            rows.append(
                jnp.concatenate([V[e, ch, 128 * t : 128 * t + 128] for t in range(3)] + [tail], axis=1)
            )
            pair = U[2 * ch + e, 192:208].astype(F32)[8:9]
            numbers.append(jnp.where(ln < 64, pair[:, 0:1], pair[:, 1:2]))
        place = (PM[...] == jnp.concatenate(numbers, axis=1)).astype(BF)
        hacc[0:128] += jnp.dot(place, jnp.concatenate(rows, axis=0), preferred_element_type=F32)

    def take4(kind):
        def body(n, carry):
            h, m = n // 2, lax.rem(n, 2)
            if kind == 0:
                dx, dy = (1 - m) * (n + 1), m * n
            elif kind == 1:
                dx, dy = 1 + 2 * m, 1 + 2 * h
            else:
                dx, dy = 2 * (1 - h) + h * (1 + 2 * m), (1 - h) * (1 + 2 * m) + 2 * h
            take(lax.rem(y + dy, 4) * 4 + lax.rem(x + dx, 4))
            return carry

        lax.fori_loop(0, 4, body, 0)

    def vstep(k, carry):
        for u in UU:
            vg.bfwd(u, k)
        for u in UU:
            vg.brest(u, k - 1)
            fwd(u, da_of(k - 1), 3).start()
            fwd(u, da_of(k - 1), 1).start()
        return carry

    lax.fori_loop(1, 4, vstep, 0)

    to_fin.wait_recv()
    mine = GS[...]
    other = [fin[208 * t : 208 * t + 208].astype(F32) for t in range(3)] + [unfold_tail(fin[624:656])]
    other = jnp.concatenate(other, axis=1)
    for h in (0, 1):
        half = jnp.where(c == h, mine, other)
        gin_out[:, HH * h : HH * h + HH] = half[0:FE, 0:HH]
        gout_out[:, HH * h : HH * h + HH] = half[FE : 2 * FE, 0:HH]

    for u in UU:
        vg.brest(u, 3)
        fwd(u, 2, 3).start()
        fwd(u, 2, 1).start()
    take(me)
    take4(0)
    take4(1)
    for k in range(4):
        for u in UU:
            vg.blast(u, k)
            fwd(u, da_of(k), 2).start()
        if k == 0:
            take(lax.rem(y, 4) * 4 + lax.rem(x + 2, 4))
            take(lax.rem(y + 2, 4) * 4 + x)
    take4(2)
    take(lax.rem(y + 2, 4) * 4 + lax.rem(x + 2, 4))
    low, high = hacc[0:64], hacc[64:128]
    for b in range(BLK):
        number = first_block + float(b)
        tile = jnp.where(least == number, low, jnp.where(most == number, high, 0.0)).astype(BF)
        for q in range(4):
            VT[q, 16 * b : 16 * b + 16, :] = tile[16 * q : 16 * q + 16]
    for q in range(4):
        vis_out[q] = VT[q].T[:HH]

    def vfwd_wait(ch, carry):
        for u in UU:
            ref = V.at[1 - c, ch, pl.ds(208 * u, 208 - 16 * u)]
            rc(ref, ref, vf_s.at[u, ch], vf_r.at[u, ch], sib).wait_send()
        return carry

    lax.fori_loop(0, 16, vfwd_wait, 0)

    ag.done()
    vg.done()
    to_sib.wait_send()
    act_sib.wait_send()
    to_fin.wait_send()
    for s in range(8):
        to_sibling(s, zorder[s]).wait_send()
    for t in (0, 1):
        for way in (0, 1):
            zcopy(t, way, 0, way).wait_send()
            for j in (1, 2, 3):
                for h in (0, 1):
                    zcopy(t, way, j, h).wait_send()

    def rs_done(m, carry):
        for u in UU:
            for p in (0, 1):
                rs(u, m, p, 0, ra1.at[u], sib).wait_send()
        return carry

    lax.fori_loop(0, 15, rs_done, 0)


def mega(slots, w_in, w_out, gain, lscale, patches, upstream):
    dma = pltpu.SemaphoreType.DMA
    vm = pl.BlockSpec(memory_space=pltpu.VMEM)
    sm = pl.BlockSpec(memory_space=pltpu.SMEM)
    hbm = pl.BlockSpec(memory_space=pl.ANY)
    return pl.pallas_call(
        kernel,
        out_shape=(
            jax.ShapeDtypeStruct((FE, 2 * HH), F32),
            jax.ShapeDtypeStruct((FE, 2 * HH), F32),
            jax.ShapeDtypeStruct((HH, 128), BF),
            jax.ShapeDtypeStruct((4, HH, BLK * 16), BF),
        ),
        in_specs=[sm, vm, vm, vm, vm, hbm, hbm],
        out_specs=(vm, vm, vm, vm),
        scratch_shapes=[
            pltpu.VMEM((128, 3200), BF),
            pltpu.VMEM((128, 3200), BF),
            pltpu.VMEM((2, 16, 3200), F32),
            pltpu.VMEM((2, 16, 3200), F32),
            pltpu.VMEM((128, 128), F32),
            pltpu.VMEM((2, 8, 3200), F32),
            pltpu.VMEM((128, 256), F32),
            pltpu.VMEM((4, 128, 512), BF),
            pltpu.VMEM((UR, 896), F32),
            pltpu.VMEM((2, PK, 128), BF),
            pltpu.VMEM((2, 32, 8, 128), F32),
            pltpu.VMEM((32, PK, 128), BF),
            pltpu.VMEM((32, UR, 128), BF),
            pltpu.VMEM((2, 32, 128, 256), BF),
            pltpu.VMEM((32, 128, 128), BF),
            pltpu.VMEM((32, 128, 128), BF),
            pltpu.VMEM((32, UR, 256), BF),
            pltpu.VMEM((512, 512), F32),
            pltpu.VMEM((512, 512), BF),
            pltpu.VMEM((512, 512), BF),
            pltpu.VMEM((32, PK, 128), BF),
            pltpu.VMEM((2, 4, PK, 128), BF),
            pltpu.VMEM((2, 2, 4, PK, 128), BF),
            pltpu.VMEM((2, PK, 128), BF),
            pltpu.VMEM((2, 2, PK, 128), BF),
            pltpu.VMEM((PK, 128), BF),
            pltpu.VMEM((UR, 512), F32),
            pltpu.VMEM((2, 2, 32, 112, 128), BF),
            pltpu.VMEM((2, 32, 112, 128), BF),
            pltpu.VMEM((2, 4, 4, 112, 128), BF),
            pltpu.VMEM((2, 4, 4, 112, 128), BF),
            pltpu.VMEM((2, 16, 400, 128), BF),
            pltpu.VMEM((HH, 128), F32),
            pltpu.VMEM((256, 128), F32),
            dma((2, 15, 2)), dma((2, 15, 2)),
            dma((2, 15, 2)), dma((2, 15, 2)),
            dma((2, 15, 2)), dma((2, 15, 2)),
            dma((2, 16)), dma((2, 16)),
            dma((8,)), dma((8,)),
            dma((2, 2, 4, 2)), dma((2, 2, 4, 2)),
            dma((3,)), dma((3,)),
            dma((3,)),
        ],
        compiler_params=pltpu.CompilerParams(
            collective_id=0, has_side_effects=True, vmem_limit_bytes=60 * 2**20
        ),
    )(slots, w_in, w_out, gain, lscale, patches, upstream)


def shards(patches, upstream, norm_gain, layer_scale, w_in, w_out, slot_block):
    grad_w_in, grad_w_out, grad_patches, vision = mega(
        slot_block, w_in, w_out.T, norm_gain.reshape(25, 128), layer_scale.reshape(25, 128), patches, upstream
    )
    return (vision.transpose(2, 0, 1), grad_patches.T, grad_w_in, grad_w_out.T)


def solution(mesh):
    return jax.shard_map(
        shards,
        mesh=mesh,
        in_specs=(P("dp", None), P("dp", None), P(), P(), P("dp", "mp"), P("mp", "dp"), P("dp")),
        out_specs=(P("dp", None, "mp"), P("dp", "mp"), P("dp", "mp"), P("mp", "dp")),
        check_vma=False,
    )
```

```python
import jax
import jax.numpy as jnp
from jax import lax
from jax.experimental import pallas as pl
from jax.experimental.pallas import tpu as pltpu
from jax.sharding import PartitionSpec as P

BLK = 8
FE = 100
HH = 400
UR = 208
PK = 656
HA = 336
PARTS = ((0, HA), (HA, PK - HA))
MESH = pl.DeviceIdType.MESH
F32 = jnp.float32
BF = jnp.bfloat16


def fold_tail(tail):
    tail = jnp.concatenate([tail, jnp.zeros((16, 128), F32)], axis=0)
    out = tail[0:32]
    for g in range(1, 7):
        out = out + pltpu.roll(tail[32 * g : 32 * g + 32], 16 * g, 1)
    return out


def unfold_tail(packed):
    packed = packed.astype(F32)
    rows = [packed] + [pltpu.roll(packed, 128 - 16 * g, 1) for g in range(1, 7)]
    return jnp.concatenate(rows, axis=0)[:UR]


def kernel(
    slots, w_in_hbm, w_out_hbm, gain_hbm, lscale_hbm, patches, upstream, gin_out, gout_out, gp_out, vis_out,
    gin_v, gout_v, gp_v, vis, w_in, w_out, gain, lscale, xin, uin, nsc, rsc, RM, VC, PM, VT, WB, wu, GU, U, WT, C2, XU, XP, CT, hacc, S, ST, PG, rb1, rb2, ra1, ra2, fin, GS,
    M, MR, zrm, zrp, V, GP, cen,
    ag_s, ag_r, rs_s, rs_r, vg_s, vg_r, vf_s, vf_r, sq_s, sq_r, zz_s, zz_r, mi_s, mi_r, loc,
):
    dp = lax.axis_index("dp")
    z = lax.axis_index("mp")
    c = lax.rem(dp, 2)
    x = lax.rem(dp // 2, 4)
    y = dp // 8
    me = y * 4 + x
    UU = (0, 1)

    def chip_of(u, da, db):
        if u == 0:
            return lax.rem(y + db, 4) * 4 + lax.rem(x + da, 4)
        return lax.rem(y + da, 4) * 4 + lax.rem(x + db, 4)

    def dev(u, da, db):
        return (chip_of(u, da, db) * 2 + c, z)

    def zdev(dz):
        return (dp, lax.rem(z + dz, 8))

    sib = (me * 2 + 1 - c, z)
    ap = [dev(u, 1, 0) for u in UU]
    am = [dev(u, 3, 0) for u in UU]
    bp = [dev(u, 0, 1) for u in UU]
    bm = [dev(u, 0, 3) for u in UU]
    nbrs = [sib, ap[0], am[0], bp[0], bm[0], zdev(1), zdev(7)]

    def rc(src, dst, ss, rs, d):
        return pltpu.make_async_remote_copy(
            src_ref=src, dst_ref=dst, send_sem=ss, recv_sem=rs, device_id=d, device_id_type=MESH
        )

    def uidx(u, da, db):
        return chip_of(u, da, db) * 2 + (c if u == 0 else 1 - c)

    def da_of(k):
        return k + k // 2 - 2 * (k // 3)

    get_p = pltpu.make_async_copy(patches, xin, loc.at[1])
    get_u = pltpu.make_async_copy(upstream, uin, loc.at[2])
    small = [
        pltpu.make_async_copy(a, b, loc.at[3 + n])
        for n, (a, b) in enumerate(
            ((w_in_hbm, w_in), (w_out_hbm, w_out), (gain_hbm, gain), (lscale_hbm, lscale))
        )
    ]
    for copy in small:
        copy.start()
    get_p.start()
    get_u.start()
    barrier = pltpu.get_barrier_semaphore()
    for d in nbrs:
        pl.semaphore_signal(barrier, inc=1, device_id=d, device_id_type=MESH)

    for copy in small:
        copy.wait()
    WB[0:FE, 0:800] = w_in[...].astype(F32)
    WB[FE : 2 * FE, 0:800] = w_out[...].astype(F32)
    at = lax.broadcasted_iota(jnp.int32, (8, 800), 1)
    at = jnp.where(at < HH, at, at - HH)
    slot0 = slots[0].astype(F32)
    slot1 = slots[1].astype(F32)
    WB[2 * FE : UR, 0:800] = jnp.where(at == 0, slot0, jnp.where(at == 1, slot1, 0.0))
    for h in (0, 1):
        part = WB[:, 0:512] if h == 0 else pltpu.roll(WB[:, 384:896], 496, 1)
        for t in range(3):
            wu[h, UR * t : UR * t + UR] = part[:, 128 * t : 128 * t + 128].astype(BF)
        tail = part[:, 384:512]
        tail = jnp.where(lax.broadcasted_iota(jnp.int32, tail.shape, 1) < 16, tail, 0.0)
        wu[h, 3 * UR : PK] = fold_tail(tail).astype(BF)
    pl.semaphore_wait(barrier, len(nbrs))

    class Gather:
        def __init__(self, slot, ss, rs):
            self.slot, self.ss, self.rs = slot, ss, rs

        def copy(self, u, m, p, da, db, d, src=None):
            ref = self.slot(u, p, da, db)
            src = ref if src is None else src.at[c, pl.ds(*PARTS[p])]
            return rc(src, ref, self.ss.at[u, m, p], self.rs.at[u, m, p], d)

        def send(self, u, m, p, da, db, d, src=None):
            self.copy(u, m, p, da, db, d, src).start()

        def wait(self, u, m, p, da, db):
            self.copy(u, m, p, da, db, sib).wait_recv()

        def bsend(self, u, k, p):
            da = da_of(k)
            self.send(u, 3 + 3 * k, p, da, 0, bp[u])
            self.send(u, 4 + 3 * k, p, da, 0, bm[u])

        def start_a(self, u, src=None):
            self.send(u, 0, 0, 0, 0, ap[u], src)
            self.send(u, 1, 1, 0, 0, am[u], src)
            self.send(u, 0, 1, 0, 0, ap[u], src)
            self.send(u, 1, 0, 0, 0, am[u], src)

        def start_b(self, u, src=None):
            self.send(u, 3, 0, 0, 0, bp[u], src)
            self.send(u, 4, 1, 0, 0, bm[u], src)
            self.send(u, 3, 1, 0, 0, bp[u], src)
            self.send(u, 4, 0, 0, 0, bm[u], src)

        def near0(self, u):
            self.wait(u, 0, 0, 3, 0)
            self.send(u, 2, 0, 3, 0, ap[u])
            self.wait(u, 1, 1, 1, 0)
            self.send(u, 2, 1, 1, 0, am[u])
            self.bsend(u, 2, 0)
            self.bsend(u, 1, 1)

        def near1(self, u):
            self.wait(u, 0, 1, 3, 0)
            self.bsend(u, 2, 1)
            self.wait(u, 1, 0, 1, 0)
            self.bsend(u, 1, 0)

        def far(self, u):
            self.wait(u, 2, 0, 2, 0)
            self.bsend(u, 3, 0)
            self.wait(u, 2, 1, 2, 0)
            self.bsend(u, 3, 1)

        def bfwd(self, u, k):
            da = da_of(k)
            self.wait(u, 3 + 3 * k, 0, da, 3)
            self.send(u, 5 + 3 * k, 0, da, 3, bp[u])
            self.wait(u, 4 + 3 * k, 1, da, 1)
            self.send(u, 5 + 3 * k, 1, da, 1, bm[u])

        def brest(self, u, k):
            da = da_of(k)
            self.wait(u, 3 + 3 * k, 1, da, 3)
            self.wait(u, 4 + 3 * k, 0, da, 1)

        def blast(self, u, k):
            da = da_of(k)
            self.wait(u, 5 + 3 * k, 0, da, 2)
            self.wait(u, 5 + 3 * k, 1, da, 2)

        def done(self):
            def body(m, carry):
                for u in UU:
                    for p in (0, 1):
                        self.copy(u, m, p, 0, 0, sib).wait_send()
                return carry

            lax.fori_loop(0, 15, body, 0)

    def wslot(u, p, da, db):
        return U.at[uidx(u, da, db), pl.ds(*PARTS[p])]

    ag = Gather(wslot, ag_s, ag_r)

    to_sib = rc(wu.at[1 - c], U.at[me * 2 + c], mi_s.at[0], mi_r.at[0], sib)
    to_sib.start()
    own = pltpu.make_async_copy(wu.at[c], U.at[me * 2 + c], loc.at[0])
    own.start()
    ag.start_a(0, wu)
    ag.start_b(0, wu)
    rc(wu.at[0], U.at[me * 2 + 1 - c], mi_s.at[0], mi_r.at[0], sib).wait_recv()
    ag.start_a(1)
    ag.start_b(1)

    hacc[...] = jnp.zeros_like(hacc)
    get_p.wait()
    get_u.wait()

    def act_step(r, carry):
        r0 = pl.multiple_of(r * 16, 16)
        xs = xin[pl.ds(r0, 16), :].astype(F32)
        root = jnp.sqrt(jnp.sum(xs * xs, axis=1, keepdims=True) * (1.0 / 3200.0) + 1e-06)
        RM[pl.ds(r0, 16), :] = jnp.broadcast_to(root, (16, 128))
        up_live = uin[pl.ds(r0, 16), :].astype(F32)
        up_live = up_live * jnp.where(slots[r // 4] >= 0, 1.0, 0.0)
        nsc[0] = xs / root * VC[0, 0:1, :]
        nsc[1] = up_live * VC[1, 0:1, :]
        rsc[0] = up_live
        rsc[1] = xs
        lane = lax.broadcasted_iota(jnp.int32, (16, 256), 1)
        for i in range(32):
            q = min(100 * i // 128, 23)
            sh = 100 * i - 128 * q
            win = slice(128 * q, 128 * q + 256)
            a = pltpu.roll(nsc[0, :, win], (256 - sh) % 256, 1)
            b = pltpu.roll(nsc[1, :, win], (100 - sh) % 256, 1)
            both = jnp.where(lane < FE, a, jnp.where(lane < 2 * FE, b, 0.0))
            C2[c, i, pl.ds(r0, 16), :] = both.astype(BF)
            a = pltpu.roll(rsc[0, :, win], (256 - sh) % 256, 1)
            b = pltpu.roll(rsc[1, :, win], (4 - sh) % 256, 1)
            XU[i, pl.ds(r0, 16), :] = a[:, :128].astype(BF)
            XP[i, pl.ds(r0, 16), :] = b[:, :128].astype(BF)
        return carry

    for q in range(25):
        VC[0, :, 128 * q : 128 * q + 128] = jnp.broadcast_to(gain[q : q + 1, :], (8, 128))
        VC[1, :, 128 * q : 128 * q + 128] = jnp.broadcast_to(lscale[q : q + 1, :], (8, 128))
    for i in range(32):
        q = min(100 * i // 128, 23)
        sh = 100 * i - 128 * q
        win = slice(128 * q, 128 * q + 256)
        GU[0, i] = pltpu.roll(VC[0, :, win], (256 - sh) % 256, 1)[:, :128]
        GU[1, i] = pltpu.roll(VC[1, :, win], (4 - sh) % 256, 1)[:, :128]
    lax.fori_loop(0, 8, act_step, 0)
    act_sib = rc(C2.at[c], C2.at[c], mi_s.at[1], mi_r.at[1], sib)
    act_sib.start()
    def weight(i):
        w = U[i]
        return jnp.concatenate([w[0:208], w[208:416], w[416:624], WT[i]], axis=1)

    def up(i):
        act = jnp.concatenate([C2[0, i], C2[1, i]], axis=0)
        CT[i] = act.T[:UR]
        a = act[:, :UR]
        first = lax.broadcasted_iota(jnp.int32, a.shape, 1) < FE
        zero = jnp.zeros_like(a)
        lhs = jnp.concatenate([jnp.where(first, a, zero), jnp.where(first, zero, a)], axis=0)
        WT[i] = unfold_tail(U[i, 3 * UR : PK]).astype(BF)
        hacc[...] += jnp.dot(lhs, weight(i), preferred_element_type=F32)

    def up_all(units):
        for u, da, db in units:
            up(uidx(u, da, db))

    for u in UU:
        ag.near0(u)
    for u in UU:
        ag.near1(u)
    rc(C2.at[c], C2.at[1 - c], mi_s.at[1], mi_r.at[1], sib).wait_recv()
    for u in UU:
        ag.bfwd(u, 0)
    own.wait()
    up_all([(0, 0, 0), (1, 0, 0)])
    for u in UU:
        ag.far(u)
    up_all([(u, da, 0) for u in UU for da in (3, 1)])

    def fwd_step(k, carry):
        for u in UU:
            ag.bfwd(u, k)
        for u in UU:
            ag.brest(u, k - 1)
        up_all([(u, da_of(k - 1), db) for u in UU for db in (3, 1)])
        return carry

    lax.fori_loop(1, 4, fwd_step, 0)
    up_all([(0, 2, 0), (1, 2, 0)])

    def last_step(k, carry):
        for u in UU:
            ag.blast(u, k)
        up_all([(u, da_of(k), 2) for u in UU])
        return carry

    lax.fori_loop(0, 3, last_step, 0)
    for u in UU:
        ag.brest(u, 3)
    up_all([(u, da_of(3), db) for u in UU for db in (3, 1)])
    last_step(3, 0)

    def gelu_step(r, carry):
        r0 = pl.multiple_of(r * 32, 32)
        h = hacc[pl.ds(r0, 32), :]
        gh = hacc[pl.ds(r0 + 256, 32), :]
        valid = lax.broadcasted_iota(jnp.int32, h.shape, 1) < HH
        cumul = 0.5 * (1.0 + lax.erf(h * 0.7071067811865476))
        density = jnp.exp(-0.5 * h * h) * 0.3989422804014327
        ho = jnp.where(valid, h * cumul, 0.0).astype(BF)
        gi = jnp.where(valid, gh * (cumul + h * density), 0.0).astype(BF)
        S[pl.ds(r0, 32), :] = gi
        S[pl.ds(r0 + 256, 32), :] = ho
        row = jnp.sum(gi.astype(F32) * jnp.where(valid, h, 0.0), axis=1, keepdims=True)
        cen[pl.ds(r0, 32), :] = jnp.broadcast_to(row, (32, 128))
        return carry

    lax.fori_loop(0, 8, gelu_step, 0)

    def down_all(units):
        lows = jnp.concatenate([CT[i, 0:112] for i in units], axis=0)
        highs = jnp.concatenate([CT[i, 96:208] for i in units], axis=0)
        lows = jnp.dot(lows, S[0:256], preferred_element_type=F32)
        highs = jnp.dot(highs, S[256:512], preferred_element_type=F32)
        row = lax.broadcasted_iota(jnp.int32, (16, 512), 0)
        res = []
        for n in range(len(units)):
            low, high = lows[112 * n : 112 * n + 112], highs[112 * n : 112 * n + 112]
            mid = jnp.where(row < 4, low[96:112], high[0:16])
            out = jnp.concatenate([low[0:96], mid, high[16:112]], axis=0)
            tail = fold_tail(out[:, 384:512])
            res.append([out[:, 0:128], out[:, 128:256], out[:, 256:384], tail])
        return res

    def down(i):
        return down_all([i])[0]

    ROWS4 = ((0, 208), (208, 416), (416, 624), (624, 656))

    def store_units(*units):
        for i, parts in zip(units, down_all(units)):
            for (lo, hi), part in zip(ROWS4, parts):
                PG[i, lo:hi] = part.astype(BF)

    def store_unit(i, *adds):
        for (lo, hi), part in zip(ROWS4, down(i)):
            for ref in adds:
                part = part + ref[lo:hi].astype(F32)
            PG[i, lo:hi] = part.astype(BF)

    def add_part(i, p, ref):
        lo, n = PARTS[p]
        PG[i, lo : lo + n] = (PG[i, lo : lo + n].astype(F32) + ref[lo : lo + n].astype(F32)).astype(BF)

    def rs(u, m, p, i, buf, d):
        return rc(
            PG.at[i, pl.ds(*PARTS[p])], buf.at[pl.ds(*PARTS[p])], rs_s.at[u, m, p], rs_r.at[u, m, p], d
        )

    def rs_wait(u, m, p, buf):
        rs(u, m, p, 0, buf, sib).wait_recv()

    def first_down(kk, carry):
        ks = (3 - 2 * kk, 2 - 2 * kk)
        store_units(*[uidx(u, da_of(k), 2) for k in ks for u in UU])
        for k in ks:
            for u in UU:
                i = uidx(u, da_of(k), 2)
                rs(u, 3 + 3 * k, 0, i, rb1.at[u, k], bp[u]).start()
                rs(u, 3 + 3 * k, 1, i, rb1.at[u, k], bm[u]).start()
        return carry

    def second_free(k):
        store_units(*[uidx(u, da_of(k), db) for db in (1, 3) for u in UU])
        for u in UU:
            rs(u, 4 + 3 * k, 1, uidx(u, da_of(k), 1), rb2.at[u, 0, k], bp[u]).start()
            rs(u, 5 + 3 * k, 0, uidx(u, da_of(k), 3), rb2.at[u, 1, k], bm[u]).start()

    def second_sum(k):
        for u in UU:
            i = uidx(u, da_of(k), 1)
            rs_wait(u, 3 + 3 * k, 0, rb1.at[u, k])
            add_part(i, 0, rb1.at[u, k])
            rs(u, 4 + 3 * k, 0, i, rb2.at[u, 0, k], bp[u]).start()
            i = uidx(u, da_of(k), 3)
            rs_wait(u, 3 + 3 * k, 1, rb1.at[u, k])
            add_part(i, 1, rb1.at[u, k])
            rs(u, 5 + 3 * k, 1, i, rb2.at[u, 1, k], bm[u]).start()

    def third(u, k):
        for w in (0, 1):
            for p in (1, 0) if w == 0 else (0, 1):
                rs_wait(u, 4 + 3 * k + w, p, rb2.at[u, w, k])
        i = uidx(u, da_of(k), 0)
        store_unit(i, rb2.at[u, 0, k], rb2.at[u, 1, k])
        return i

    def zblk(r):
        return lax.rem(z + r, 8)

    def mix(b):
        def rows(lo):
            tiles = []
            for j in range(4):
                w = [U[b * 4 + j, UR * t + lo : UR * t + lo + 112] for t in range(3)]
                tiles.append(jnp.concatenate(w + [WT[b * 4 + j, lo : lo + 112]], axis=1))
            return jnp.concatenate(tiles, axis=0)

        ms = jnp.dot(rows(96), ST[:, 256:512], preferred_element_type=F32)
        ns = jnp.dot(rows(0), ST[:, 0:256], preferred_element_type=F32).astype(BF)
        row = lax.broadcasted_iota(jnp.int32, (112, 256), 0)
        for j in range(4):
            m = ms[112 * j : 112 * j + 112]
            m = jnp.where(row == 104, cen_hi, jnp.where(row == 105, cen_lo, m)).astype(BF)
            n = ns[112 * j : 112 * j + 112]
            for e in (0, 1):
                M[e, 0, b * 4 + j] = m[:, 128 * e : 128 * e + 128]
                M[e, 1, b * 4 + j] = n[:, 128 * e : 128 * e + 128]

    def to_sibling(s, r):
        b = 4 * zblk(r)
        return rc(
            M.at[1 - c, :, pl.ds(b, 4)], MR.at[:, pl.ds(b, 4)], sq_s.at[s], sq_r.at[s], sib
        )

    zorder = (4, 3, 5, 2, 6, 1, 7, 0)

    def mix_step(s, carry):
        h = (s + 1) // 2
        r = 4 + h - 2 * h * lax.rem(s, 2)
        mix(zblk(r))
        to_sibling(s, r).start()
        return carry

    def zcopy(t, way, j, h):
        r = 4 + j if way == 0 else 4 - j
        buf = zrm if way == 0 else zrp
        return rc(
            M.at[c, t, pl.ds(4 * zblk(r) + 2 * h, 2)], buf.at[t, j, pl.ds(2 * h, 2)],
            zz_s.at[t, way, j, h], zz_r.at[t, way, j, h], zdev(7 if way == 0 else 1),
        )

    def combine(t, r, h, ref):
        b = zblk(r)
        for j in (2 * h, 2 * h + 1):
            i = b * 4 + j
            v = M[c, t, i].astype(F32) + MR[t, i].astype(F32)
            if ref is not None:
                v = v + ref[j].astype(F32)
            M[c, t, i] = v.astype(BF)

    def zfirst(t):
        if t == 0:
            to_sibling(0, 4).wait_recv()
        for way in (0, 1):
            combine(t, 4, way, None)
            zcopy(t, way, 0, way).start()

    def zstep(t, j):
        for n in (0, 1):
            for way in (0, 1):
                buf = zrm if way == 0 else zrp
                r = 4 + j if way == 0 else 4 - j
                if n == 0 and t == 0:
                    to_sibling(2 * j if way == 0 else 2 * j - 1, r).wait_recv()
                h = (1 - way if n == 0 else way) if j == 1 else n
                if j == 1 and n == 0:
                    combine(t, r, h, None)
                else:
                    zcopy(t, way, j - 1, h).wait_recv()
                    combine(t, r, h, buf.at[t, j - 1])
                zcopy(t, way, j, h).start()

    def zlast(t, j):
        i = z * 4 + j
        v = M[c, t, i].astype(F32) + MR[t, i].astype(F32)
        v = v + zrm[t, 3, j].astype(F32) + zrp[t, 3, j].astype(F32)
        return jnp.concatenate([v, jnp.zeros((16, 128), F32)], axis=0).T

    lax.fori_loop(0, 2, first_down, 0)
    second_free(3)
    ST[...] = S[...].T
    center = cen[...].T[0:1]
    cen_hi = center.astype(BF).astype(F32)
    cen_lo = center - cen_hi
    lax.fori_loop(0, 4, mix_step, 0)
    zfirst(0)
    second_free(2)
    second_sum(3)
    lax.fori_loop(4, 8, mix_step, 0)
    second_sum(2)
    zstep(0, 1)
    zfirst(1)
    second_free(1)
    second_sum(1)
    second_free(0)
    zstep(0, 2)
    second_sum(0)
    zstep(1, 1)

    for u in UU:
        i = third(u, 3)
        rs(u, 0, 0, i, ra1.at[u], ap[u]).start()
        rs(u, 0, 1, i, ra1.at[u], am[u]).start()
    zstep(0, 3)
    for u in UU:
        i = third(u, 2)
        rs(u, 2, 0, i, ra2.at[u, 1], am[u]).start()
    zstep(1, 2)
    for u in UU:
        i = third(u, 1)
        rs(u, 1, 1, i, ra2.at[u, 0], ap[u]).start()

    to_sibling(7, 0).wait_recv()
    for h in (0, 1):
        for way in (0, 1):
            zcopy(0, way, 3, h).wait_recv()
    ln = lax.broadcasted_iota(jnp.int32, (128, 128), 1)
    wide = [jnp.zeros((128, 128), F32) for _ in range(4)]
    centre = None
    for j in range(4):
        t = zlast(0, j)
        if j == 0:
            centre = (t[:, 104:105] + t[:, 105:106]) * (1.0 / 3200.0)
        i = z * 4 + j
        r = XP[i].astype(F32) + GU[1, i][0:1] * t
        at, sh = divmod(FE * j, 128)
        r = pltpu.roll(r, (sh + 124) % 128, 1)
        wide[at] = jnp.where((ln >= sh) & (ln < sh + FE), r, wide[at])
        if sh + FE > 128:
            wide[at + 1] = jnp.where(ln < sh + FE - 128, r, wide[at + 1])
    cen[0:128, :] = jnp.broadcast_to(centre, (128, 128))
    to, fr = (lax.broadcasted_iota(jnp.int32, (128, 128), d) for d in (0, 1))
    tr = lax.rem(to, 64)
    perm = fr == 64 * (to // 64) + 32 * (tr // 32) + 2 * lax.rem(tr, 16) + lax.rem(tr // 16, 2)
    wide = jnp.concatenate(wide, axis=1).astype(BF)
    wide = jnp.dot(perm.astype(BF), wide, preferred_element_type=F32)
    tail = jnp.where(ln < 16, wide[:, 384:512], 0.0)
    wide = [wide[:, 128 * t : 128 * t + 128].astype(BF) for t in range(3)]
    folded = tail[0:16]
    for g in range(1, 8):
        folded = folded + pltpu.roll(tail[16 * g : 16 * g + 16], 16 * g, 1)
    for t in range(3):
        V[c, me, 128 * t : 128 * t + 128, :] = wide[t]
    V[c, me, 384:400, :] = folded.astype(BF)

    VP = (((0, 112), (112, 96)), ((208, 96), (304, 96)))

    def vslot(u, p, da, db):
        return V.at[c, chip_of(u, da, db), pl.ds(*VP[u][p])]

    vg = Gather(vslot, vg_s, vg_r)

    def fwd(u, da, db):
        ch = chip_of(u, da, db)
        ref = V.at[c, ch, pl.ds(208 * u, 208 - 16 * u)]
        return rc(ref, ref, vf_s.at[u, ch], vf_r.at[u, ch], sib)

    for u in UU:
        vg.start_a(u)
    for u in UU:
        vg.start_b(u)
    for u in UU:
        fwd(u, 0, 0).start()

    zstep(1, 3)
    for u in UU:
        rs_wait(u, 0, 0, ra1.at[u])
        i = uidx(u, 1, 0)
        add_part(i, 0, ra1.at[u])
        rs(u, 1, 0, i, ra2.at[u, 0], ap[u]).start()
        rs_wait(u, 0, 1, ra1.at[u])
        i = uidx(u, 3, 0)
        add_part(i, 1, ra1.at[u])
        rs(u, 2, 1, i, ra2.at[u, 1], am[u]).start()

    def finish(u):
        for w in (0, 1):
            for p in (1, 0) if w == 0 else (0, 1):
                rs_wait(u, 4 + w, p, rb2.at[u, w, 0])
        i = uidx(u, 0, 0)
        parts = down(i)
        for w in (0, 1):
            for p in (1, 0) if w == 0 else (0, 1):
                rs_wait(u, 1 + w, p, ra2.at[u, w])
        out = []
        for (lo, hi), part in zip(ROWS4, parts):
            for ref in (rb2.at[u, 0, 0], rb2.at[u, 1, 0], ra2.at[u, 0], ra2.at[u, 1]):
                part = part + ref[lo:hi].astype(F32)
            out.append(part)
        return i, out

    for u in UU:
        vg.near0(u)
    for u in UU:
        vg.near1(u)
    for u in UU:
        fwd(u, 3, 0).start()
        fwd(u, 1, 0).start()
    for u in UU:
        vg.bfwd(u, 0)
    i, parts = finish(1)
    for (lo, hi), part in zip(ROWS4, parts):
        PG[i, lo:hi] = part.astype(BF)
    to_fin = rc(PG.at[i], fin, mi_s.at[2], mi_r.at[2], sib)
    to_fin.start()
    for u in UU:
        vg.far(u)
        fwd(u, 2, 0).start()
    _, parts = finish(0)
    for t in range(3):
        GS[:, 128 * t : 128 * t + 128] = parts[t]
    GS[:, 384:512] = unfold_tail(parts[3])
    for h in (0, 1):
        for way in (0, 1):
            zcopy(1, way, 3, h).wait_recv()
    root = RM[:, 0:1]
    centre = cen[0:128, 0:1]
    for j in range(4):
        i = z * 4 + j
        t = zlast(1, j)
        moved = pltpu.roll(XP[i].astype(F32), 124, 1)
        gp = XU[i].astype(F32) + (GU[0, i][0:1] * t - moved / root * centre) / root
        GP[FE * j : FE * j + FE, :] = gp.T[:FE]
    gp_v[...] = GP[...].astype(BF)

    table = U[:, 192:208, :].astype(F32)[:, 8, :]
    first_block = (dp * BLK).astype(F32)
    hit = (table >= first_block) & (table < first_block + BLK)
    hit = hit & (lax.broadcasted_iota(jnp.int32, table.shape, 1) < 2)
    least = jnp.min(jnp.where(hit, table, 1000.0))
    most = jnp.max(jnp.where(hit, table, -9.0))
    to, fr = (lax.broadcasted_iota(jnp.int32, (128, 256), d) for d in (0, 1))
    PM[...] = jnp.where(lax.rem(to, 64) == lax.rem(fr, 64), jnp.where(to < 64, least, most), -5.0)
    hacc[0:128] = jnp.zeros((128, 512), F32)

    def take(ch):
        for u in UU:
            ref = V.at[1 - c, ch, pl.ds(208 * u, 208 - 16 * u)]
            rc(ref, ref, vf_s.at[u, ch], vf_r.at[u, ch], sib).wait_recv()
        rows = []
        numbers = []
        ln = lax.broadcasted_iota(jnp.int32, (1, 128), 1)
        for e in (0, 1):
            tail = V[e, ch, 384:400].astype(F32)
            tail = [tail] + [pltpu.roll(tail, 128 - 16 * g, 1) for g in range(1, 8)]
            tail = jnp.concatenate(tail, axis=0).astype(BF)
            rows.append(
                jnp.concatenate([V[e, ch, 128 * t : 128 * t + 128] for t in range(3)] + [tail], axis=1)
            )
            pair = U[2 * ch + e, 192:208].astype(F32)[8:9]
            numbers.append(jnp.where(ln < 64, pair[:, 0:1], pair[:, 1:2]))
        place = (PM[...] == jnp.concatenate(numbers, axis=1)).astype(BF)
        hacc[0:128] += jnp.dot(place, jnp.concatenate(rows, axis=0), preferred_element_type=F32)

    def take4(kind):
        def body(n, carry):
            h, m = n // 2, lax.rem(n, 2)
            if kind == 0:
                dx, dy = (1 - m) * (n + 1), m * n
            elif kind == 1:
                dx, dy = 1 + 2 * m, 1 + 2 * h
            else:
                dx, dy = 2 * (1 - h) + h * (1 + 2 * m), (1 - h) * (1 + 2 * m) + 2 * h
            take(lax.rem(y + dy, 4) * 4 + lax.rem(x + dx, 4))
            return carry

        lax.fori_loop(0, 4, body, 0)

    def vstep(k, carry):
        for u in UU:
            vg.bfwd(u, k)
        for u in UU:
            vg.brest(u, k - 1)
            fwd(u, da_of(k - 1), 3).start()
            fwd(u, da_of(k - 1), 1).start()
        return carry

    lax.fori_loop(1, 4, vstep, 0)

    to_fin.wait_recv()
    mine = GS[...]
    other = [fin[208 * t : 208 * t + 208].astype(F32) for t in range(3)] + [unfold_tail(fin[624:656])]
    other = jnp.concatenate(other, axis=1)
    for h in (0, 1):
        half = jnp.where(c == h, mine, other)
        gin_v[:, HH * h : HH * h + HH] = half[0:FE, 0:HH]
        gout_v[:, HH * h : HH * h + HH] = half[FE : 2 * FE, 0:HH]
    outs = [
        pltpu.make_async_copy(a, b, loc.at[3 + n])
        for n, (a, b) in enumerate(((gin_v, gin_out), (gout_v, gout_out), (gp_v, gp_out)))
    ]
    for copy in outs:
        copy.start()

    ag.done()
    to_sib.wait_send()
    act_sib.wait_send()
    for n in range(8):
        to_sibling(n, zorder[n]).wait_send()
    for t in (0, 1):
        for way in (0, 1):
            zcopy(t, way, 0, way).wait_send()
            for n in (1, 2, 3):
                for h in (0, 1):
                    zcopy(t, way, n, h).wait_send()

    def rs_done(m, carry):
        for u in UU:
            for p in (0, 1):
                rs(u, m, p, 0, ra1.at[u], sib).wait_send()
        return carry

    lax.fori_loop(0, 15, rs_done, 0)
    to_fin.wait_send()

    for u in UU:
        vg.brest(u, 3)
        fwd(u, 2, 3).start()
        fwd(u, 2, 1).start()
    take(me)
    take4(0)
    take4(1)
    for k in range(4):
        for u in UU:
            vg.blast(u, k)
            fwd(u, da_of(k), 2).start()
        if k == 0:
            take(lax.rem(y, 4) * 4 + lax.rem(x + 2, 4))
            take(lax.rem(y + 2, 4) * 4 + x)
    take4(2)
    take(lax.rem(y + 2, 4) * 4 + lax.rem(x + 2, 4))
    low, high = hacc[0:64], hacc[64:128]
    for b in range(BLK):
        number = first_block + float(b)
        tile = jnp.where(least == number, low, jnp.where(most == number, high, 0.0)).astype(BF)
        for q in range(4):
            VT[q, 16 * b : 16 * b + 16, :] = tile[16 * q : 16 * q + 16]
    for q in range(4):
        vis[q] = VT[q].T[:HH]

    def vfwd_wait(ch, carry):
        for u in UU:
            ref = V.at[1 - c, ch, pl.ds(208 * u, 208 - 16 * u)]
            rc(ref, ref, vf_s.at[u, ch], vf_r.at[u, ch], sib).wait_send()
        return carry

    lax.fori_loop(0, 16, vfwd_wait, 0)

    vg.done()
    for copy in outs:
        copy.wait()
    last = pltpu.make_async_copy(vis, vis_out, loc.at[2])
    last.start()
    last.wait()


def mega(slots, w_in, w_out, gain, lscale, patches, upstream):
    dma = pltpu.SemaphoreType.DMA
    sm = pl.BlockSpec(memory_space=pltpu.SMEM)
    hbm = pl.BlockSpec(memory_space=pl.ANY)
    return pl.pallas_call(
        kernel,
        out_shape=(
            jax.ShapeDtypeStruct((FE, 2 * HH), F32),
            jax.ShapeDtypeStruct((FE, 2 * HH), F32),
            jax.ShapeDtypeStruct((HH, 128), BF),
            jax.ShapeDtypeStruct((4, HH, BLK * 16), BF),
        ),
        in_specs=[sm, hbm, hbm, hbm, hbm, hbm, hbm],
        out_specs=(hbm, hbm, hbm, hbm),
        scratch_shapes=[
            pltpu.VMEM((FE, 2 * HH), F32),
            pltpu.VMEM((FE, 2 * HH), F32),
            pltpu.VMEM((HH, 128), BF),
            pltpu.VMEM((4, HH, BLK * 16), BF),
            pltpu.VMEM((FE, 2 * HH), BF),
            pltpu.VMEM((FE, 2 * HH), BF),
            pltpu.VMEM((25, 128), F32),
            pltpu.VMEM((25, 128), F32),
            pltpu.VMEM((128, 3200), BF),
            pltpu.VMEM((128, 3200), BF),
            pltpu.VMEM((2, 16, 3200), F32),
            pltpu.VMEM((2, 16, 3200), F32),
            pltpu.VMEM((128, 128), F32),
            pltpu.VMEM((2, 8, 3200), F32),
            pltpu.VMEM((128, 256), F32),
            pltpu.VMEM((4, 128, 512), BF),
            pltpu.VMEM((UR, 896), F32),
            pltpu.VMEM((2, PK, 128), BF),
            pltpu.VMEM((2, 32, 8, 128), F32),
            pltpu.VMEM((32, PK, 128), BF),
            pltpu.VMEM((32, UR, 128), BF),
            pltpu.VMEM((2, 32, 128, 256), BF),
            pltpu.VMEM((32, 128, 128), BF),
            pltpu.VMEM((32, 128, 128), BF),
            pltpu.VMEM((32, UR, 256), BF),
            pltpu.VMEM((512, 512), F32),
            pltpu.VMEM((512, 512), BF),
            pltpu.VMEM((512, 512), BF),
            pltpu.VMEM((32, PK, 128), BF),
            pltpu.VMEM((2, 4, PK, 128), BF),
            pltpu.VMEM((2, 2, 4, PK, 128), BF),
            pltpu.VMEM((2, PK, 128), BF),
            pltpu.VMEM((2, 2, PK, 128), BF),
            pltpu.VMEM((PK, 128), BF),
            pltpu.VMEM((UR, 512), F32),
            pltpu.VMEM((2, 2, 32, 112, 128), BF),
            pltpu.VMEM((2, 32, 112, 128), BF),
            pltpu.VMEM((2, 4, 4, 112, 128), BF),
            pltpu.VMEM((2, 4, 4, 112, 128), BF),
            pltpu.VMEM((2, 16, 400, 128), BF),
            pltpu.VMEM((HH, 128), F32),
            pltpu.VMEM((256, 128), F32),
            dma((2, 15, 2)), dma((2, 15, 2)),
            dma((2, 15, 2)), dma((2, 15, 2)),
            dma((2, 15, 2)), dma((2, 15, 2)),
            dma((2, 16)), dma((2, 16)),
            dma((8,)), dma((8,)),
            dma((2, 2, 4, 2)), dma((2, 2, 4, 2)),
            dma((3,)), dma((3,)),
            dma((7,)),
        ],
        compiler_params=pltpu.CompilerParams(
            collective_id=0, has_side_effects=True, vmem_limit_bytes=60 * 2**20
        ),
    )(slots, w_in, w_out, gain, lscale, patches, upstream)


def shards(patches, upstream, norm_gain, layer_scale, w_in, w_out, slot_block):
    grad_w_in, grad_w_out, grad_patches, vision = mega(
        slot_block, w_in, w_out.T, norm_gain.reshape(25, 128), layer_scale.reshape(25, 128), patches, upstream
    )
    return (vision.transpose(2, 0, 1), grad_patches.T, grad_w_in, grad_w_out.T)


def solution(mesh):
    return jax.shard_map(
        shards,
        mesh=mesh,
        in_specs=(P("dp", None), P("dp", None), P(), P(), P("dp", "mp"), P("mp", "dp"), P("dp")),
        out_specs=(P("dp", None, "mp"), P("dp", "mp"), P("dp", "mp"), P("mp", "dp")),
        check_vma=False,
    )
```

```python
import jax
import jax.numpy as jnp
from jax import lax
from jax.experimental import pallas as pl
from jax.experimental.pallas import tpu as pltpu
from jax.sharding import PartitionSpec as P

BLK = 8
FE = 100
HH = 400
UR = 208
PK = 656
HA = 336
PARTS = ((0, HA), (HA, PK - HA))
MESH = pl.DeviceIdType.MESH
F32 = jnp.float32
BF = jnp.bfloat16


def fold_tail(tail):
    tail = jnp.concatenate([tail, jnp.zeros((16, 128), F32)], axis=0)
    out = tail[0:32]
    for g in range(1, 7):
        out = out + pltpu.roll(tail[32 * g : 32 * g + 32], 16 * g, 1)
    return out


def unfold_tail(packed):
    packed = packed.astype(F32)
    rows = [packed] + [pltpu.roll(packed, 128 - 16 * g, 1) for g in range(1, 7)]
    return jnp.concatenate(rows, axis=0)[:UR]


def kernel(
    slots, w_in_hbm, w_out_hbm, gain_hbm, lscale_hbm, patches, upstream, gin_out, gout_out, gp_out, vis_out,
    gin_v, gout_v, gp_v, vis, w_in, w_out, gain, lscale, xin, uin, nsc, rsc, RM, VC, PM, VT, WB, wu, GU, U, WT, C2, XU, XP, CT, hacc, S, ST, PG, rb1, rb2, ra1, ra2, fin, GS,
    M, MR, zrm, zrp, V, GP, cen,
    ag_s, ag_r, rs_s, rs_r, vg_s, vg_r, vf_s, vf_r, sq_s, sq_r, zz_s, zz_r, mi_s, mi_r, loc,
):
    dp = lax.axis_index("dp")
    z = lax.axis_index("mp")
    c = lax.rem(dp, 2)
    x = lax.rem(dp // 2, 4)
    y = dp // 8
    me = y * 4 + x
    UU = (0, 1)

    def chip_of(u, da, db):
        if u == 0:
            return lax.rem(y + db, 4) * 4 + lax.rem(x + da, 4)
        return lax.rem(y + da, 4) * 4 + lax.rem(x + db, 4)

    def dev(u, da, db):
        return (chip_of(u, da, db) * 2 + c, z)

    def zdev(dz):
        return (dp, lax.rem(z + dz, 8))

    sib = (me * 2 + 1 - c, z)
    ap = [dev(u, 1, 0) for u in UU]
    am = [dev(u, 3, 0) for u in UU]
    bp = [dev(u, 0, 1) for u in UU]
    bm = [dev(u, 0, 3) for u in UU]
    cross = [(chip_of(1, da, db) * 2 + 1 - c, z) for da, db in ((1, 0), (3, 0), (0, 1), (0, 3))]
    nbrs = [sib, ap[0], am[0], bp[0], bm[0], zdev(1), zdev(7)] + cross

    def rc(src, dst, ss, rs, d):
        return pltpu.make_async_remote_copy(
            src_ref=src, dst_ref=dst, send_sem=ss, recv_sem=rs, device_id=d, device_id_type=MESH
        )

    def uidx(u, da, db):
        return chip_of(u, da, db) * 2 + (c if u == 0 else 1 - c)

    def da_of(k):
        return k + k // 2 - 2 * (k // 3)

    get_p = pltpu.make_async_copy(patches, xin, loc.at[1])
    get_u = pltpu.make_async_copy(upstream, uin, loc.at[2])
    small = [
        pltpu.make_async_copy(a, b, loc.at[3 + n])
        for n, (a, b) in enumerate(
            ((w_in_hbm, w_in), (w_out_hbm, w_out), (gain_hbm, gain), (lscale_hbm, lscale))
        )
    ]
    for copy in small:
        copy.start()
    get_p.start()
    get_u.start()
    barrier = pltpu.get_barrier_semaphore()
    for d in nbrs:
        pl.semaphore_signal(barrier, inc=1, device_id=d, device_id_type=MESH)

    for copy in small:
        copy.wait()
    WB[0:FE, 0:800] = w_in[...].astype(F32)
    WB[FE : 2 * FE, 0:800] = w_out[...].astype(F32)
    at = lax.broadcasted_iota(jnp.int32, (8, 800), 1)
    at = jnp.where(at < HH, at, at - HH)
    slot0 = slots[0].astype(F32)
    slot1 = slots[1].astype(F32)
    WB[2 * FE : UR, 0:800] = jnp.where(at == 0, slot0, jnp.where(at == 1, slot1, 0.0))
    for h in (0, 1):
        part = WB[:, 0:512] if h == 0 else pltpu.roll(WB[:, 384:896], 496, 1)
        for t in range(3):
            wu[h, UR * t : UR * t + UR] = part[:, 128 * t : 128 * t + 128].astype(BF)
        tail = part[:, 384:512]
        tail = jnp.where(lax.broadcasted_iota(jnp.int32, tail.shape, 1) < 16, tail, 0.0)
        wu[h, 3 * UR : PK] = fold_tail(tail).astype(BF)
    pl.semaphore_wait(barrier, len(nbrs))

    class Gather:
        def __init__(self, slot, ss, rs):
            self.slot, self.ss, self.rs = slot, ss, rs

        def copy(self, u, m, p, da, db, d, src=None):
            ref = self.slot(u, p, da, db)
            src = ref if src is None else src.at[c, pl.ds(*PARTS[p])]
            return rc(src, ref, self.ss.at[u, m, p], self.rs.at[u, m, p], d)

        def send(self, u, m, p, da, db, d, src=None):
            self.copy(u, m, p, da, db, d, src).start()

        def wait(self, u, m, p, da, db):
            self.copy(u, m, p, da, db, sib).wait_recv()

        def bsend(self, u, k, p):
            da = da_of(k)
            self.send(u, 3 + 3 * k, p, da, 0, bp[u])
            self.send(u, 4 + 3 * k, p, da, 0, bm[u])

        def start_a(self, u, src=None):
            self.send(u, 0, 0, 0, 0, ap[u], src)
            self.send(u, 1, 1, 0, 0, am[u], src)
            self.send(u, 0, 1, 0, 0, ap[u], src)
            self.send(u, 1, 0, 0, 0, am[u], src)

        def start_b(self, u, src=None):
            self.send(u, 3, 0, 0, 0, bp[u], src)
            self.send(u, 4, 1, 0, 0, bm[u], src)
            self.send(u, 3, 1, 0, 0, bp[u], src)
            self.send(u, 4, 0, 0, 0, bm[u], src)

        def near0(self, u):
            self.wait(u, 0, 0, 3, 0)
            self.send(u, 2, 0, 3, 0, ap[u])
            self.wait(u, 1, 1, 1, 0)
            self.send(u, 2, 1, 1, 0, am[u])
            self.bsend(u, 2, 0)
            self.bsend(u, 1, 1)

        def near1(self, u):
            self.wait(u, 0, 1, 3, 0)
            self.bsend(u, 2, 1)
            self.wait(u, 1, 0, 1, 0)
            self.bsend(u, 1, 0)

        def far(self, u):
            self.wait(u, 2, 0, 2, 0)
            self.bsend(u, 3, 0)
            self.wait(u, 2, 1, 2, 0)
            self.bsend(u, 3, 1)

        def bfwd(self, u, k):
            da = da_of(k)
            self.wait(u, 3 + 3 * k, 0, da, 3)
            self.send(u, 5 + 3 * k, 0, da, 3, bp[u])
            self.wait(u, 4 + 3 * k, 1, da, 1)
            self.send(u, 5 + 3 * k, 1, da, 1, bm[u])

        def brest(self, u, k):
            da = da_of(k)
            self.wait(u, 3 + 3 * k, 1, da, 3)
            self.wait(u, 4 + 3 * k, 0, da, 1)

        def blast(self, u, k):
            da = da_of(k)
            self.wait(u, 5 + 3 * k, 0, da, 2)
            self.wait(u, 5 + 3 * k, 1, da, 2)

        def done(self):
            def body(m, carry):
                for u in UU:
                    for p in (0, 1):
                        self.copy(u, m, p, 0, 0, sib).wait_send()
                return carry

            lax.fori_loop(0, 15, body, 0)

    def wslot(u, p, da, db):
        return U.at[uidx(u, da, db), pl.ds(*PARTS[p])]

    ag = Gather(wslot, ag_s, ag_r)

    to_sib = rc(wu.at[1 - c], U.at[me * 2 + c], mi_s.at[0], mi_r.at[0], sib)
    to_sib.start()
    own = pltpu.make_async_copy(wu.at[c], U.at[me * 2 + c], loc.at[0])
    own.start()
    ag.start_a(0, wu)
    ag.start_b(0, wu)
    for m, p, n in ((0, 0, 0), (1, 1, 1), (0, 1, 0), (1, 0, 1), (3, 0, 2), (4, 1, 3), (3, 1, 2), (4, 0, 3)):
        part = pl.ds(*PARTS[p])
        rc(
            wu.at[1 - c, part], U.at[me * 2 + c, part], ag_s.at[1, m, p], ag_r.at[1, m, p], cross[n]
        ).start()

    hacc[...] = jnp.zeros_like(hacc)
    get_p.wait()
    get_u.wait()

    def act_step(r, carry):
        r0 = pl.multiple_of(r * 16, 16)
        xs = xin[pl.ds(r0, 16), :].astype(F32)
        root = jnp.sqrt(jnp.sum(xs * xs, axis=1, keepdims=True) * (1.0 / 3200.0) + 1e-06)
        RM[pl.ds(r0, 16), :] = jnp.broadcast_to(root, (16, 128))
        up_live = uin[pl.ds(r0, 16), :].astype(F32)
        up_live = up_live * jnp.where(slots[r // 4] >= 0, 1.0, 0.0)
        nsc[0] = xs / root * VC[0, 0:1, :]
        nsc[1] = up_live * VC[1, 0:1, :]
        rsc[0] = up_live
        rsc[1] = xs
        lane = lax.broadcasted_iota(jnp.int32, (16, 256), 1)
        for i in range(32):
            q = min(100 * i // 128, 23)
            sh = 100 * i - 128 * q
            win = slice(128 * q, 128 * q + 256)
            a = pltpu.roll(nsc[0, :, win], (256 - sh) % 256, 1)
            b = pltpu.roll(nsc[1, :, win], (100 - sh) % 256, 1)
            both = jnp.where(lane < FE, a, jnp.where(lane < 2 * FE, b, 0.0))
            C2[c, i, pl.ds(r0, 16), :] = both.astype(BF)
            a = pltpu.roll(rsc[0, :, win], (256 - sh) % 256, 1)
            b = pltpu.roll(rsc[1, :, win], (4 - sh) % 256, 1)
            XU[i, pl.ds(r0, 16), :] = a[:, :128].astype(BF)
            XP[i, pl.ds(r0, 16), :] = b[:, :128].astype(BF)
        return carry

    for q in range(25):
        VC[0, :, 128 * q : 128 * q + 128] = jnp.broadcast_to(gain[q : q + 1, :], (8, 128))
        VC[1, :, 128 * q : 128 * q + 128] = jnp.broadcast_to(lscale[q : q + 1, :], (8, 128))
    for i in range(32):
        q = min(100 * i // 128, 23)
        sh = 100 * i - 128 * q
        win = slice(128 * q, 128 * q + 256)
        GU[0, i] = pltpu.roll(VC[0, :, win], (256 - sh) % 256, 1)[:, :128]
        GU[1, i] = pltpu.roll(VC[1, :, win], (4 - sh) % 256, 1)[:, :128]
    lax.fori_loop(0, 8, act_step, 0)
    act_sib = rc(C2.at[c], C2.at[c], mi_s.at[1], mi_r.at[1], sib)
    act_sib.start()
    def weight(i):
        w = U[i]
        return jnp.concatenate([w[0:208], w[208:416], w[416:624], WT[i]], axis=1)

    def up(i):
        act = jnp.concatenate([C2[0, i], C2[1, i]], axis=0)
        CT[i] = act.T[:UR]
        a = act[:, :UR]
        first = lax.broadcasted_iota(jnp.int32, a.shape, 1) < FE
        zero = jnp.zeros_like(a)
        lhs = jnp.concatenate([jnp.where(first, a, zero), jnp.where(first, zero, a)], axis=0)
        WT[i] = unfold_tail(U[i, 3 * UR : PK]).astype(BF)
        hacc[...] += jnp.dot(lhs, weight(i), preferred_element_type=F32)

    def up_all(units):
        for u, da, db in units:
            up(uidx(u, da, db))

    for u in UU:
        ag.near0(u)
    for u in UU:
        ag.near1(u)
    rc(C2.at[c], C2.at[1 - c], mi_s.at[1], mi_r.at[1], sib).wait_recv()
    for u in UU:
        ag.bfwd(u, 0)
    own.wait()
    rc(wu.at[0], U.at[me * 2 + 1 - c], mi_s.at[0], mi_r.at[0], sib).wait_recv()
    up_all([(0, 0, 0), (1, 0, 0)])
    for u in UU:
        ag.far(u)
    up_all([(u, da, 0) for u in UU for da in (3, 1)])

    def fwd_step(k, carry):
        for u in UU:
            ag.bfwd(u, k)
        for u in UU:
            ag.brest(u, k - 1)
        up_all([(u, da_of(k - 1), db) for u in UU for db in (3, 1)])
        return carry

    lax.fori_loop(1, 4, fwd_step, 0)
    up_all([(0, 2, 0), (1, 2, 0)])

    def last_step(k, carry):
        for u in UU:
            ag.blast(u, k)
        up_all([(u, da_of(k), 2) for u in UU])
        return carry

    lax.fori_loop(0, 3, last_step, 0)
    for u in UU:
        ag.brest(u, 3)
    up_all([(u, da_of(3), db) for u in UU for db in (3, 1)])
    last_step(3, 0)

    def gelu_step(r, carry):
        r0 = pl.multiple_of(r * 32, 32)
        h = hacc[pl.ds(r0, 32), :]
        gh = hacc[pl.ds(r0 + 256, 32), :]
        valid = lax.broadcasted_iota(jnp.int32, h.shape, 1) < HH
        cumul = 0.5 * (1.0 + lax.erf(h * 0.7071067811865476))
        density = jnp.exp(-0.5 * h * h) * 0.3989422804014327
        ho = jnp.where(valid, h * cumul, 0.0).astype(BF)
        gi = jnp.where(valid, gh * (cumul + h * density), 0.0).astype(BF)
        S[pl.ds(r0, 32), :] = gi
        S[pl.ds(r0 + 256, 32), :] = ho
        row = jnp.sum(gi.astype(F32) * jnp.where(valid, h, 0.0), axis=1, keepdims=True)
        cen[pl.ds(r0, 32), :] = jnp.broadcast_to(row, (32, 128))
        return carry

    lax.fori_loop(0, 8, gelu_step, 0)

    def down_all(units):
        lows = jnp.concatenate([CT[i, 0:112] for i in units], axis=0)
        highs = jnp.concatenate([CT[i, 96:208] for i in units], axis=0)
        lows = jnp.dot(lows, S[0:256], preferred_element_type=F32)
        highs = jnp.dot(highs, S[256:512], preferred_element_type=F32)
        row = lax.broadcasted_iota(jnp.int32, (16, 512), 0)
        res = []
        for n in range(len(units)):
            low, high = lows[112 * n : 112 * n + 112], highs[112 * n : 112 * n + 112]
            mid = jnp.where(row < 4, low[96:112], high[0:16])
            out = jnp.concatenate([low[0:96], mid, high[16:112]], axis=0)
            tail = fold_tail(out[:, 384:512])
            res.append([out[:, 0:128], out[:, 128:256], out[:, 256:384], tail])
        return res

    def down(i):
        return down_all([i])[0]

    ROWS4 = ((0, 208), (208, 416), (416, 624), (624, 656))

    def store_units(*units):
        for i, parts in zip(units, down_all(units)):
            for (lo, hi), part in zip(ROWS4, parts):
                PG[i, lo:hi] = part.astype(BF)

    def store_unit(i, *adds):
        for (lo, hi), part in zip(ROWS4, down(i)):
            for ref in adds:
                part = part + ref[lo:hi].astype(F32)
            PG[i, lo:hi] = part.astype(BF)

    def add_part(i, p, ref):
        lo, n = PARTS[p]
        PG[i, lo : lo + n] = (PG[i, lo : lo + n].astype(F32) + ref[lo : lo + n].astype(F32)).astype(BF)

    def rs(u, m, p, i, buf, d):
        return rc(
            PG.at[i, pl.ds(*PARTS[p])], buf.at[pl.ds(*PARTS[p])], rs_s.at[u, m, p], rs_r.at[u, m, p], d
        )

    def rs_wait(u, m, p, buf):
        rs(u, m, p, 0, buf, sib).wait_recv()

    def first_down(kk, carry):
        ks = (3 - 2 * kk, 2 - 2 * kk)
        store_units(*[uidx(u, da_of(k), 2) for k in ks for u in UU])
        for k in ks:
            for u in UU:
                i = uidx(u, da_of(k), 2)
                rs(u, 3 + 3 * k, 0, i, rb1.at[u, k], bp[u]).start()
                rs(u, 3 + 3 * k, 1, i, rb1.at[u, k], bm[u]).start()
        return carry

    def second_free(k):
        store_units(*[uidx(u, da_of(k), db) for db in (1, 3) for u in UU])
        for u in UU:
            rs(u, 4 + 3 * k, 1, uidx(u, da_of(k), 1), rb2.at[u, 0, k], bp[u]).start()
            rs(u, 5 + 3 * k, 0, uidx(u, da_of(k), 3), rb2.at[u, 1, k], bm[u]).start()

    def second_sum(k):
        for u in UU:
            i = uidx(u, da_of(k), 1)
            rs_wait(u, 3 + 3 * k, 0, rb1.at[u, k])
            add_part(i, 0, rb1.at[u, k])
            rs(u, 4 + 3 * k, 0, i, rb2.at[u, 0, k], bp[u]).start()
            i = uidx(u, da_of(k), 3)
            rs_wait(u, 3 + 3 * k, 1, rb1.at[u, k])
            add_part(i, 1, rb1.at[u, k])
            rs(u, 5 + 3 * k, 1, i, rb2.at[u, 1, k], bm[u]).start()

    def third(u, k):
        for w in (0, 1):
            for p in (1, 0) if w == 0 else (0, 1):
                rs_wait(u, 4 + 3 * k + w, p, rb2.at[u, w, k])
        i = uidx(u, da_of(k), 0)
        store_unit(i, rb2.at[u, 0, k], rb2.at[u, 1, k])
        return i

    def zblk(r):
        return lax.rem(z + r, 8)

    def mix(b):
        def rows(lo):
            tiles = []
            for j in range(4):
                w = [U[b * 4 + j, UR * t + lo : UR * t + lo + 112] for t in range(3)]
                tiles.append(jnp.concatenate(w + [WT[b * 4 + j, lo : lo + 112]], axis=1))
            return jnp.concatenate(tiles, axis=0)

        ms = jnp.dot(rows(96), ST[:, 256:512], preferred_element_type=F32)
        ns = jnp.dot(rows(0), ST[:, 0:256], preferred_element_type=F32).astype(BF)
        row = lax.broadcasted_iota(jnp.int32, (112, 256), 0)
        for j in range(4):
            m = ms[112 * j : 112 * j + 112]
            m = jnp.where(row == 104, cen_hi, jnp.where(row == 105, cen_lo, m)).astype(BF)
            n = ns[112 * j : 112 * j + 112]
            for e in (0, 1):
                M[e, 0, b * 4 + j] = m[:, 128 * e : 128 * e + 128]
                M[e, 1, b * 4 + j] = n[:, 128 * e : 128 * e + 128]

    def to_sibling(s, r):
        b = 4 * zblk(r)
        return rc(
            M.at[1 - c, :, pl.ds(b, 4)], MR.at[:, pl.ds(b, 4)], sq_s.at[s], sq_r.at[s], sib
        )

    zorder = (4, 3, 5, 2, 6, 1, 7, 0)

    def mix_step(s, carry):
        h = (s + 1) // 2
        r = 4 + h - 2 * h * lax.rem(s, 2)
        mix(zblk(r))
        to_sibling(s, r).start()
        return carry

    def zcopy(t, way, j, h):
        r = 4 + j if way == 0 else 4 - j
        buf = zrm if way == 0 else zrp
        return rc(
            M.at[c, t, pl.ds(4 * zblk(r) + 2 * h, 2)], buf.at[t, j, pl.ds(2 * h, 2)],
            zz_s.at[t, way, j, h], zz_r.at[t, way, j, h], zdev(7 if way == 0 else 1),
        )

    def combine(t, r, h, ref):
        b = zblk(r)
        for j in (2 * h, 2 * h + 1):
            i = b * 4 + j
            v = M[c, t, i].astype(F32) + MR[t, i].astype(F32)
            if ref is not None:
                v = v + ref[j].astype(F32)
            M[c, t, i] = v.astype(BF)

    def zfirst(t):
        if t == 0:
            to_sibling(0, 4).wait_recv()
        for way in (0, 1):
            combine(t, 4, way, None)
            zcopy(t, way, 0, way).start()

    def zstep(t, j):
        for n in (0, 1):
            for way in (0, 1):
                buf = zrm if way == 0 else zrp
                r = 4 + j if way == 0 else 4 - j
                if n == 0 and t == 0:
                    to_sibling(2 * j if way == 0 else 2 * j - 1, r).wait_recv()
                h = (1 - way if n == 0 else way) if j == 1 else n
                if j == 1 and n == 0:
                    combine(t, r, h, None)
                else:
                    zcopy(t, way, j - 1, h).wait_recv()
                    combine(t, r, h, buf.at[t, j - 1])
                zcopy(t, way, j, h).start()

    def zlast(t, j):
        i = z * 4 + j
        v = M[c, t, i].astype(F32) + MR[t, i].astype(F32)
        v = v + zrm[t, 3, j].astype(F32) + zrp[t, 3, j].astype(F32)
        return jnp.concatenate([v, jnp.zeros((16, 128), F32)], axis=0).T

    lax.fori_loop(0, 2, first_down, 0)
    second_free(3)
    ST[...] = S[...].T
    center = cen[...].T[0:1]
    cen_hi = center.astype(BF).astype(F32)
    cen_lo = center - cen_hi
    lax.fori_loop(0, 4, mix_step, 0)
    zfirst(0)
    second_free(2)
    second_sum(3)
    lax.fori_loop(4, 8, mix_step, 0)
    second_sum(2)
    zstep(0, 1)
    zfirst(1)
    second_free(1)
    second_sum(1)
    second_free(0)
    zstep(0, 2)
    second_sum(0)
    zstep(1, 1)

    for u in UU:
        i = third(u, 3)
        rs(u, 0, 0, i, ra1.at[u], ap[u]).start()
        rs(u, 0, 1, i, ra1.at[u], am[u]).start()
    zstep(0, 3)
    for u in UU:
        i = third(u, 2)
        rs(u, 2, 0, i, ra2.at[u, 1], am[u]).start()
    zstep(1, 2)
    for u in UU:
        i = third(u, 1)
        rs(u, 1, 1, i, ra2.at[u, 0], ap[u]).start()

    to_sibling(7, 0).wait_recv()
    for h in (0, 1):
        for way in (0, 1):
            zcopy(0, way, 3, h).wait_recv()
    ln = lax.broadcasted_iota(jnp.int32, (128, 128), 1)
    wide = [jnp.zeros((128, 128), F32) for _ in range(4)]
    centre = None
    for j in range(4):
        t = zlast(0, j)
        if j == 0:
            centre = (t[:, 104:105] + t[:, 105:106]) * (1.0 / 3200.0)
        i = z * 4 + j
        r = XP[i].astype(F32) + GU[1, i][0:1] * t
        at, sh = divmod(FE * j, 128)
        r = pltpu.roll(r, (sh + 124) % 128, 1)
        wide[at] = jnp.where((ln >= sh) & (ln < sh + FE), r, wide[at])
        if sh + FE > 128:
            wide[at + 1] = jnp.where(ln < sh + FE - 128, r, wide[at + 1])
    cen[0:128, :] = jnp.broadcast_to(centre, (128, 128))
    to, fr = (lax.broadcasted_iota(jnp.int32, (128, 128), d) for d in (0, 1))
    tr = lax.rem(to, 64)
    perm = fr == 64 * (to // 64) + 32 * (tr // 32) + 2 * lax.rem(tr, 16) + lax.rem(tr // 16, 2)
    wide = jnp.concatenate(wide, axis=1).astype(BF)
    wide = jnp.dot(perm.astype(BF), wide, preferred_element_type=F32)
    tail = jnp.where(ln < 16, wide[:, 384:512], 0.0)
    wide = [wide[:, 128 * t : 128 * t + 128].astype(BF) for t in range(3)]
    folded = tail[0:16]
    for g in range(1, 8):
        folded = folded + pltpu.roll(tail[16 * g : 16 * g + 16], 16 * g, 1)
    for t in range(3):
        V[c, me, 128 * t : 128 * t + 128, :] = wide[t]
    V[c, me, 384:400, :] = folded.astype(BF)

    VP = (((0, 112), (112, 96)), ((208, 96), (304, 96)))

    def vslot(u, p, da, db):
        return V.at[c, chip_of(u, da, db), pl.ds(*VP[u][p])]

    vg = Gather(vslot, vg_s, vg_r)

    def fwd(u, da, db):
        ch = chip_of(u, da, db)
        ref = V.at[c, ch, pl.ds(208 * u, 208 - 16 * u)]
        return rc(ref, ref, vf_s.at[u, ch], vf_r.at[u, ch], sib)

    for u in UU:
        vg.start_a(u)
    for u in UU:
        vg.start_b(u)
    for u in UU:
        fwd(u, 0, 0).start()

    zstep(1, 3)
    for u in UU:
        rs_wait(u, 0, 0, ra1.at[u])
        i = uidx(u, 1, 0)
        add_part(i, 0, ra1.at[u])
        rs(u, 1, 0, i, ra2.at[u, 0], ap[u]).start()
        rs_wait(u, 0, 1, ra1.at[u])
        i = uidx(u, 3, 0)
        add_part(i, 1, ra1.at[u])
        rs(u, 2, 1, i, ra2.at[u, 1], am[u]).start()

    def finish(u):
        for w in (0, 1):
            for p in (1, 0) if w == 0 else (0, 1):
                rs_wait(u, 4 + w, p, rb2.at[u, w, 0])
        i = uidx(u, 0, 0)
        parts = down(i)
        for w in (0, 1):
            for p in (1, 0) if w == 0 else (0, 1):
                rs_wait(u, 1 + w, p, ra2.at[u, w])
        out = []
        for (lo, hi), part in zip(ROWS4, parts):
            for ref in (rb2.at[u, 0, 0], rb2.at[u, 1, 0], ra2.at[u, 0], ra2.at[u, 1]):
                part = part + ref[lo:hi].astype(F32)
            out.append(part)
        return i, out

    for u in UU:
        vg.near0(u)
    for u in UU:
        vg.near1(u)
    for u in UU:
        fwd(u, 3, 0).start()
        fwd(u, 1, 0).start()
    for u in UU:
        vg.bfwd(u, 0)
    i, parts = finish(1)
    for (lo, hi), part in zip(ROWS4, parts):
        PG[i, lo:hi] = part.astype(BF)
    to_fin = rc(PG.at[i], fin, mi_s.at[2], mi_r.at[2], sib)
    to_fin.start()
    for u in UU:
        vg.far(u)
        fwd(u, 2, 0).start()
    _, parts = finish(0)
    for t in range(3):
        GS[:, 128 * t : 128 * t + 128] = parts[t]
    GS[:, 384:512] = unfold_tail(parts[3])
    for h in (0, 1):
        for way in (0, 1):
            zcopy(1, way, 3, h).wait_recv()
    root = RM[:, 0:1]
    centre = cen[0:128, 0:1]
    for j in range(4):
        i = z * 4 + j
        t = zlast(1, j)
        moved = pltpu.roll(XP[i].astype(F32), 124, 1)
        gp = XU[i].astype(F32) + (GU[0, i][0:1] * t - moved / root * centre) / root
        GP[FE * j : FE * j + FE, :] = gp.T[:FE]
    gp_v[...] = GP[...].astype(BF)

    table = U[:, 192:208, :].astype(F32)[:, 8, :]
    first_block = (dp * BLK).astype(F32)
    hit = (table >= first_block) & (table < first_block + BLK)
    hit = hit & (lax.broadcasted_iota(jnp.int32, table.shape, 1) < 2)
    least = jnp.min(jnp.where(hit, table, 1000.0))
    most = jnp.max(jnp.where(hit, table, -9.0))
    to, fr = (lax.broadcasted_iota(jnp.int32, (128, 256), d) for d in (0, 1))
    PM[...] = jnp.where(lax.rem(to, 64) == lax.rem(fr, 64), jnp.where(to < 64, least, most), -5.0)
    hacc[0:128] = jnp.zeros((128, 512), F32)

    def take(ch):
        for u in UU:
            ref = V.at[1 - c, ch, pl.ds(208 * u, 208 - 16 * u)]
            rc(ref, ref, vf_s.at[u, ch], vf_r.at[u, ch], sib).wait_recv()
        rows = []
        numbers = []
        ln = lax.broadcasted_iota(jnp.int32, (1, 128), 1)
        for e in (0, 1):
            tail = V[e, ch, 384:400].astype(F32)
            tail = [tail] + [pltpu.roll(tail, 128 - 16 * g, 1) for g in range(1, 8)]
            tail = jnp.concatenate(tail, axis=0).astype(BF)
            rows.append(
                jnp.concatenate([V[e, ch, 128 * t : 128 * t + 128] for t in range(3)] + [tail], axis=1)
            )
            pair = U[2 * ch + e, 192:208].astype(F32)[8:9]
            numbers.append(jnp.where(ln < 64, pair[:, 0:1], pair[:, 1:2]))
        place = (PM[...] == jnp.concatenate(numbers, axis=1)).astype(BF)
        hacc[0:128] += jnp.dot(place, jnp.concatenate(rows, axis=0), preferred_element_type=F32)

    def take4(kind):
        def body(n, carry):
            h, m = n // 2, lax.rem(n, 2)
            if kind == 0:
                dx, dy = (1 - m) * (n + 1), m * n
            elif kind == 1:
                dx, dy = 1 + 2 * m, 1 + 2 * h
            else:
                dx, dy = 2 * (1 - h) + h * (1 + 2 * m), (1 - h) * (1 + 2 * m) + 2 * h
            take(lax.rem(y + dy, 4) * 4 + lax.rem(x + dx, 4))
            return carry

        lax.fori_loop(0, 4, body, 0)

    def vstep(k, carry):
        for u in UU:
            vg.bfwd(u, k)
        for u in UU:
            vg.brest(u, k - 1)
            fwd(u, da_of(k - 1), 3).start()
            fwd(u, da_of(k - 1), 1).start()
        return carry

    lax.fori_loop(1, 4, vstep, 0)

    to_fin.wait_recv()
    mine = GS[...]
    other = [fin[208 * t : 208 * t + 208].astype(F32) for t in range(3)] + [unfold_tail(fin[624:656])]
    other = jnp.concatenate(other, axis=1)
    for h in (0, 1):
        half = jnp.where(c == h, mine, other)
        gin_v[:, HH * h : HH * h + HH] = half[0:FE, 0:HH]
        gout_v[:, HH * h : HH * h + HH] = half[FE : 2 * FE, 0:HH]
    outs = [
        pltpu.make_async_copy(a, b, loc.at[3 + n])
        for n, (a, b) in enumerate(((gin_v, gin_out), (gout_v, gout_out), (gp_v, gp_out)))
    ]
    for copy in outs:
        copy.start()

    ag.done()
    to_sib.wait_send()
    act_sib.wait_send()
    for n in range(8):
        to_sibling(n, zorder[n]).wait_send()
    for t in (0, 1):
        for way in (0, 1):
            zcopy(t, way, 0, way).wait_send()
            for n in (1, 2, 3):
                for h in (0, 1):
                    zcopy(t, way, n, h).wait_send()

    def rs_done(m, carry):
        for u in UU:
            for p in (0, 1):
                rs(u, m, p, 0, ra1.at[u], sib).wait_send()
        return carry

    lax.fori_loop(0, 15, rs_done, 0)
    to_fin.wait_send()

    for u in UU:
        vg.brest(u, 3)
        fwd(u, 2, 3).start()
        fwd(u, 2, 1).start()
    take(me)
    take4(0)
    take4(1)
    for k in range(4):
        for u in UU:
            vg.blast(u, k)
            fwd(u, da_of(k), 2).start()
        if k == 0:
            take(lax.rem(y, 4) * 4 + lax.rem(x + 2, 4))
            take(lax.rem(y + 2, 4) * 4 + x)
    take4(2)
    take(lax.rem(y + 2, 4) * 4 + lax.rem(x + 2, 4))
    low, high = hacc[0:64], hacc[64:128]
    for b in range(BLK):
        number = first_block + float(b)
        tile = jnp.where(least == number, low, jnp.where(most == number, high, 0.0)).astype(BF)
        for q in range(4):
            VT[q, 16 * b : 16 * b + 16, :] = tile[16 * q : 16 * q + 16]
    for q in range(4):
        vis[q] = VT[q].T[:HH]

    def vfwd_wait(ch, carry):
        for u in UU:
            ref = V.at[1 - c, ch, pl.ds(208 * u, 208 - 16 * u)]
            rc(ref, ref, vf_s.at[u, ch], vf_r.at[u, ch], sib).wait_send()
        return carry

    lax.fori_loop(0, 16, vfwd_wait, 0)

    vg.done()
    for copy in outs:
        copy.wait()
    last = pltpu.make_async_copy(vis, vis_out, loc.at[2])
    last.start()
    last.wait()


def mega(slots, w_in, w_out, gain, lscale, patches, upstream):
    dma = pltpu.SemaphoreType.DMA
    sm = pl.BlockSpec(memory_space=pltpu.SMEM)
    hbm = pl.BlockSpec(memory_space=pl.ANY)
    return pl.pallas_call(
        kernel,
        out_shape=(
            jax.ShapeDtypeStruct((FE, 2 * HH), F32),
            jax.ShapeDtypeStruct((FE, 2 * HH), F32),
            jax.ShapeDtypeStruct((HH, 128), BF),
            jax.ShapeDtypeStruct((4, HH, BLK * 16), BF),
        ),
        in_specs=[sm, hbm, hbm, hbm, hbm, hbm, hbm],
        out_specs=(hbm, hbm, hbm, hbm),
        scratch_shapes=[
            pltpu.VMEM((FE, 2 * HH), F32),
            pltpu.VMEM((FE, 2 * HH), F32),
            pltpu.VMEM((HH, 128), BF),
            pltpu.VMEM((4, HH, BLK * 16), BF),
            pltpu.VMEM((FE, 2 * HH), BF),
            pltpu.VMEM((FE, 2 * HH), BF),
            pltpu.VMEM((25, 128), F32),
            pltpu.VMEM((25, 128), F32),
            pltpu.VMEM((128, 3200), BF),
            pltpu.VMEM((128, 3200), BF),
            pltpu.VMEM((2, 16, 3200), F32),
            pltpu.VMEM((2, 16, 3200), F32),
            pltpu.VMEM((128, 128), F32),
            pltpu.VMEM((2, 8, 3200), F32),
            pltpu.VMEM((128, 256), F32),
            pltpu.VMEM((4, 128, 512), BF),
            pltpu.VMEM((UR, 896), F32),
            pltpu.VMEM((2, PK, 128), BF),
            pltpu.VMEM((2, 32, 8, 128), F32),
            pltpu.VMEM((32, PK, 128), BF),
            pltpu.VMEM((32, UR, 128), BF),
            pltpu.VMEM((2, 32, 128, 256), BF),
            pltpu.VMEM((32, 128, 128), BF),
            pltpu.VMEM((32, 128, 128), BF),
            pltpu.VMEM((32, UR, 256), BF),
            pltpu.VMEM((512, 512), F32),
            pltpu.VMEM((512, 512), BF),
            pltpu.VMEM((512, 512), BF),
            pltpu.VMEM((32, PK, 128), BF),
            pltpu.VMEM((2, 4, PK, 128), BF),
            pltpu.VMEM((2, 2, 4, PK, 128), BF),
            pltpu.VMEM((2, PK, 128), BF),
            pltpu.VMEM((2, 2, PK, 128), BF),
            pltpu.VMEM((PK, 128), BF),
            pltpu.VMEM((UR, 512), F32),
            pltpu.VMEM((2, 2, 32, 112, 128), BF),
            pltpu.VMEM((2, 32, 112, 128), BF),
            pltpu.VMEM((2, 4, 4, 112, 128), BF),
            pltpu.VMEM((2, 4, 4, 112, 128), BF),
            pltpu.VMEM((2, 16, 400, 128), BF),
            pltpu.VMEM((HH, 128), F32),
            pltpu.VMEM((256, 128), F32),
            dma((2, 15, 2)), dma((2, 15, 2)),
            dma((2, 15, 2)), dma((2, 15, 2)),
            dma((2, 15, 2)), dma((2, 15, 2)),
            dma((2, 16)), dma((2, 16)),
            dma((8,)), dma((8,)),
            dma((2, 2, 4, 2)), dma((2, 2, 4, 2)),
            dma((3,)), dma((3,)),
            dma((7,)),
        ],
        compiler_params=pltpu.CompilerParams(
            collective_id=0, has_side_effects=True, vmem_limit_bytes=60 * 2**20
        ),
    )(slots, w_in, w_out, gain, lscale, patches, upstream)


def shards(patches, upstream, norm_gain, layer_scale, w_in, w_out, slot_block):
    grad_w_in, grad_w_out, grad_patches, vision = mega(
        slot_block, w_in, w_out.T, norm_gain.reshape(25, 128), layer_scale.reshape(25, 128), patches, upstream
    )
    return (vision.transpose(2, 0, 1), grad_patches.T, grad_w_in, grad_w_out.T)


def solution(mesh):
    return jax.shard_map(
        shards,
        mesh=mesh,
        in_specs=(P("dp", None), P("dp", None), P(), P(), P("dp", "mp"), P("mp", "dp"), P("dp")),
        out_specs=(P("dp", None, "mp"), P("dp", "mp"), P("dp", "mp"), P("mp", "dp")),
        check_vma=False,
    )
```
